32 devices in a mesh: pts: 16 (over z, y, x), slab: 2 (over core).
Axes of the slice: x: 2, y: 2, z: 4, core: 2. Of those that a mesh axis runs over, the one named last changes fastest.
Arguments:
- features: float32 [8192, 256], P(('slab', 'pts')), parts along dimension 0, may hold values from -25 to 25
- orders: int32 [2, 8192], P(None, ('slab', 'pts')), parts along dimension 1, may hold values from 0 to 4095, as said below
- norm_gains: float32 [2, 2, 256], replicated, may hold values from 0.1 to 1.9
- qkv_weight: bfloat16 [2, 256, 768], replicated, may hold values from -4 to 4
- proj_weight: bfloat16 [2, 256, 256], replicated, may hold values from -0.375 to 0.375
- fc1_weight: bfloat16 [2, 256, 1024], replicated, may hold values from -0.375 to 0.375
- fc2_weight: bfloat16 [2, 1024, 256], replicated, may hold values from -0.1875 to 0.1875
Outputs:
- output_features: float32 [8192, 256], P(('slab', 'pts')), parts along dimension 0
The draws below stay inside these ranges and needn't reach their ends.
There are 2 independent parts, one for each index of `slab`. The reference program is written for one: setup_inputs(seed, part) draws one part's arguments, and reference() takes and returns one part's arrays. A program takes and returns all parts, laid end to end along the dimension named above; an argument that names none is the same for every part. Nothing has to cross between parts.
Inputs may be any that keep to these rules, and one draw needn't show every extreme that they name: `orders`: each row is a permutation of the 4096 storage rows. In each row the 256 serial positions of one device take exactly 8 or 24 of their points from the rows stored on each device, 24 from half of the devices.
All inputs are finite; a program needn't handle non-finite values.
Results may differ from the reference program's by a relative error of at most 0.013.
Values may be sent and summed in bfloat16 or wider, within the bound.
No kernel may reach another device: no remote copies, remote signals or barrier semaphores. Data moves between devices by JAX's collectives and lax.ppermute only.
A program may use at most 64 MiB of HBM per device.

```python
import jax
import jax.numpy as jnp
from jax import lax

C = 256
HEADS = 16
FFN_WIDTH = 1024
PATCH = 1024
BLOCKS = 2
PDEV = 256
NPTS = 4096


def draw_features(key, part):
    first = jax.random.fold_in(jax.random.fold_in(key, 11), 0)
    base_rows = jax.random.normal(first, (NPTS, C), jnp.float32)
    return jnp.clip(base_rows, -25.0, 25.0)


def draw_qkv_weight(key, part):
    base_weight = jax.random.normal(jax.random.fold_in(key, 23), (BLOCKS, C, 3 * C), jnp.float32) * C ** (-0.5)
    return jnp.clip(base_weight, -4.0, 4.0).astype(jnp.bfloat16)


def one_order(order_key):
    peers = NPTS // PDEV
    base_load = PDEV // (2 * peers)
    extra_load = PDEV // peers
    key_heavy, key_shuffle, key_final = jax.random.split(order_key, 3)
    heavy = (jax.random.permutation(key_heavy, peers) < peers // 2).astype(jnp.int32)
    dest_ids = jnp.arange(peers, dtype=jnp.int32)[:, None]
    source_ids = jnp.arange(peers, dtype=jnp.int32)[None, :]
    loads = base_load + extra_load * heavy[(source_ids - dest_ids) % peers]
    before = jnp.cumsum(loads, axis=0) - loads
    row_end = jnp.cumsum(loads, axis=1)
    slot_ids = jnp.arange(PDEV, dtype=jnp.int32)
    sources = jax.vmap(lambda ends: jnp.searchsorted(ends, slot_ids, side='right'))(row_end).astype(jnp.int32)
    dest_grid = jnp.broadcast_to(dest_ids, (peers, PDEV))
    start_in_row = row_end[dest_grid, sources] - loads[dest_grid, sources]
    ranks = before[dest_grid, sources] + slot_ids[None, :] - start_in_row
    shuffles = jax.vmap(lambda sub_key: jax.random.permutation(sub_key, PDEV))(jax.random.split(key_shuffle, peers)).astype(jnp.int32)
    storage_rows = sources * PDEV + shuffles[sources, ranks]
    finals = jax.vmap(lambda sub_key: jax.random.permutation(sub_key, PDEV))(jax.random.split(key_final, peers)).astype(jnp.int32)
    placed = jnp.take_along_axis(storage_rows, finals, axis=1)
    return placed.reshape(NPTS).astype(jnp.int32)


def draw_orders(key, part):
    block_keys = jax.random.split(jax.random.fold_in(key, 37), BLOCKS)
    return jax.vmap(one_order)(block_keys).astype(jnp.int32)


def scatter_about(key, dims, scale, most, held_as=jnp.bfloat16):
    entries = jax.random.normal(key, dims, jnp.float32) * scale
    return jnp.minimum(jnp.maximum(entries, -most), most).astype(held_as)


def setup_inputs(seed: int = 0, part: int = 0) -> dict:
    key_of = jax.random.split(jax.random.key(seed), 8)
    part_keys = jax.random.split(jax.random.fold_in(key_of[7], part), 8)
    return {
        "features": draw_features(jax.random.fold_in(jax.random.fold_in(key_of[7], part), 71), part),
        "orders": draw_orders(jax.random.fold_in(jax.random.fold_in(key_of[7], part), 71), part),
        "norm_gains": jnp.clip(1.0 + 0.18 * jax.random.normal(key_of[2], (BLOCKS, 2, C), jnp.float32), 0.1, 1.9),
        "qkv_weight": draw_qkv_weight(jax.random.fold_in(key_of[7], 71), part),
        "proj_weight": scatter_about(key_of[4], (BLOCKS, C, C), C ** -0.5, 0.375),
        "fc1_weight": scatter_about(key_of[5], (BLOCKS, C, FFN_WIDTH), C ** -0.5, 0.375),
        "fc2_weight": scatter_about(key_of[6], (BLOCKS, FFN_WIDTH, C), FFN_WIDTH ** -0.5, 0.1875),
    }


def layer_norm(values, gain_row):
    center = values - lax.optimization_barrier(jnp.mean(values, axis=1, keepdims=True))
    spread = lax.optimization_barrier(jnp.mean(center * center, axis=1, keepdims=True))
    return center * lax.rsqrt(spread + 1e-05) * gain_row

def reference(features, orders, norm_gains, qkv_weight, proj_weight, fc1_weight, fc2_weight):
    state_rows = features
    head_size = C // HEADS
    score_scale = head_size ** (-0.5)
    for block_index in range(BLOCKS):
        order_row = orders[block_index].astype(jnp.int32)
        serial = state_rows[order_row]
        normed = layer_norm(serial, norm_gains[block_index, 0]).astype(jnp.bfloat16)
        projected_all = jnp.dot(normed, qkv_weight[block_index], preferred_element_type=jnp.float32).astype(jnp.bfloat16)
        shaped = projected_all.astype(jnp.float32).reshape(NPTS // PATCH, PATCH, 3, HEADS, head_size)

        def one_patch(patch_rows):
            scores = jnp.einsum('qhd,khd->hqk', patch_rows[:, 0], patch_rows[:, 1]) * score_scale
            row_peak = lax.optimization_barrier(jnp.max(scores, axis=2, keepdims=True))
            weights = jnp.exp(scores - row_peak)
            probabilities = (weights / lax.optimization_barrier(jnp.sum(weights, axis=2, keepdims=True))).astype(jnp.bfloat16)
            probabilities = lax.optimization_barrier(probabilities).astype(jnp.float32)
            return jnp.einsum('hqk,khd->qhd', probabilities, patch_rows[:, 2])
        mixed_heads = lax.map(one_patch, shaped).reshape(NPTS, C).astype(jnp.bfloat16)
        attended = serial + jnp.dot(mixed_heads, proj_weight[block_index], preferred_element_type=jnp.float32)
        normed_two = layer_norm(attended, norm_gains[block_index, 1]).astype(jnp.bfloat16)
        expanded = jax.nn.gelu(jnp.dot(normed_two, fc1_weight[block_index], preferred_element_type=jnp.float32), approximate=False).astype(jnp.bfloat16)
        updated = attended + jnp.dot(expanded, fc2_weight[block_index], preferred_element_type=jnp.float32)
        state_rows = jnp.zeros_like(state_rows).at[order_row].set(updated)
    return state_rows
```

```python
import functools

import jax
import jax.numpy as jnp
from jax import lax
from jax.experimental import pallas as pl
from jax.experimental.pallas import tpu as pltpu
from jax.sharding import PartitionSpec as P

HEADS = 16
PATCH = 1024
BF16, F32, I32 = jnp.bfloat16, jnp.float32, jnp.int32
NT = (((1,), (1,)), ((), ()))
TN = (((0,), (0,)), ((), ()))
VMEM = pltpu.VMEM
SMEM = pltpu.SMEM


def layer_norm(values, gain_row):
    center = values - jnp.mean(values, axis=1, keepdims=True)
    spread = jnp.mean(center * center, axis=1, keepdims=True)
    return center * lax.rsqrt(spread + 1e-05) * gain_row


def matmul(a, b, dims=(((1,), (0,)), ((), ()))):
    return lax.dot_general(a, b, dims, preferred_element_type=F32)


def iota(shape, axis):
    return lax.broadcasted_iota(I32, shape, axis)


def ones_where(mask):
    return jnp.where(mask, 1.0, 0.0).astype(BF16)


def earlier_mask(count):
    return ones_where(iota((count, count), 0) < iota((count, count), 1))


def as_index(row):
    return row.astype(I32)


def slot_rows(members, ranks):
    return jnp.where(members > 0.5, ranks, -1.0)


class Plan:
    def __init__(self, row_count, peers, width):
        self.rows, self.peers, self.width = row_count, peers, width
        self.group = PATCH // row_count
        self.lines = peers // self.group
        self.base = row_count // (2 * peers)
        self.cap = 3 * self.base * self.group
        self.held = self.cap * self.lines

    def fits(self):
        return (
            self.group == 4
            and self.lines == 4
            and self.rows == self.width == 256
            and self.base % 8 == 0
        )


def kernel_call(body, outs, in_specs, scratch=()):
    return pl.pallas_call(
        body,
        out_shape=outs,
        in_specs=in_specs,
        out_specs=[pl.BlockSpec(memory_space=VMEM)] * len(outs),
        scratch_shapes=list(scratch),
        compiler_params=pltpu.CompilerParams(vmem_limit_bytes=40 * 2**20),
    )


def whole():
    return pl.BlockSpec(memory_space=VMEM)


def scalars():
    return pl.BlockSpec(memory_space=SMEM)


def open_body(plan, place, feature_ref, order_ref, gain_ref, normed_ref, *note_refs):
    normed_ref[...] = layer_norm(feature_ref[...], gain_ref[0, 0:1, :]).astype(BF16)
    line, column = place[0], place[1]
    bits = plan.rows.bit_length() - 1
    entry = iota((32, 1), 0)
    notes = [None] * plan.group
    for b in range(order_ref.shape[0]):
        order_row = order_ref[b : b + 1, :]
        owner = order_row >> bits
        within = order_row & (plan.rows - 1)
        inside = ones_where(iota((plan.rows, 1), 0) == within)
        picks = []
        for k in range(plan.group):
            target = column ^ k
            member = entry - 8 * b
            stored = jnp.where(
                (member >= 0) & (member < plan.lines), (member ^ line) * plan.group + target, -1
            )
            other = entry - 16
            counted = ((other & 3) ^ line) * plan.group + (target ^ (other >> 2))
            picks.append(ones_where(owner == jnp.where(other >= 0, counted, stored)))
        pick = jnp.concatenate(picks, axis=0)
        found = matmul(pick, inside, NT)
        counts = jnp.sum(found, axis=1, keepdims=True)
        lane = iota((1, plan.width), 1)
        rowid = iota((32 * plan.group, 1), 0) & 31
        mine = (lane >= 128 * b) & (lane < 128 * (b + 1))
        part = jnp.where(rowid < 16, found, jnp.where(mine, counts, 0.0))
        notes = part if b == 0 else notes + part
    for k in range(plan.group):
        note_refs[k][...] = notes[32 * k : 32 * (k + 1)].astype(BF16)


def first_pack_body(plan, *refs):
    row_refs, note_refs = refs[:4], refs[4:8]
    packed_ref, count_ref, member_ref = refs[8:]
    total = sum(r[...].astype(F32) for r in note_refs)
    members = total[:16]
    member_ref[...] = members.astype(BF16)
    count_ref[...] = jnp.concatenate([total[16:, :64], total[16:, 128:192]], axis=1).astype(I32)
    ranks = matmul(members.astype(BF16), earlier_mask(plan.rows))
    slot = iota((plan.held, 1), 0).astype(F32)
    offset = jnp.zeros((1, 1), F32)
    out = jnp.zeros((plan.held, plan.width), F32)
    for j in range(plan.lines):
        row = members[j : j + 1]
        where = jnp.where(row > 0.5, ranks[j : j + 1] + offset, -1.0)
        out = out + matmul(ones_where(slot == where), row_refs[j][...])
        offset = offset + jnp.sum(row, axis=1, keepdims=True)
    packed_ref[...] = out.astype(BF16)


def pack_body(plan, b, count_ref, *refs):
    piece_refs, packed_ref, room = refs[:4], refs[4], refs[5]
    room[...] = jnp.zeros(room.shape, room.dtype)
    offset = 0
    for j in range(plan.lines):
        room[pl.ds(pl.multiple_of(offset, 16), plan.cap), :] = piece_refs[j][...]
        offset = offset + count_ref[j, 64 * b]
    packed_ref[...] = room[0 : plan.held]


def attend_body(plan, b, with_notes, count_ref, *refs):
    group, lines, held, cap, width = plan.group, plan.lines, plan.held, plan.cap, plan.width
    part_refs, weight_ref = refs[:group], refs[group]
    refs = refs[group + 1 :]
    if with_notes:
        member_ref, refs = refs[0], refs[1:]
    out_refs, (all_rows, keys, values, queries, mixed) = refs[:lines], refs[lines:]
    head_size = width // HEADS
    offset = 0
    for k in range(group):
        all_rows[pl.ds(pl.multiple_of(offset, 16), held), :] = part_refs[k][...]
        for j in range(lines):
            offset = offset + count_ref[k * lines + j, 64 * b]
    patch_rows = all_rows[0:PATCH]
    keys[...] = matmul(patch_rows, weight_ref[b, :, width : 2 * width]).astype(BF16)
    values[...] = matmul(patch_rows, weight_ref[b, :, 2 * width :]).astype(BF16)
    scaled = matmul(part_refs[0][...], weight_ref[b, :, :width]).astype(BF16) * (head_size**-0.5)
    queries[...] = scaled.astype(BF16)
    mixed[...] = jnp.zeros(mixed.shape, mixed.dtype)
    own = 0
    offsets = []
    for j in range(lines):
        offsets.append(own)
        own = own + count_ref[j, 64 * b]
    head_mask = iota((HEADS, 1, width), 0) == iota((HEADS, 1, width), 2) // head_size

    def sixteen(start):
        block = queries[pl.ds(start, 16), :]
        spread = jnp.where(head_mask, block[None], jnp.zeros((), BF16)).reshape(HEADS * 16, width)
        scores = matmul(spread, keys[...], NT)
        weights = jnp.exp(scores - jnp.max(scores, axis=1, keepdims=True))
        total = jnp.sum(weights, axis=1, keepdims=True)
        summed = matmul(weights.astype(BF16), values[...]) / total
        kept = jnp.where(head_mask, summed.reshape(HEADS, 16, width), 0.0)
        mixed[pl.ds(start, 16), :] = jnp.sum(kept, axis=0).astype(BF16)

    def step(i, carry):
        start = pl.multiple_of(i * 32, 32)
        sixteen(start)
        sixteen(pl.multiple_of(start + 16, 16))
        return carry

    lax.fori_loop(0, (own + 31) // 32, step, 0)
    for j in range(lines):
        out_refs[j][0:cap, :] = mixed[pl.ds(pl.multiple_of(offsets[j], 16), cap), :]
        if with_notes:
            entry = iota((16, 1), 0)
            now = member_ref[j : j + 1, :].astype(F32)
            later = member_ref[8 + j : 9 + j, :].astype(F32)
            note = jnp.where(entry == 0, now, jnp.where(entry == 1, later, 0.0))
            out_refs[j][cap : cap + 16, :] = note.astype(BF16)


def store_body(plan, b, last, *refs):
    lines, cap, rows = plan.lines, plan.cap, plan.rows
    piece_refs, refs = refs[:lines], refs[lines:]
    if b:
        note_refs, refs = refs[:lines], refs[lines:]
    else:
        note_refs = piece_refs
    state_ref, gain_ref, proj_ref, fc1_ref, fc2_ref = refs[:5]
    refs = refs[5:]
    state_out, send_refs = refs[0], refs[1:]
    notes = [r[cap : cap + 16, :].astype(F32) for r in note_refs]
    members = jnp.concatenate(notes, axis=0)
    ranks = matmul(members.astype(BF16), earlier_mask(rows))
    slot = iota((cap, 1), 0).astype(F32)

    def places(j, block):
        at = 16 * j + block
        where = jnp.where(members[at : at + 1] > 0.5, ranks[at : at + 1], -1.0)
        return ones_where(slot == where)

    where_from = jnp.concatenate([places(j, b) for j in range(lines)], axis=0)
    pieces = jnp.concatenate([r[0:cap, :] for r in piece_refs], axis=0)
    mixed = matmul(where_from, pieces, TN).astype(BF16)
    attended = state_ref[...] + matmul(mixed, proj_ref[b])
    normed_two = layer_norm(attended, gain_ref[b, 1:2, :]).astype(BF16)
    hidden = matmul(normed_two, fc1_ref[b])
    expanded = (0.5 * hidden * (1.0 + lax.erf(hidden * (0.5**0.5)))).astype(BF16)
    state = attended + matmul(expanded, fc2_ref[b])
    state_out[...] = state
    if not last:
        normed = layer_norm(state, gain_ref[b + 1, 0:1, :]).astype(BF16)
        for j in range(lines):
            send_refs[j][...] = matmul(places(j, b + 1), normed).astype(BF16)


def flip(block, count, bit):
    return lax.ppermute(block, "pts", [(i, i ^ bit) for i in range(count)])


def struct(shape, dtype):
    return jax.ShapeDtypeStruct(shape, dtype)


def by_lines(plan, features, orders, norm_gains, qkv_weight, proj_weight, fc1_weight, fc2_weight):
    rows, width, peers = plan.rows, plan.width, plan.peers
    group, lines, held, cap = plan.group, plan.lines, plan.held, plan.cap
    blocks = orders.shape[0]
    me = lax.axis_index("pts")
    place = jnp.stack([me // group, me % group]).astype(I32)

    def along_line(pieces):
        return [pieces[0]] + [flip(pieces[j], peers, group * j) for j in range(1, lines)]

    def in_group(piece):
        return [piece] + [flip(piece, peers, k) for k in range(1, group)]

    opened = kernel_call(
        functools.partial(open_body, plan),
        [struct((rows, width), BF16)] + [struct((32, width), BF16)] * group,
        [scalars(), whole(), whole(), whole()],
    )(place, features, orders, norm_gains)
    normed, notes = opened[0], opened[1:]
    line_rows = along_line([normed] * lines)
    notes = [notes[0]] + [flip(notes[k], peers, k) for k in range(1, group)]
    packed, counts, members = kernel_call(
        functools.partial(first_pack_body, plan),
        [struct((held, width), BF16), struct((16, 128), I32), struct((16, width), BF16)],
        [whole()] * (lines + group),
    )(*line_rows, *notes)
    state = features
    for b in range(blocks):
        last = b == blocks - 1
        tall = cap if b else cap + 16
        parts = in_group(packed)
        extra = [] if b else [members]
        mixed = kernel_call(
            functools.partial(attend_body, plan, b, b == 0),
            [struct((tall, width), BF16)] * lines,
            [scalars()] + [whole()] * (group + 1 + len(extra)),
            [
                pltpu.VMEM((PATCH + held, width), BF16),
                pltpu.VMEM((PATCH, width), BF16),
                pltpu.VMEM((PATCH, width), BF16),
                pltpu.VMEM((held, width), BF16),
                pltpu.VMEM((held + cap, width), BF16),
            ],
        )(counts, *parts, qkv_weight, *extra)
        pieces = along_line(mixed)
        if b == 0:
            kept = pieces
        outs = [struct((rows, width), F32)]
        if not last:
            outs += [struct((cap, width), BF16)] * lines
        stored = kernel_call(
            functools.partial(store_body, plan, b, last),
            outs,
            [whole()] * (lines * (2 if b else 1) + 5),
        )(
            *pieces,
            *(kept if b else []),
            state,
            norm_gains,
            proj_weight,
            fc1_weight,
            fc2_weight,
        )
        state = stored[0]
        if not last:
            arrived = along_line(stored[1:])
            (packed,) = kernel_call(
                functools.partial(pack_body, plan, b + 1),
                [struct((held, width), BF16)],
                [scalars()] + [whole()] * lines,
                [pltpu.VMEM((held + cap, width), BF16)],
            )(counts, *arrived)
    return state


def from_partner(block, axis, bit):
    count = lax.axis_size(axis)
    route = []
    for low in range(count):
        high = low | 1 << bit
        if high != low and high < count:
            route += [(low, high), (high, low)]
    return lax.ppermute(block, axis, route)


def routing(order_row, row_count, peers, capacity):
    owner_dev = order_row // row_count
    within = order_row % row_count
    onehot = (owner_dev[:, None] == jnp.arange(peers, dtype=jnp.int32)[None, :]).astype(jnp.int32)
    earlier = jnp.cumsum(onehot, axis=0) - onehot
    rank_pos = jnp.sum(onehot * earlier, axis=1)
    slot_pos = owner_dev * capacity + rank_pos
    request = jnp.full((peers * capacity,), row_count, jnp.int32).at[slot_pos].set(within)
    received = lax.all_to_all(request, "pts", split_axis=0, concat_axis=0, tiled=True)
    return (slot_pos, received)


def feed_forward(attended, gain_row, first_weight, second_weight):
    normed_two = layer_norm(attended, gain_row).astype(jnp.bfloat16)
    expanded = jax.nn.gelu(
        jnp.dot(normed_two, first_weight, preferred_element_type=jnp.float32), approximate=False
    ).astype(jnp.bfloat16)
    return jnp.dot(expanded, second_weight, preferred_element_type=jnp.float32)


def mix_heads(normed, in_weight):
    row_count, model_width = normed.shape
    projected_all = jnp.dot(normed, in_weight, preferred_element_type=jnp.float32).astype(
        jnp.bfloat16
    )
    queries = projected_all[:, :model_width]
    paired = projected_all[:, model_width:]
    doublings = (PATCH // row_count).bit_length() - 1
    gathered = paired
    for bit_index in range(doublings):
        gathered = jnp.concatenate((gathered, from_partner(gathered, "pts", bit_index)), axis=0)
    keys_all = gathered[:, :model_width]
    values_all = gathered[:, model_width:]
    head_size = model_width // HEADS
    per_group = min(4, HEADS)
    groups = HEADS // per_group
    score_scale = head_size ** (-0.5)

    def split_heads(matrix):
        return matrix.reshape(matrix.shape[0], groups, per_group, head_size).transpose(1, 0, 2, 3)

    def one_group(operands):
        query_part, key_part, value_part = operands
        scores = (
            jnp.einsum("qhd,khd->hqk", query_part, key_part, preferred_element_type=jnp.float32)
            * score_scale
        )
        row_peak = jnp.max(scores, axis=2, keepdims=True)
        weights = jnp.exp(scores - row_peak)
        probabilities = (weights / jnp.sum(weights, axis=2, keepdims=True)).astype(jnp.bfloat16)
        return jnp.einsum(
            "hqk,khd->qhd", probabilities, value_part, preferred_element_type=jnp.float32
        )

    mixed_heads = lax.map(
        one_group, (split_heads(queries), split_heads(keys_all), split_heads(values_all))
    )
    return mixed_heads.transpose(1, 0, 2, 3).reshape(row_count, model_width).astype(jnp.bfloat16)


def by_request(features, orders, norm_gains, qkv_weight, proj_weight, fc1_weight, fc2_weight):
    row_count, model_width = features.shape
    peers = lax.axis_size("pts")
    capacity = 3 * row_count // (2 * peers)
    state_rows = features
    for block_index in range(orders.shape[0]):
        slot_pos, received = routing(orders[block_index], row_count, peers, capacity)
        source_rows = jnp.minimum(received, row_count - 1)
        normed_local = layer_norm(state_rows, norm_gains[block_index, 0]).astype(jnp.bfloat16)
        arrived = lax.all_to_all(
            normed_local[source_rows], "pts", split_axis=0, concat_axis=0, tiled=True
        )
        mixed_heads = mix_heads(arrived[slot_pos], qkv_weight[block_index])
        returning = (
            jnp.zeros((peers * capacity, model_width), jnp.bfloat16).at[slot_pos].set(mixed_heads)
        )
        landed = lax.all_to_all(returning, "pts", split_axis=0, concat_axis=0, tiled=True)
        stored_mixed = (
            jnp.zeros((row_count, model_width), jnp.bfloat16).at[received].set(landed, mode="drop")
        )
        attended = state_rows + jnp.dot(
            stored_mixed, proj_weight[block_index], preferred_element_type=jnp.float32
        )
        state_rows = attended + feed_forward(
            attended, norm_gains[block_index, 1], fc1_weight[block_index], fc2_weight[block_index]
        )
    return state_rows


def local(*arrays):
    row_count, model_width = arrays[0].shape
    peers = lax.axis_size("pts")
    plan = Plan(row_count, peers, model_width)
    return by_lines(plan, *arrays) if plan.fits() else by_request(*arrays)


def solution(mesh):
    placed = (P(("slab", "pts"), None), P(None, ("slab", "pts")), P(), P(), P(), P(), P())
    return jax.shard_map(
        local, mesh=mesh, in_specs=placed, out_specs=P(("slab", "pts"), None), check_vma=False
    )
```

```python
import functools

import jax
import jax.numpy as jnp
from jax import lax
from jax.experimental import pallas as pl
from jax.experimental.pallas import tpu as pltpu
from jax.sharding import PartitionSpec as P

HEADS = 16
PATCH = 1024
TALL = 32
BF16, F32, I32 = jnp.bfloat16, jnp.float32, jnp.int32
NT = (((1,), (1,)), ((), ()))
TN = (((0,), (0,)), ((), ()))
VMEM = pltpu.VMEM
SMEM = pltpu.SMEM


def layer_norm(values, gain_row):
    center = values - jnp.mean(values, axis=1, keepdims=True)
    spread = jnp.mean(center * center, axis=1, keepdims=True)
    return center * lax.rsqrt(spread + 1e-05) * gain_row


def matmul(a, b, dims=(((1,), (0,)), ((), ()))):
    return lax.dot_general(a, b, dims, preferred_element_type=F32)


def iota(shape, axis):
    return lax.broadcasted_iota(I32, shape, axis)


def ones_where(mask):
    return jnp.where(mask, 1.0, 0.0).astype(BF16)


def earlier_mask(count):
    return ones_where(iota((count, count), 0) < iota((count, count), 1))


def as_index(row):
    return row.astype(I32)


def slot_rows(members, ranks):
    return jnp.where(members > 0.5, ranks, -1.0)


class Plan:
    def __init__(self, row_count, peers, width):
        self.rows, self.peers, self.width = row_count, peers, width
        self.group = PATCH // row_count
        self.lines = peers // self.group
        self.base = row_count // (2 * peers)
        self.cap = 3 * self.base * self.group
        self.held = self.cap * self.lines

    def fits(self):
        return (
            self.group == 4
            and self.lines == 4
            and self.rows == self.width == 256
            and self.base % 8 == 0
        )


def kernel_call(body, outs, in_specs, scratch=()):
    return pl.pallas_call(
        body,
        out_shape=outs,
        in_specs=in_specs,
        out_specs=[pl.BlockSpec(memory_space=VMEM)] * len(outs),
        scratch_shapes=list(scratch),
        compiler_params=pltpu.CompilerParams(vmem_limit_bytes=40 * 2**20),
    )


def whole():
    return pl.BlockSpec(memory_space=VMEM)


def scalars():
    return pl.BlockSpec(memory_space=SMEM)


def open_body(plan, place, feature_ref, order_ref, gain_ref, normed_ref, *note_refs):
    normed_ref[...] = layer_norm(feature_ref[...], gain_ref[0, 0:1, :]).astype(BF16)
    line, column = place[0], place[1]
    bits = plan.rows.bit_length() - 1
    entry = iota((32, 1), 0)
    notes = [None] * plan.group
    for b in range(order_ref.shape[0]):
        order_row = order_ref[b : b + 1, :]
        owner = order_row >> bits
        within = order_row & (plan.rows - 1)
        inside = ones_where(iota((plan.rows, 1), 0) == within)
        picks = []
        for k in range(plan.group):
            target = column ^ k
            member = entry - 8 * b
            stored = jnp.where(
                (member >= 0) & (member < plan.lines), (member ^ line) * plan.group + target, -1
            )
            other = entry - 16
            counted = ((other & 3) ^ line) * plan.group + (target ^ (other >> 2))
            picks.append(ones_where(owner == jnp.where(other >= 0, counted, stored)))
        pick = jnp.concatenate(picks, axis=0)
        found = matmul(pick, inside, NT)
        counts = jnp.sum(found, axis=1, keepdims=True)
        lane = iota((1, plan.width), 1)
        rowid = iota((32 * plan.group, 1), 0) & 31
        mine = (lane >= 128 * b) & (lane < 128 * (b + 1))
        part = jnp.where(rowid < 16, found, jnp.where(mine, counts, 0.0))
        notes = part if b == 0 else notes + part
    for k in range(plan.group):
        note_refs[k][...] = notes[32 * k : 32 * (k + 1)].astype(BF16)


def first_pack_body(plan, *refs):
    row_refs, note_refs = refs[:4], refs[4:8]
    packed_ref, count_ref, member_ref = refs[8:]
    total = sum(r[...].astype(F32) for r in note_refs)
    members = total[:16]
    member_ref[...] = members.astype(BF16)
    count_ref[...] = jnp.concatenate([total[16:, :64], total[16:, 128:192]], axis=1).astype(I32)
    ranks = matmul(members.astype(BF16), earlier_mask(plan.rows))
    slot = iota((plan.held, 1), 0).astype(F32)
    offset = jnp.zeros((1, 1), F32)
    out = jnp.zeros((plan.held, plan.width), F32)
    for j in range(plan.lines):
        row = members[j : j + 1]
        where = jnp.where(row > 0.5, ranks[j : j + 1] + offset, -1.0)
        out = out + matmul(ones_where(slot == where), row_refs[j][...])
        offset = offset + jnp.sum(row, axis=1, keepdims=True)
    packed_ref[...] = out.astype(BF16)


def pack_body(plan, b, count_ref, *refs):
    piece_refs, packed_ref, room = refs[:4], refs[4], refs[5]
    room[...] = jnp.zeros(room.shape, room.dtype)
    offset = 0
    for j in range(plan.lines):
        room[pl.ds(pl.multiple_of(offset, 16), plan.cap), :] = piece_refs[j][...]
        offset = offset + count_ref[j, 64 * b]
    packed_ref[...] = room[0 : plan.held]


def query_body(plan, b, row_ref, weight_ref, query_ref):
    head_size = plan.width // HEADS
    projected = matmul(row_ref[...], weight_ref[b, :, : plan.width]).astype(BF16)
    query_ref[0 : plan.held] = (projected * (head_size**-0.5)).astype(BF16)
    query_ref[plan.held :] = jnp.zeros((2 * TALL, plan.width), BF16)


def attend_body(plan, b, with_notes, count_ref, *refs):
    group, lines, held, cap, width = plan.group, plan.lines, plan.held, plan.cap, plan.width
    part_refs, weight_ref, query_ref = refs[:group], refs[group], refs[group + 1]
    refs = refs[group + 2 :]
    if with_notes:
        member_ref, refs = refs[0], refs[1:]
    out_refs, (all_rows, keys, values, mixed, scores) = refs[:lines], refs[lines:]
    half = width // 2
    half_heads = HEADS // 2
    offset = 0
    for k in range(group):
        all_rows[pl.ds(pl.multiple_of(offset, 16), held), :] = part_refs[k][...]
        for j in range(lines):
            offset = offset + count_ref[k * lines + j, 64 * b]
    patch_rows = all_rows[0:PATCH]
    keys[...] = matmul(
        weight_ref[b, :, width : 2 * width], patch_rows, (((0,), (1,)), ((), ()))
    ).astype(BF16)
    projected = matmul(patch_rows, weight_ref[b, :, 2 * width :]).astype(BF16)
    ones = jnp.ones((PATCH, half), BF16)
    for g in range(2):
        values[g] = jnp.concatenate([projected[:, g * half : (g + 1) * half], ones], axis=1)
    mixed[...] = jnp.zeros(mixed.shape, mixed.dtype)
    own = 0
    offsets = []
    for j in range(lines):
        offsets.append(own)
        own = own + count_ref[j, 64 * b]
    shape = (half_heads, 1, half)
    head_mask = iota(shape, 0) == iota(shape, 2) // (width // HEADS)

    def scored(slot, start, g):
        block = query_ref[pl.ds(start, TALL), g * half : (g + 1) * half]
        spread = jnp.where(head_mask, block[None], jnp.zeros((), BF16))
        scores[slot] = matmul(
            spread.reshape(half_heads * TALL, half), keys[g * half : (g + 1) * half]
        )

    def averaged(slot, start, g):
        table = scores[slot]
        weights = jnp.exp(table - jnp.max(table, axis=1, keepdims=True)).astype(BF16)
        summed = matmul(weights, values[g])
        summed = summed[:, :half] / summed[:, half:]
        kept = jnp.where(head_mask, summed.reshape(half_heads, TALL, half), 0.0)
        mixed[pl.ds(start, TALL), g * half : (g + 1) * half] = jnp.sum(kept, axis=0).astype(BF16)

    scored(0, 0, 0)
    scored(1, 0, 1)

    def step(i, carry):
        first = pl.multiple_of(i * 2 * TALL, 2 * TALL)
        second = pl.multiple_of(first + TALL, TALL)
        third = pl.multiple_of(second + TALL, TALL)
        scored(2, second, 0)
        averaged(0, first, 0)
        scored(3, second, 1)
        averaged(1, first, 1)
        scored(0, third, 0)
        averaged(2, second, 0)
        scored(1, third, 1)
        averaged(3, second, 1)
        return carry

    lax.fori_loop(0, (own + 2 * TALL - 1) // (2 * TALL), step, 0)
    for j in range(lines):
        out_refs[j][0:cap, :] = mixed[pl.ds(pl.multiple_of(offsets[j], 16), cap), :]
        if with_notes:
            entry = iota((16, 1), 0)
            now = member_ref[j : j + 1, :].astype(F32)
            later = member_ref[8 + j : 9 + j, :].astype(F32)
            note = jnp.where(entry == 0, now, jnp.where(entry == 1, later, 0.0))
            out_refs[j][cap : cap + 16, :] = note.astype(BF16)


def store_body(plan, b, last, *refs):
    lines, cap, rows = plan.lines, plan.cap, plan.rows
    piece_refs, refs = refs[:lines], refs[lines:]
    if b:
        note_refs, refs = refs[:lines], refs[lines:]
    else:
        note_refs = piece_refs
    state_ref, gain_ref, proj_ref, fc1_ref, fc2_ref = refs[:5]
    refs = refs[5:]
    state_out, send_refs = refs[0], refs[1:]
    notes = [r[cap : cap + 16, :].astype(F32) for r in note_refs]
    members = jnp.concatenate(notes, axis=0)
    ranks = matmul(members.astype(BF16), earlier_mask(rows))
    slot = iota((cap, 1), 0).astype(F32)

    def places(j, block):
        at = 16 * j + block
        where = jnp.where(members[at : at + 1] > 0.5, ranks[at : at + 1], -1.0)
        return ones_where(slot == where)

    where_from = jnp.concatenate([places(j, b) for j in range(lines)], axis=0)
    pieces = jnp.concatenate([r[0:cap, :] for r in piece_refs], axis=0)
    mixed = matmul(where_from, pieces, TN).astype(BF16)
    attended = state_ref[...] + matmul(mixed, proj_ref[b])
    normed_two = layer_norm(attended, gain_ref[b, 1:2, :]).astype(BF16)
    hidden = matmul(normed_two, fc1_ref[b])
    expanded = (0.5 * hidden * (1.0 + lax.erf(hidden * (0.5**0.5)))).astype(BF16)
    state = attended + matmul(expanded, fc2_ref[b])
    state_out[...] = state
    if not last:
        normed = layer_norm(state, gain_ref[b + 1, 0:1, :]).astype(BF16)
        for j in range(lines):
            send_refs[j][...] = matmul(places(j, b + 1), normed).astype(BF16)


def flip(block, count, bit):
    return lax.ppermute(block, "pts", [(i, i ^ bit) for i in range(count)])


def struct(shape, dtype):
    return jax.ShapeDtypeStruct(shape, dtype)


def by_lines(plan, features, orders, norm_gains, qkv_weight, proj_weight, fc1_weight, fc2_weight):
    rows, width, peers = plan.rows, plan.width, plan.peers
    group, lines, held, cap = plan.group, plan.lines, plan.held, plan.cap
    blocks = orders.shape[0]
    me = lax.axis_index("pts")
    place = jnp.stack([me // group, me % group]).astype(I32)

    def along_line(pieces):
        return [pieces[0]] + [flip(pieces[j], peers, group * j) for j in range(1, lines)]

    def in_group(piece):
        return [piece] + [flip(piece, peers, k) for k in range(1, group)]

    opened = kernel_call(
        functools.partial(open_body, plan),
        [struct((rows, width), BF16)] + [struct((32, width), BF16)] * group,
        [scalars(), whole(), whole(), whole()],
    )(place, features, orders, norm_gains)
    normed, notes = opened[0], opened[1:]
    line_rows = along_line([normed] * lines)
    notes = [notes[0]] + [flip(notes[k], peers, k) for k in range(1, group)]
    packed, counts, members = kernel_call(
        functools.partial(first_pack_body, plan),
        [struct((held, width), BF16), struct((16, 128), I32), struct((16, width), BF16)],
        [whole()] * (lines + group),
    )(*line_rows, *notes)
    state = features
    for b in range(blocks):
        last = b == blocks - 1
        tall = cap if b else cap + 16
        parts = in_group(packed)
        (queries,) = kernel_call(
            functools.partial(query_body, plan, b),
            [struct((held + 2 * TALL, width), BF16)],
            [whole(), whole()],
        )(packed, qkv_weight)
        extra = [] if b else [members]
        mixed = kernel_call(
            functools.partial(attend_body, plan, b, b == 0),
            [struct((tall, width), BF16)] * lines,
            [scalars()] + [whole()] * (group + 2 + len(extra)),
            [
                pltpu.VMEM((PATCH + held, width), BF16),
                pltpu.VMEM((width, PATCH), BF16),
                pltpu.VMEM((2, PATCH, width), BF16),
                pltpu.VMEM((held + cap, width), BF16),
                pltpu.VMEM((4, HEADS // 2 * TALL, PATCH), F32),
            ],
        )(counts, *parts, qkv_weight, queries, *extra)
        pieces = along_line(mixed)
        if b == 0:
            kept = pieces
        outs = [struct((rows, width), F32)]
        if not last:
            outs += [struct((cap, width), BF16)] * lines
        stored = kernel_call(
            functools.partial(store_body, plan, b, last),
            outs,
            [whole()] * (lines * (2 if b else 1) + 5),
        )(
            *pieces,
            *(kept if b else []),
            state,
            norm_gains,
            proj_weight,
            fc1_weight,
            fc2_weight,
        )
        state = stored[0]
        if not last:
            arrived = along_line(stored[1:])
            (packed,) = kernel_call(
                functools.partial(pack_body, plan, b + 1),
                [struct((held, width), BF16)],
                [scalars()] + [whole()] * lines,
                [pltpu.VMEM((held + cap, width), BF16)],
            )(counts, *arrived)
    return state


def from_partner(block, axis, bit):
    count = lax.axis_size(axis)
    route = []
    for low in range(count):
        high = low | 1 << bit
        if high != low and high < count:
            route += [(low, high), (high, low)]
    return lax.ppermute(block, axis, route)


def routing(order_row, row_count, peers, capacity):
    owner_dev = order_row // row_count
    within = order_row % row_count
    onehot = (owner_dev[:, None] == jnp.arange(peers, dtype=jnp.int32)[None, :]).astype(jnp.int32)
    earlier = jnp.cumsum(onehot, axis=0) - onehot
    rank_pos = jnp.sum(onehot * earlier, axis=1)
    slot_pos = owner_dev * capacity + rank_pos
    request = jnp.full((peers * capacity,), row_count, jnp.int32).at[slot_pos].set(within)
    received = lax.all_to_all(request, "pts", split_axis=0, concat_axis=0, tiled=True)
    return (slot_pos, received)


def feed_forward(attended, gain_row, first_weight, second_weight):
    normed_two = layer_norm(attended, gain_row).astype(jnp.bfloat16)
    expanded = jax.nn.gelu(
        jnp.dot(normed_two, first_weight, preferred_element_type=jnp.float32), approximate=False
    ).astype(jnp.bfloat16)
    return jnp.dot(expanded, second_weight, preferred_element_type=jnp.float32)


def mix_heads(normed, in_weight):
    row_count, model_width = normed.shape
    projected_all = jnp.dot(normed, in_weight, preferred_element_type=jnp.float32).astype(
        jnp.bfloat16
    )
    queries = projected_all[:, :model_width]
    paired = projected_all[:, model_width:]
    doublings = (PATCH // row_count).bit_length() - 1
    gathered = paired
    for bit_index in range(doublings):
        gathered = jnp.concatenate((gathered, from_partner(gathered, "pts", bit_index)), axis=0)
    keys_all = gathered[:, :model_width]
    values_all = gathered[:, model_width:]
    head_size = model_width // HEADS
    per_group = min(4, HEADS)
    groups = HEADS // per_group
    score_scale = head_size ** (-0.5)

    def split_heads(matrix):
        return matrix.reshape(matrix.shape[0], groups, per_group, head_size).transpose(1, 0, 2, 3)

    def one_group(operands):
        query_part, key_part, value_part = operands
        scores = (
            jnp.einsum("qhd,khd->hqk", query_part, key_part, preferred_element_type=jnp.float32)
            * score_scale
        )
        row_peak = jnp.max(scores, axis=2, keepdims=True)
        weights = jnp.exp(scores - row_peak)
        probabilities = (weights / jnp.sum(weights, axis=2, keepdims=True)).astype(jnp.bfloat16)
        return jnp.einsum(
            "hqk,khd->qhd", probabilities, value_part, preferred_element_type=jnp.float32
        )

    mixed_heads = lax.map(
        one_group, (split_heads(queries), split_heads(keys_all), split_heads(values_all))
    )
    return mixed_heads.transpose(1, 0, 2, 3).reshape(row_count, model_width).astype(jnp.bfloat16)


def by_request(features, orders, norm_gains, qkv_weight, proj_weight, fc1_weight, fc2_weight):
    row_count, model_width = features.shape
    peers = lax.axis_size("pts")
    capacity = 3 * row_count // (2 * peers)
    state_rows = features
    for block_index in range(orders.shape[0]):
        slot_pos, received = routing(orders[block_index], row_count, peers, capacity)
        source_rows = jnp.minimum(received, row_count - 1)
        normed_local = layer_norm(state_rows, norm_gains[block_index, 0]).astype(jnp.bfloat16)
        arrived = lax.all_to_all(
            normed_local[source_rows], "pts", split_axis=0, concat_axis=0, tiled=True
        )
        mixed_heads = mix_heads(arrived[slot_pos], qkv_weight[block_index])
        returning = (
            jnp.zeros((peers * capacity, model_width), jnp.bfloat16).at[slot_pos].set(mixed_heads)
        )
        landed = lax.all_to_all(returning, "pts", split_axis=0, concat_axis=0, tiled=True)
        stored_mixed = (
            jnp.zeros((row_count, model_width), jnp.bfloat16).at[received].set(landed, mode="drop")
        )
        attended = state_rows + jnp.dot(
            stored_mixed, proj_weight[block_index], preferred_element_type=jnp.float32
        )
        state_rows = attended + feed_forward(
            attended, norm_gains[block_index, 1], fc1_weight[block_index], fc2_weight[block_index]
        )
    return state_rows


def local(*arrays):
    row_count, model_width = arrays[0].shape
    peers = lax.axis_size("pts")
    plan = Plan(row_count, peers, model_width)
    return by_lines(plan, *arrays) if plan.fits() else by_request(*arrays)


def solution(mesh):
    placed = (P(("slab", "pts"), None), P(None, ("slab", "pts")), P(), P(), P(), P(), P())
    return jax.shard_map(
        local, mesh=mesh, in_specs=placed, out_specs=P(("slab", "pts"), None), check_vma=False
    )
```

```python
import functools

import jax
import jax.numpy as jnp
from jax import lax
from jax.experimental import pallas as pl
from jax.experimental.pallas import tpu as pltpu
from jax.sharding import PartitionSpec as P

HEADS = 16
PATCH = 1024
TALL = 32
BF16, F32, I32 = jnp.bfloat16, jnp.float32, jnp.int32
NT = (((1,), (1,)), ((), ()))
TN = (((0,), (0,)), ((), ()))
VMEM = pltpu.VMEM
SMEM = pltpu.SMEM


def layer_norm(values, gain_row):
    center = values - jnp.mean(values, axis=1, keepdims=True)
    spread = jnp.mean(center * center, axis=1, keepdims=True)
    return center * lax.rsqrt(spread + 1e-05) * gain_row


def matmul(a, b, dims=(((1,), (0,)), ((), ()))):
    return lax.dot_general(a, b, dims, preferred_element_type=F32)


def iota(shape, axis):
    return lax.broadcasted_iota(I32, shape, axis)


def ones_where(mask):
    return jnp.where(mask, 1.0, 0.0).astype(BF16)


def earlier_mask(count):
    return ones_where(iota((count, count), 0) < iota((count, count), 1))


def as_index(row):
    return row.astype(I32)


def slot_rows(members, ranks):
    return jnp.where(members > 0.5, ranks, -1.0)


class Plan:
    def __init__(self, row_count, peers, width):
        self.rows, self.peers, self.width = row_count, peers, width
        self.group = PATCH // row_count
        self.lines = peers // self.group
        self.base = row_count // (2 * peers)
        self.cap = 3 * self.base * self.group
        self.held = self.cap * self.lines

    def fits(self):
        return (
            self.group == 4
            and self.lines == 4
            and self.rows == self.width == 256
            and self.base % 8 == 0
        )


def kernel_call(body, outs, in_specs, scratch=()):
    return pl.pallas_call(
        body,
        out_shape=outs,
        in_specs=in_specs,
        out_specs=[pl.BlockSpec(memory_space=VMEM)] * len(outs),
        scratch_shapes=list(scratch),
        compiler_params=pltpu.CompilerParams(vmem_limit_bytes=40 * 2**20),
    )


def whole():
    return pl.BlockSpec(memory_space=VMEM)


def scalars():
    return pl.BlockSpec(memory_space=SMEM)


def norm_body(feature_ref, gain_ref, order_ref, normed_ref, passed_ref):
    passed_ref[...] = order_ref[...]
    normed_ref[...] = layer_norm(feature_ref[...], gain_ref[0, 0:1, :]).astype(BF16)


def note_body(plan, place, row_ref, order_ref, turned_ref, passed_ref, kept_ref, sent_ref):
    passed_ref[...] = row_ref[...]
    line, column, line_step, column_step, slab = (place[i] for i in range(5))
    order = jnp.where(slab == 0, order_ref[...], turned_ref[...])
    bits = plan.rows.bit_length() - 1
    entry = iota((32, 1), 0)
    notes = None
    for b in range(order.shape[0]):
        order_row = order[b : b + 1, :]
        owner = order_row >> bits
        within = order_row & (plan.rows - 1)
        inside = ones_where(iota((plan.rows, 1), 0) == within)
        picks = []
        for k in range(plan.group):
            target = column ^ k
            member = entry - 8 * b
            stored = jnp.where(
                (member >= 0) & (member < plan.lines),
                (member ^ line) * line_step + target * column_step,
                -1,
            )
            other = entry - 16
            counted = ((other & 3) ^ line) * line_step + (target ^ (other >> 2)) * column_step
            picks.append(ones_where(owner == jnp.where(other >= 0, counted, stored)))
        pick = jnp.concatenate(picks, axis=0)
        found = matmul(pick, inside, NT)
        counts = jnp.sum(found, axis=1, keepdims=True)
        lane = iota((1, plan.width), 1)
        rowid = iota((32 * plan.group, 1), 0) & 31
        mine = (lane >= 128 * b) & (lane < 128 * (b + 1))
        part = jnp.where(rowid < 16, found, jnp.where(mine, counts, 0.0))
        notes = part if notes is None else notes + part
    for k in range(plan.group):
        half = (kept_ref, sent_ref)[k & 1]
        half[32 * (k >> 1) : 32 * (k >> 1) + 32] = notes[32 * k : 32 * (k + 1)].astype(BF16)


def join_body(kept_ref, got_ref, mine_ref, sent_ref):
    total = (kept_ref[...].astype(F32) + got_ref[...].astype(F32)).astype(BF16)
    mine_ref[...] = total[:32]
    sent_ref[...] = total[32:]


def first_pack_body(plan, *refs):
    row_refs, note_refs = refs[:4], refs[4:6]
    packed_ref, count_ref, member_ref = refs[6:]
    total = sum(r[...].astype(F32) for r in note_refs)
    members = total[:16]
    member_ref[...] = members.astype(BF16)
    count_ref[...] = jnp.concatenate([total[16:, :64], total[16:, 128:192]], axis=1).astype(I32)
    ranks = matmul(members.astype(BF16), earlier_mask(plan.rows))
    slot = iota((plan.held, 1), 0).astype(F32)
    offset = jnp.zeros((1, 1), F32)
    out = jnp.zeros((plan.held, plan.width), F32)
    for j in range(plan.lines):
        row = members[j : j + 1]
        where = jnp.where(row > 0.5, ranks[j : j + 1] + offset, -1.0)
        out = out + matmul(ones_where(slot == where), row_refs[j][...])
        offset = offset + jnp.sum(row, axis=1, keepdims=True)
    packed_ref[...] = out.astype(BF16)


def pack_body(plan, b, count_ref, *refs):
    piece_refs, packed_ref, room = refs[:4], refs[4], refs[5]
    room[...] = jnp.zeros(room.shape, room.dtype)
    offset = 0
    for j in range(plan.lines):
        room[pl.ds(pl.multiple_of(offset, 16), plan.cap), :] = piece_refs[j][...]
        offset = offset + count_ref[j, 64 * b]
    packed_ref[...] = room[0 : plan.held]


def query_body(plan, b, row_ref, weight_ref, query_ref):
    head_size = plan.width // HEADS
    projected = matmul(row_ref[...], weight_ref[b, :, : plan.width]).astype(BF16)
    query_ref[0 : plan.held] = (projected * (head_size**-0.5)).astype(BF16)
    query_ref[plan.held :] = jnp.zeros((2 * TALL, plan.width), BF16)


def attend_body(plan, b, with_notes, count_ref, *refs):
    group, lines, held, cap, width = plan.group, plan.lines, plan.held, plan.cap, plan.width
    part_refs, weight_ref, query_ref = refs[:group], refs[group], refs[group + 1]
    refs = refs[group + 2 :]
    if with_notes:
        member_ref, refs = refs[0], refs[1:]
    out_refs, (all_rows, keys, values, mixed, scores) = refs[:lines], refs[lines:]
    half = width // 2
    half_heads = HEADS // 2
    offset = 0
    for k in range(group):
        all_rows[pl.ds(pl.multiple_of(offset, 16), held), :] = part_refs[k][...]
        for j in range(lines):
            offset = offset + count_ref[k * lines + j, 64 * b]
    patch_rows = all_rows[0:PATCH]
    keys[...] = matmul(
        weight_ref[b, :, width : 2 * width], patch_rows, (((0,), (1,)), ((), ()))
    ).astype(BF16)
    projected = matmul(patch_rows, weight_ref[b, :, 2 * width :]).astype(BF16)
    ones = jnp.ones((PATCH, half), BF16)
    for g in range(2):
        values[g] = jnp.concatenate([projected[:, g * half : (g + 1) * half], ones], axis=1)
    mixed[...] = jnp.zeros(mixed.shape, mixed.dtype)
    own = 0
    offsets = []
    for j in range(lines):
        offsets.append(own)
        own = own + count_ref[j, 64 * b]
    shape = (half_heads, 1, half)
    head_mask = iota(shape, 0) == iota(shape, 2) // (width // HEADS)

    def scored(slot, start, g):
        block = query_ref[pl.ds(start, TALL), g * half : (g + 1) * half]
        spread = jnp.where(head_mask, block[None], jnp.zeros((), BF16))
        scores[slot] = matmul(
            spread.reshape(half_heads * TALL, half), keys[g * half : (g + 1) * half]
        )

    def averaged(slot, start, g):
        table = scores[slot]
        weights = jnp.exp(table - jnp.max(table, axis=1, keepdims=True)).astype(BF16)
        summed = matmul(weights, values[g])
        summed = summed[:, :half] / summed[:, half:]
        kept = jnp.where(head_mask, summed.reshape(half_heads, TALL, half), 0.0)
        mixed[pl.ds(start, TALL), g * half : (g + 1) * half] = jnp.sum(kept, axis=0).astype(BF16)

    scored(0, 0, 0)
    scored(1, 0, 1)

    def step(i, carry):
        first = pl.multiple_of(i * 2 * TALL, 2 * TALL)
        second = pl.multiple_of(first + TALL, TALL)
        third = pl.multiple_of(second + TALL, TALL)
        scored(2, second, 0)
        averaged(0, first, 0)
        scored(3, second, 1)
        averaged(1, first, 1)
        scored(0, third, 0)
        averaged(2, second, 0)
        scored(1, third, 1)
        averaged(3, second, 1)
        return carry

    lax.fori_loop(0, (own + 2 * TALL - 1) // (2 * TALL), step, 0)
    for j in range(lines):
        out_refs[j][0:cap, :] = mixed[pl.ds(pl.multiple_of(offsets[j], 16), cap), :]
        if with_notes:
            entry = iota((16, 1), 0)
            now = member_ref[j : j + 1, :].astype(F32)
            later = member_ref[8 + j : 9 + j, :].astype(F32)
            note = jnp.where(entry == 0, now, jnp.where(entry == 1, later, 0.0))
            out_refs[j][cap : cap + 16, :] = note.astype(BF16)


def store_body(plan, b, last, *refs):
    lines, cap, rows = plan.lines, plan.cap, plan.rows
    piece_refs, refs = refs[:lines], refs[lines:]
    if b:
        note_refs, refs = refs[:lines], refs[lines:]
    else:
        note_refs = piece_refs
    state_ref, gain_ref, proj_ref, fc1_ref, fc2_ref = refs[:5]
    refs = refs[5:]
    state_out, send_refs = refs[0], refs[1:]
    notes = [r[cap : cap + 16, :].astype(F32) for r in note_refs]
    members = jnp.concatenate(notes, axis=0)
    ranks = matmul(members.astype(BF16), earlier_mask(rows))
    slot = iota((cap, 1), 0).astype(F32)

    def places(j, block):
        at = 16 * j + block
        where = jnp.where(members[at : at + 1] > 0.5, ranks[at : at + 1], -1.0)
        return ones_where(slot == where)

    where_from = jnp.concatenate([places(j, b) for j in range(lines)], axis=0)
    pieces = jnp.concatenate([r[0:cap, :] for r in piece_refs], axis=0)
    mixed = matmul(where_from, pieces, TN).astype(BF16)
    attended = state_ref[...] + matmul(mixed, proj_ref[b])
    normed_two = layer_norm(attended, gain_ref[b, 1:2, :]).astype(BF16)
    hidden = matmul(normed_two, fc1_ref[b])
    expanded = (0.5 * hidden * (1.0 + lax.erf(hidden * (0.5**0.5)))).astype(BF16)
    state = attended + matmul(expanded, fc2_ref[b])
    state_out[...] = state
    if not last:
        normed = layer_norm(state, gain_ref[b + 1, 0:1, :]).astype(BF16)
        for j in range(lines):
            send_refs[j][...] = matmul(places(j, b + 1), normed).astype(BF16)


def move(block, peers, route):
    slabs = len(route)
    pairs = [
        (slabs * i + s, slabs * route[s](i) + s)
        for s in range(slabs)
        if route[s]
        for i in range(peers)
    ]
    return lax.ppermute(block, ("pts", "slab"), pairs)


def struct(shape, dtype):
    return jax.ShapeDtypeStruct(shape, dtype)


def by_lines(plan, features, orders, norm_gains, qkv_weight, proj_weight, fc1_weight, fc2_weight):
    rows, width, peers = plan.rows, plan.width, plan.peers
    group, lines, held, cap = plan.group, plan.lines, plan.held, plan.cap
    blocks = orders.shape[0]
    me = lax.axis_index("pts").astype(I32)
    slab = lax.axis_index("slab").astype(I32)
    shift = group.bit_length() - 1
    high, low = me >> shift, me & (group - 1)
    by_slab = lambda first, second: jnp.where(slab == 0, first, second)
    place = jnp.stack(
        [by_slab(high, low), by_slab(low, high), by_slab(group, 1), by_slab(1, group), slab]
    ).astype(I32)

    def along_line(pieces):
        def far(j):
            return move(pieces[j], peers, [lambda i: i ^ (group * j), lambda i: i ^ j])

        return [pieces[0]] + [far(j) for j in range(1, lines)]

    def from_group(piece, k):
        return move(piece, peers, [lambda i: i ^ k, lambda i: i ^ (group * k)])

    turned = move(
        orders, peers, [None, lambda i: (i & (group - 1)) * group + (i >> shift)]
    )
    normed, own_orders = kernel_call(
        norm_body, [struct((rows, width), BF16), struct(orders.shape, I32)], [whole()] * 3
    )(features, norm_gains, orders)
    normed, kept, sent = kernel_call(
        functools.partial(note_body, plan),
        [struct((rows, width), BF16)] + [struct((64, width), BF16)] * 2,
        [scalars()] + [whole()] * 3,
    )(place, normed, own_orders, turned)
    line_rows = along_line([normed] * lines)
    mine, sent = kernel_call(join_body, [struct((32, width), BF16)] * 2, [whole()] * 2)(
        kept, from_group(sent, 1)
    )
    notes = [mine, from_group(sent, 2)]
    packed, counts, members = kernel_call(
        functools.partial(first_pack_body, plan),
        [struct((held, width), BF16), struct((16, 128), I32), struct((16, width), BF16)],
        [whole()] * (lines + 2),
    )(*line_rows, *notes)
    state = features
    for b in range(blocks):
        last = b == blocks - 1
        tall = cap if b else cap + 16
        parts = [packed] + [from_group(packed, k) for k in range(1, group)]
        (queries,) = kernel_call(
            functools.partial(query_body, plan, b),
            [struct((held + 2 * TALL, width), BF16)],
            [whole(), whole()],
        )(packed, qkv_weight)
        extra = [] if b else [members]
        mixed = kernel_call(
            functools.partial(attend_body, plan, b, b == 0),
            [struct((tall, width), BF16)] * lines,
            [scalars()] + [whole()] * (group + 2 + len(extra)),
            [
                pltpu.VMEM((PATCH + held, width), BF16),
                pltpu.VMEM((width, PATCH), BF16),
                pltpu.VMEM((2, PATCH, width), BF16),
                pltpu.VMEM((held + cap, width), BF16),
                pltpu.VMEM((4, HEADS // 2 * TALL, PATCH), F32),
            ],
        )(counts, *parts, qkv_weight, queries, *extra)
        pieces = along_line(mixed)
        if b == 0:
            kept = pieces
        outs = [struct((rows, width), F32)]
        if not last:
            outs += [struct((cap, width), BF16)] * lines
        stored = kernel_call(
            functools.partial(store_body, plan, b, last),
            outs,
            [whole()] * (lines * (2 if b else 1) + 5),
        )(
            *pieces,
            *(kept if b else []),
            state,
            norm_gains,
            proj_weight,
            fc1_weight,
            fc2_weight,
        )
        state = stored[0]
        if not last:
            arrived = along_line(stored[1:])
            (packed,) = kernel_call(
                functools.partial(pack_body, plan, b + 1),
                [struct((held, width), BF16)],
                [scalars()] + [whole()] * lines,
                [pltpu.VMEM((held + cap, width), BF16)],
            )(counts, *arrived)
    return state


def from_partner(block, axis, bit):
    count = lax.axis_size(axis)
    route = []
    for low in range(count):
        high = low | 1 << bit
        if high != low and high < count:
            route += [(low, high), (high, low)]
    return lax.ppermute(block, axis, route)


def routing(order_row, row_count, peers, capacity):
    owner_dev = order_row // row_count
    within = order_row % row_count
    onehot = (owner_dev[:, None] == jnp.arange(peers, dtype=jnp.int32)[None, :]).astype(jnp.int32)
    earlier = jnp.cumsum(onehot, axis=0) - onehot
    rank_pos = jnp.sum(onehot * earlier, axis=1)
    slot_pos = owner_dev * capacity + rank_pos
    request = jnp.full((peers * capacity,), row_count, jnp.int32).at[slot_pos].set(within)
    received = lax.all_to_all(request, "pts", split_axis=0, concat_axis=0, tiled=True)
    return (slot_pos, received)


def feed_forward(attended, gain_row, first_weight, second_weight):
    normed_two = layer_norm(attended, gain_row).astype(jnp.bfloat16)
    expanded = jax.nn.gelu(
        jnp.dot(normed_two, first_weight, preferred_element_type=jnp.float32), approximate=False
    ).astype(jnp.bfloat16)
    return jnp.dot(expanded, second_weight, preferred_element_type=jnp.float32)


def mix_heads(normed, in_weight):
    row_count, model_width = normed.shape
    projected_all = jnp.dot(normed, in_weight, preferred_element_type=jnp.float32).astype(
        jnp.bfloat16
    )
    queries = projected_all[:, :model_width]
    paired = projected_all[:, model_width:]
    doublings = (PATCH // row_count).bit_length() - 1
    gathered = paired
    for bit_index in range(doublings):
        gathered = jnp.concatenate((gathered, from_partner(gathered, "pts", bit_index)), axis=0)
    keys_all = gathered[:, :model_width]
    values_all = gathered[:, model_width:]
    head_size = model_width // HEADS
    per_group = min(4, HEADS)
    groups = HEADS // per_group
    score_scale = head_size ** (-0.5)

    def split_heads(matrix):
        return matrix.reshape(matrix.shape[0], groups, per_group, head_size).transpose(1, 0, 2, 3)

    def one_group(operands):
        query_part, key_part, value_part = operands
        scores = (
            jnp.einsum("qhd,khd->hqk", query_part, key_part, preferred_element_type=jnp.float32)
            * score_scale
        )
        row_peak = jnp.max(scores, axis=2, keepdims=True)
        weights = jnp.exp(scores - row_peak)
        probabilities = (weights / jnp.sum(weights, axis=2, keepdims=True)).astype(jnp.bfloat16)
        return jnp.einsum(
            "hqk,khd->qhd", probabilities, value_part, preferred_element_type=jnp.float32
        )

    mixed_heads = lax.map(
        one_group, (split_heads(queries), split_heads(keys_all), split_heads(values_all))
    )
    return mixed_heads.transpose(1, 0, 2, 3).reshape(row_count, model_width).astype(jnp.bfloat16)


def by_request(features, orders, norm_gains, qkv_weight, proj_weight, fc1_weight, fc2_weight):
    row_count, model_width = features.shape
    peers = lax.axis_size("pts")
    capacity = 3 * row_count // (2 * peers)
    state_rows = features
    for block_index in range(orders.shape[0]):
        slot_pos, received = routing(orders[block_index], row_count, peers, capacity)
        source_rows = jnp.minimum(received, row_count - 1)
        normed_local = layer_norm(state_rows, norm_gains[block_index, 0]).astype(jnp.bfloat16)
        arrived = lax.all_to_all(
            normed_local[source_rows], "pts", split_axis=0, concat_axis=0, tiled=True
        )
        mixed_heads = mix_heads(arrived[slot_pos], qkv_weight[block_index])
        returning = (
            jnp.zeros((peers * capacity, model_width), jnp.bfloat16).at[slot_pos].set(mixed_heads)
        )
        landed = lax.all_to_all(returning, "pts", split_axis=0, concat_axis=0, tiled=True)
        stored_mixed = (
            jnp.zeros((row_count, model_width), jnp.bfloat16).at[received].set(landed, mode="drop")
        )
        attended = state_rows + jnp.dot(
            stored_mixed, proj_weight[block_index], preferred_element_type=jnp.float32
        )
        state_rows = attended + feed_forward(
            attended, norm_gains[block_index, 1], fc1_weight[block_index], fc2_weight[block_index]
        )
    return state_rows


def local(*arrays):
    row_count, model_width = arrays[0].shape
    peers = lax.axis_size("pts")
    plan = Plan(row_count, peers, model_width)
    return by_lines(plan, *arrays) if plan.fits() else by_request(*arrays)


def solution(mesh):
    placed = (P(("slab", "pts"), None), P(None, ("slab", "pts")), P(), P(), P(), P(), P())
    return jax.shard_map(
        local, mesh=mesh, in_specs=placed, out_specs=P(("slab", "pts"), None), check_vma=False
    )
```

```python
import functools

import jax
import jax.numpy as jnp
from jax import lax
from jax.experimental import pallas as pl
from jax.experimental.pallas import tpu as pltpu
from jax.sharding import PartitionSpec as P

HEADS = 16
PATCH = 1024
TALL = 32
BF16, F32, I32 = jnp.bfloat16, jnp.float32, jnp.int32
NT = (((1,), (1,)), ((), ()))
TN = (((0,), (0,)), ((), ()))
VMEM = pltpu.VMEM


def layer_norm(values, gain_row):
    center = values - jnp.mean(values, axis=1, keepdims=True)
    spread = jnp.mean(center * center, axis=1, keepdims=True)
    return center * lax.rsqrt(spread + 1e-05) * gain_row


def matmul(a, b, dims=(((1,), (0,)), ((), ()))):
    return lax.dot_general(a, b, dims, preferred_element_type=F32)


def iota(shape, axis):
    return lax.broadcasted_iota(I32, shape, axis)


def ones_where(mask):
    return jnp.where(mask, 1.0, 0.0).astype(BF16)


def earlier_mask(count):
    return ones_where(iota((count, count), 0) < iota((count, count), 1))


def as_index(row):
    return row.astype(I32)


def slot_rows(members, ranks):
    return jnp.where(members > 0.5, ranks, -1.0)


class Plan:
    def __init__(self, row_count, peers, width):
        self.rows, self.peers, self.width = row_count, peers, width
        self.group = PATCH // row_count
        self.lines = peers // self.group
        self.base = row_count // (2 * peers)
        self.cap = 3 * self.base * self.group
        self.held = self.cap * self.lines

    def fits(self):
        return (
            self.group == 4
            and self.lines == 4
            and self.rows == self.width == 256
            and self.base % 8 == 0
        )


def kernel_call(body, outs, in_specs, scratch=()):
    return pl.pallas_call(
        body,
        out_shape=outs,
        in_specs=in_specs,
        out_specs=[pl.BlockSpec(memory_space=VMEM)] * len(outs),
        scratch_shapes=list(scratch),
        compiler_params=pltpu.CompilerParams(vmem_limit_bytes=40 * 2**20),
    )


def whole():
    return pl.BlockSpec(memory_space=VMEM)


def norm_body(feature_ref, gain_ref, order_ref, normed_ref, passed_ref):
    passed_ref[...] = order_ref[...]
    normed_ref[...] = layer_norm(feature_ref[...], gain_ref[0, 0:1, :]).astype(BF16)


def note_body(plan, place, row_ref, order_ref, turned_ref, passed_ref, kept_ref, sent_ref):
    passed_ref[...] = row_ref[...]
    line, column, line_step, column_step, slab = (place[0, i] for i in range(5))
    order = jnp.where(slab == 0, order_ref[...], turned_ref[...])
    bits = plan.rows.bit_length() - 1
    entry = iota((32, 1), 0)
    notes = None
    for b in range(order.shape[0]):
        order_row = order[b : b + 1, :]
        owner = order_row >> bits
        within = order_row & (plan.rows - 1)
        inside = ones_where(iota((plan.rows, 1), 0) == within)
        picks = []
        for k in range(plan.group):
            target = column ^ k
            member = entry - 8 * b
            stored = jnp.where(
                (member >= 0) & (member < plan.lines),
                (member ^ line) * line_step + target * column_step,
                -1,
            )
            other = entry - 16
            counted = ((other & 3) ^ line) * line_step + (target ^ (other >> 2)) * column_step
            picks.append(ones_where(owner == jnp.where(other >= 0, counted, stored)))
        pick = jnp.concatenate(picks, axis=0)
        found = matmul(pick, inside, NT)
        counts = jnp.sum(found, axis=1, keepdims=True)
        lane = iota((1, plan.width), 1)
        rowid = iota((32 * plan.group, 1), 0) & 31
        mine = (lane >= 128 * b) & (lane < 128 * (b + 1))
        part = jnp.where(rowid < 16, found, jnp.where(mine, counts, 0.0))
        notes = part if notes is None else notes + part
    for k in range(plan.group):
        half = (kept_ref, sent_ref)[k & 1]
        half[32 * (k >> 1) : 32 * (k >> 1) + 32] = notes[32 * k : 32 * (k + 1)].astype(BF16)


def join_body(kept_ref, got_ref, row_ref, mine_ref, sent_ref, passed_ref):
    passed_ref[...] = row_ref[...]
    total = (kept_ref[...].astype(F32) + got_ref[...].astype(F32)).astype(BF16)
    mine_ref[...] = total[:32]
    sent_ref[...] = total[32:]


def first_pack_body(plan, *refs):
    row_refs, note_refs = refs[:4], refs[4:6]
    packed_ref, count_ref, member_ref = refs[6:]
    total = sum(r[...].astype(F32) for r in note_refs)
    members = total[:16]
    member_ref[...] = members.astype(BF16)
    count_ref[...] = jnp.concatenate([total[16:, :64], total[16:, 128:192]], axis=1).astype(I32)
    ranks = matmul(members.astype(BF16), earlier_mask(plan.rows))
    slot = iota((plan.held, 1), 0).astype(F32)
    offset = jnp.zeros((1, 1), F32)
    out = jnp.zeros((plan.held, plan.width), F32)
    for j in range(plan.lines):
        row = members[j : j + 1]
        where = jnp.where(row > 0.5, ranks[j : j + 1] + offset, -1.0)
        out = out + matmul(ones_where(slot == where), row_refs[j][...])
        offset = offset + jnp.sum(row, axis=1, keepdims=True)
    packed_ref[...] = out.astype(BF16)


def lay_body(plan, *refs):
    piece_refs, laid_ref = refs[:-1], refs[-1]
    for j in range(plan.lines):
        laid_ref[j * plan.cap : (j + 1) * plan.cap] = piece_refs[j][...]


def pack_rows(plan, packed, offset, counts, piece_ref, room):
    if packed:
        room[pl.ds(pl.multiple_of(offset, 16), plan.held), :] = piece_ref[...]
    for j in range(plan.lines):
        if not packed:
            piece = piece_ref[j * plan.cap : (j + 1) * plan.cap, :]
            room[pl.ds(pl.multiple_of(offset, 16), plan.cap), :] = piece
        offset = offset + counts[j]
    return offset


def query_body(plan, b, count_ref, row_ref, weight_ref, query_ref, room):
    counts = [count_ref[j, 64 * b] for j in range(plan.lines)]
    room[...] = jnp.zeros(room.shape, room.dtype)
    pack_rows(plan, b == 0, 0, counts, row_ref, room)
    projected = matmul(room[0 : plan.held], weight_ref[b, :, : plan.width]).astype(BF16)
    query_ref[0 : plan.held] = (projected * ((plan.width // HEADS) ** -0.5)).astype(BF16)
    query_ref[plan.held :] = jnp.zeros((2 * TALL, plan.width), BF16)


def attend_body(plan, b, with_notes, count_ref, *refs):
    group, lines, held, cap, width = plan.group, plan.lines, plan.held, plan.cap, plan.width
    part_refs, weight_ref, query_ref = refs[:group], refs[group], refs[group + 1]
    refs = refs[group + 2 :]
    if with_notes:
        member_ref, refs = refs[0], refs[1:]
    out_refs, (all_rows, keys, values, mixed, scores) = refs[:lines], refs[lines:]
    half = width // 2
    half_heads = HEADS // 2
    offset = 0
    for k in range(group):
        counts = [count_ref[k * lines + j, 64 * b] for j in range(lines)]
        offset = pack_rows(plan, b == 0, offset, counts, part_refs[k], all_rows)
    patch_rows = all_rows[0:PATCH]
    keys[...] = matmul(
        weight_ref[b, :, width : 2 * width], patch_rows, (((0,), (1,)), ((), ()))
    ).astype(BF16)
    projected = matmul(patch_rows, weight_ref[b, :, 2 * width :]).astype(BF16)
    ones = jnp.ones((PATCH, half), BF16)
    for g in range(2):
        values[g] = jnp.concatenate([projected[:, g * half : (g + 1) * half], ones], axis=1)
    mixed[...] = jnp.zeros(mixed.shape, mixed.dtype)
    own = 0
    offsets = []
    for j in range(lines):
        offsets.append(own)
        own = own + count_ref[j, 64 * b]
    shape = (half_heads, 1, half)
    head_mask = iota(shape, 0) == iota(shape, 2) // (width // HEADS)

    def scored(slot, start, g):
        block = query_ref[pl.ds(start, TALL), g * half : (g + 1) * half]
        spread = jnp.where(head_mask, block[None], jnp.zeros((), BF16))
        scores[slot] = matmul(
            spread.reshape(half_heads * TALL, half), keys[g * half : (g + 1) * half]
        )

    def averaged(slot, start, g):
        table = scores[slot]
        weights = jnp.exp(table - jnp.max(table, axis=1, keepdims=True)).astype(BF16)
        summed = matmul(weights, values[g])
        summed = summed[:, :half] / summed[:, half:]
        kept = jnp.where(head_mask, summed.reshape(half_heads, TALL, half), 0.0)
        mixed[pl.ds(start, TALL), g * half : (g + 1) * half] = jnp.sum(kept, axis=0).astype(BF16)

    scored(0, 0, 0)
    scored(1, 0, 1)

    def step(i, carry):
        first = pl.multiple_of(i * 2 * TALL, 2 * TALL)
        second = pl.multiple_of(first + TALL, TALL)
        third = pl.multiple_of(second + TALL, TALL)
        scored(2, second, 0)
        averaged(0, first, 0)
        scored(3, second, 1)
        averaged(1, first, 1)
        scored(0, third, 0)
        averaged(2, second, 0)
        scored(1, third, 1)
        averaged(3, second, 1)
        return carry

    lax.fori_loop(0, (own + 2 * TALL - 1) // (2 * TALL), step, 0)
    for j in range(lines):
        out_refs[j][0:cap, :] = mixed[pl.ds(pl.multiple_of(offsets[j], 16), cap), :]
        if with_notes:
            entry = iota((16, 1), 0)
            now = member_ref[j : j + 1, :].astype(F32)
            later = member_ref[8 + j : 9 + j, :].astype(F32)
            note = jnp.where(entry == 0, now, jnp.where(entry == 1, later, 0.0))
            out_refs[j][cap : cap + 16, :] = note.astype(BF16)


def store_body(plan, b, last, *refs):
    lines, cap, rows = plan.lines, plan.cap, plan.rows
    piece_refs, refs = refs[:lines], refs[lines:]
    if b:
        note_refs, refs = refs[:lines], refs[lines:]
    else:
        note_refs = piece_refs
    state_ref, gain_ref, proj_ref, fc1_ref, fc2_ref = refs[:5]
    refs = refs[5:]
    state_out, send_refs = refs[0], refs[1:]
    notes = [r[cap : cap + 16, :].astype(F32) for r in note_refs]
    members = jnp.concatenate(notes, axis=0)
    ranks = matmul(members.astype(BF16), earlier_mask(rows))
    slot = iota((cap, 1), 0).astype(F32)

    def places(j, block):
        at = 16 * j + block
        where = jnp.where(members[at : at + 1] > 0.5, ranks[at : at + 1], -1.0)
        return ones_where(slot == where)

    where_from = jnp.concatenate([places(j, b) for j in range(lines)], axis=0)
    pieces = jnp.concatenate([r[0:cap, :] for r in piece_refs], axis=0)
    mixed = matmul(where_from, pieces, TN).astype(BF16)
    attended = state_ref[...] + matmul(mixed, proj_ref[b])
    normed_two = layer_norm(attended, gain_ref[b, 1:2, :]).astype(BF16)
    hidden = matmul(normed_two, fc1_ref[b])
    expanded = (0.5 * hidden * (1.0 + lax.erf(hidden * (0.5**0.5)))).astype(BF16)
    state = attended + matmul(expanded, fc2_ref[b])
    state_out[...] = state
    if not last:
        normed = layer_norm(state, gain_ref[b + 1, 0:1, :]).astype(BF16)
        for j in range(lines):
            send_refs[j][...] = matmul(places(j, b + 1), normed).astype(BF16)


def move(block, peers, route):
    slabs = len(route)
    pairs = [
        (slabs * i + s, slabs * route[s](i) + s)
        for s in range(slabs)
        if route[s]
        for i in range(peers)
    ]
    return lax.ppermute(block, ("pts", "slab"), pairs)


def struct(shape, dtype):
    return jax.ShapeDtypeStruct(shape, dtype)


def by_lines(plan, features, orders, norm_gains, qkv_weight, proj_weight, fc1_weight, fc2_weight):
    rows, width, peers = plan.rows, plan.width, plan.peers
    group, lines, held, cap = plan.group, plan.lines, plan.held, plan.cap
    blocks = orders.shape[0]
    me = lax.axis_index("pts").astype(I32)
    slab = lax.axis_index("slab").astype(I32)
    shift = group.bit_length() - 1
    high, low = me >> shift, me & (group - 1)
    by_slab = lambda first, second: jnp.where(slab == 0, first, second)
    place = jnp.stack(
        [by_slab(high, low), by_slab(low, high), by_slab(group, 1), by_slab(1, group), slab]
    ).astype(I32)[None]

    def along_line(pieces):
        def far(j):
            return move(pieces[j], peers, [lambda i: i ^ (group * j), lambda i: i ^ j])

        return [pieces[0]] + [far(j) for j in range(1, lines)]

    def from_group(piece, k):
        return move(piece, peers, [lambda i: i ^ k, lambda i: i ^ (group * k)])

    turned = move(
        orders, peers, [None, lambda i: (i & (group - 1)) * group + (i >> shift)]
    )
    normed, own_orders = kernel_call(
        norm_body, [struct((rows, width), BF16), struct(orders.shape, I32)], [whole()] * 3
    )(features, norm_gains, orders)
    normed, kept, sent = kernel_call(
        functools.partial(note_body, plan),
        [struct((rows, width), BF16)] + [struct((64, width), BF16)] * 2,
        [whole()] * 4,
    )(place, normed, own_orders, turned)
    mine, sent, near = kernel_call(
        join_body, [struct((32, width), BF16)] * 2 + [struct((rows, width), BF16)], [whole()] * 3
    )(kept, from_group(sent, 1), normed)
    line_rows = along_line([normed, near] + [normed] * (lines - 2))
    notes = [mine, from_group(sent, 2)]
    packed, counts, members = kernel_call(
        functools.partial(first_pack_body, plan),
        [struct((held, width), BF16), struct((16, 128), I32), struct((16, width), BF16)],
        [whole()] * (lines + 2),
    )(*line_rows, *notes)
    state = features
    for b in range(blocks):
        last = b == blocks - 1
        tall = cap if b else cap + 16
        parts = [packed] + [from_group(packed, k) for k in range(1, group)]
        (queries,) = kernel_call(
            functools.partial(query_body, plan, b),
            [struct((held + 2 * TALL, width), BF16)],
            [whole()] * 3,
            [pltpu.VMEM((held + cap, width), BF16)],
        )(counts, packed, qkv_weight)
        extra = [] if b else [members]
        mixed = kernel_call(
            functools.partial(attend_body, plan, b, b == 0),
            [struct((tall, width), BF16)] * lines,
            [whole()] * (group + 3 + len(extra)),
            [
                pltpu.VMEM((PATCH + held, width), BF16),
                pltpu.VMEM((width, PATCH), BF16),
                pltpu.VMEM((2, PATCH, width), BF16),
                pltpu.VMEM((held + cap, width), BF16),
                pltpu.VMEM((4, HEADS // 2 * TALL, PATCH), F32),
            ],
        )(counts, *parts, qkv_weight, queries, *extra)
        pieces = along_line(mixed)
        if b == 0:
            kept = pieces
        outs = [struct((rows, width), F32)]
        if not last:
            outs += [struct((cap, width), BF16)] * lines
        stored = kernel_call(
            functools.partial(store_body, plan, b, last),
            outs,
            [whole()] * (lines * (2 if b else 1) + 5),
        )(
            *pieces,
            *(kept if b else []),
            state,
            norm_gains,
            proj_weight,
            fc1_weight,
            fc2_weight,
        )
        state = stored[0]
        if not last:
            arrived = along_line(stored[1:])
            (packed,) = kernel_call(
                functools.partial(lay_body, plan), [struct((held, width), BF16)], [whole()] * lines
            )(*arrived)
    return state


def from_partner(block, axis, bit):
    count = lax.axis_size(axis)
    route = []
    for low in range(count):
        high = low | 1 << bit
        if high != low and high < count:
            route += [(low, high), (high, low)]
    return lax.ppermute(block, axis, route)


def routing(order_row, row_count, peers, capacity):
    owner_dev = order_row // row_count
    within = order_row % row_count
    onehot = (owner_dev[:, None] == jnp.arange(peers, dtype=jnp.int32)[None, :]).astype(jnp.int32)
    earlier = jnp.cumsum(onehot, axis=0) - onehot
    rank_pos = jnp.sum(onehot * earlier, axis=1)
    slot_pos = owner_dev * capacity + rank_pos
    request = jnp.full((peers * capacity,), row_count, jnp.int32).at[slot_pos].set(within)
    received = lax.all_to_all(request, "pts", split_axis=0, concat_axis=0, tiled=True)
    return (slot_pos, received)


def feed_forward(attended, gain_row, first_weight, second_weight):
    normed_two = layer_norm(attended, gain_row).astype(jnp.bfloat16)
    expanded = jax.nn.gelu(
        jnp.dot(normed_two, first_weight, preferred_element_type=jnp.float32), approximate=False
    ).astype(jnp.bfloat16)
    return jnp.dot(expanded, second_weight, preferred_element_type=jnp.float32)


def mix_heads(normed, in_weight):
    row_count, model_width = normed.shape
    projected_all = jnp.dot(normed, in_weight, preferred_element_type=jnp.float32).astype(
        jnp.bfloat16
    )
    queries = projected_all[:, :model_width]
    paired = projected_all[:, model_width:]
    doublings = (PATCH // row_count).bit_length() - 1
    gathered = paired
    for bit_index in range(doublings):
        gathered = jnp.concatenate((gathered, from_partner(gathered, "pts", bit_index)), axis=0)
    keys_all = gathered[:, :model_width]
    values_all = gathered[:, model_width:]
    head_size = model_width // HEADS
    per_group = min(4, HEADS)
    groups = HEADS // per_group
    score_scale = head_size ** (-0.5)

    def split_heads(matrix):
        return matrix.reshape(matrix.shape[0], groups, per_group, head_size).transpose(1, 0, 2, 3)

    def one_group(operands):
        query_part, key_part, value_part = operands
        scores = (
            jnp.einsum("qhd,khd->hqk", query_part, key_part, preferred_element_type=jnp.float32)
            * score_scale
        )
        row_peak = jnp.max(scores, axis=2, keepdims=True)
        weights = jnp.exp(scores - row_peak)
        probabilities = (weights / jnp.sum(weights, axis=2, keepdims=True)).astype(jnp.bfloat16)
        return jnp.einsum(
            "hqk,khd->qhd", probabilities, value_part, preferred_element_type=jnp.float32
        )

    mixed_heads = lax.map(
        one_group, (split_heads(queries), split_heads(keys_all), split_heads(values_all))
    )
    return mixed_heads.transpose(1, 0, 2, 3).reshape(row_count, model_width).astype(jnp.bfloat16)


def by_request(features, orders, norm_gains, qkv_weight, proj_weight, fc1_weight, fc2_weight):
    row_count, model_width = features.shape
    peers = lax.axis_size("pts")
    capacity = 3 * row_count // (2 * peers)
    state_rows = features
    for block_index in range(orders.shape[0]):
        slot_pos, received = routing(orders[block_index], row_count, peers, capacity)
        source_rows = jnp.minimum(received, row_count - 1)
        normed_local = layer_norm(state_rows, norm_gains[block_index, 0]).astype(jnp.bfloat16)
        arrived = lax.all_to_all(
            normed_local[source_rows], "pts", split_axis=0, concat_axis=0, tiled=True
        )
        mixed_heads = mix_heads(arrived[slot_pos], qkv_weight[block_index])
        returning = (
            jnp.zeros((peers * capacity, model_width), jnp.bfloat16).at[slot_pos].set(mixed_heads)
        )
        landed = lax.all_to_all(returning, "pts", split_axis=0, concat_axis=0, tiled=True)
        stored_mixed = (
            jnp.zeros((row_count, model_width), jnp.bfloat16).at[received].set(landed, mode="drop")
        )
        attended = state_rows + jnp.dot(
            stored_mixed, proj_weight[block_index], preferred_element_type=jnp.float32
        )
        state_rows = attended + feed_forward(
            attended, norm_gains[block_index, 1], fc1_weight[block_index], fc2_weight[block_index]
        )
    return state_rows


def local(*arrays):
    row_count, model_width = arrays[0].shape
    peers = lax.axis_size("pts")
    plan = Plan(row_count, peers, model_width)
    return by_lines(plan, *arrays) if plan.fits() else by_request(*arrays)


def solution(mesh):
    placed = (P(("slab", "pts"), None), P(None, ("slab", "pts")), P(), P(), P(), P(), P())
    return jax.shard_map(
        local, mesh=mesh, in_specs=placed, out_specs=P(("slab", "pts"), None), check_vma=False
    )
```

```python
import functools

import jax
import jax.numpy as jnp
from jax import lax
from jax.experimental import pallas as pl
from jax.experimental.pallas import tpu as pltpu
from jax.sharding import PartitionSpec as P

HEADS = 16
PATCH = 1024
TALL = 32
BF16, F32, I32 = jnp.bfloat16, jnp.float32, jnp.int32
NT = (((1,), (1,)), ((), ()))
TN = (((0,), (0,)), ((), ()))
VMEM = pltpu.VMEM


def layer_norm(values, gain_row):
    center = values - jnp.mean(values, axis=1, keepdims=True)
    spread = jnp.mean(center * center, axis=1, keepdims=True)
    return center * lax.rsqrt(spread + 1e-05) * gain_row


def matmul(a, b, dims=(((1,), (0,)), ((), ()))):
    return lax.dot_general(a, b, dims, preferred_element_type=F32)


def iota(shape, axis):
    return lax.broadcasted_iota(I32, shape, axis)


def ones_where(mask):
    return jnp.where(mask, 1.0, 0.0).astype(BF16)


def earlier_mask(count):
    return ones_where(iota((count, count), 0) < iota((count, count), 1))


def as_index(row):
    return row.astype(I32)


def slot_rows(members, ranks):
    return jnp.where(members > 0.5, ranks, -1.0)


class Plan:
    def __init__(self, row_count, peers, width):
        self.rows, self.peers, self.width = row_count, peers, width
        self.group = PATCH // row_count
        self.lines = peers // self.group
        self.base = row_count // (2 * peers)
        self.cap = 3 * self.base * self.group
        self.held = self.cap * self.lines

    def fits(self):
        return (
            self.group == 4
            and self.lines == 4
            and self.rows == self.width == 256
            and self.base % 8 == 0
        )


def kernel_call(body, outs, in_specs, scratch=()):
    return pl.pallas_call(
        body,
        out_shape=outs,
        in_specs=in_specs,
        out_specs=[pl.BlockSpec(memory_space=VMEM)] * len(outs),
        scratch_shapes=list(scratch),
        compiler_params=pltpu.CompilerParams(vmem_limit_bytes=40 * 2**20),
    )


def whole():
    return pl.BlockSpec(memory_space=VMEM)


def norm_body(feature_ref, gain_ref, order_ref, normed_ref, passed_ref):
    passed_ref[...] = order_ref[...]
    normed_ref[...] = layer_norm(feature_ref[...], gain_ref[0, 0:1, :]).astype(BF16)


def note_body(plan, place, row_ref, order_ref, turned_ref, passed_ref, kept_ref, sent_ref):
    passed_ref[...] = row_ref[...]
    line, column, line_step, column_step, slab = (place[0, i] for i in range(5))
    order = jnp.where(slab == 0, order_ref[...], turned_ref[...])
    bits = plan.rows.bit_length() - 1
    entry = iota((32, 1), 0)
    notes = None
    for b in range(order.shape[0]):
        order_row = order[b : b + 1, :]
        owner = order_row >> bits
        within = order_row & (plan.rows - 1)
        inside = ones_where(iota((plan.rows, 1), 0) == within)
        picks = []
        for k in range(plan.group):
            target = column ^ k
            member = entry - 8 * b
            stored = jnp.where(
                (member >= 0) & (member < plan.lines),
                (member ^ line) * line_step + target * column_step,
                -1,
            )
            other = entry - 16
            counted = ((other & 3) ^ line) * line_step + (target ^ (other >> 2)) * column_step
            picks.append(ones_where(owner == jnp.where(other >= 0, counted, stored)))
        pick = jnp.concatenate(picks, axis=0)
        found = matmul(pick, inside, NT)
        counts = jnp.sum(found, axis=1, keepdims=True)
        lane = iota((1, plan.width), 1)
        rowid = iota((32 * plan.group, 1), 0) & 31
        mine = (lane >= 128 * b) & (lane < 128 * (b + 1))
        part = jnp.where(rowid < 16, found, jnp.where(mine, counts, 0.0))
        notes = part if notes is None else notes + part
    for k in range(plan.group):
        half = (kept_ref, sent_ref)[k & 1]
        half[32 * (k >> 1) : 32 * (k >> 1) + 32] = notes[32 * k : 32 * (k + 1)].astype(BF16)


def join_body(kept_ref, got_ref, row_ref, mine_ref, sent_ref, passed_ref):
    passed_ref[...] = row_ref[...]
    total = (kept_ref[...].astype(F32) + got_ref[...].astype(F32)).astype(BF16)
    mine_ref[...] = total[:32]
    sent_ref[...] = total[32:]


def first_pack_body(plan, *refs):
    row_refs, note_refs = refs[:4], refs[4:6]
    packed_ref, count_ref, member_ref = refs[6:]
    total = sum(r[...].astype(F32) for r in note_refs)
    members = total[:16]
    member_ref[...] = members.astype(BF16)
    count_ref[...] = jnp.concatenate([total[16:, :64], total[16:, 128:192]], axis=1).astype(I32)
    ranks = matmul(members.astype(BF16), earlier_mask(plan.rows))
    slot = iota((plan.held, 1), 0).astype(F32)
    offset = jnp.zeros((1, 1), F32)
    out = jnp.zeros((plan.held, plan.width), F32)
    for j in range(plan.lines):
        row = members[j : j + 1]
        where = jnp.where(row > 0.5, ranks[j : j + 1] + offset, -1.0)
        out = out + matmul(ones_where(slot == where), row_refs[j][...])
        offset = offset + jnp.sum(row, axis=1, keepdims=True)
    packed_ref[...] = out.astype(BF16)


def lay_body(plan, *refs):
    piece_refs, laid_ref = refs[:-1], refs[-1]
    for j in range(plan.lines):
        laid_ref[j * plan.cap : (j + 1) * plan.cap] = piece_refs[j][...]


def pack_rows(plan, packed, offset, counts, piece_ref, room):
    if packed:
        room[pl.ds(pl.multiple_of(offset, 16), plan.held), :] = piece_ref[...]
    for j in range(plan.lines):
        if not packed:
            piece = piece_ref[j * plan.cap : (j + 1) * plan.cap, :]
            room[pl.ds(pl.multiple_of(offset, 16), plan.cap), :] = piece
        offset = offset + counts[j]
    return offset


def project_pair(plan, b, rows, weight_ref, at, keys, values):
    width = plan.width
    half = width // 2
    keys[:, at] = matmul(
        weight_ref[b, :, width : 2 * width], rows, (((0,), (1,)), ((), ()))
    ).astype(BF16)
    projected = matmul(rows, weight_ref[b, :, 2 * width :]).astype(BF16)
    ones = jnp.ones((rows.shape[0], half), BF16)
    for g in range(2):
        values[g, at] = jnp.concatenate([projected[:, g * half : (g + 1) * half], ones], axis=1)


def attention(plan, own, query_ref, keys, values, at, scores, finish):
    width = plan.width
    half = width // 2
    half_heads = HEADS // 2
    shape = (half_heads, 1, half)
    head_mask = iota(shape, 0) == iota(shape, 2) // (width // HEADS)
    count = at.stop - at.start

    def own_head(table):
        kept = jnp.where(head_mask, table.reshape(half_heads, TALL, half), 0.0)
        return jnp.sum(kept, axis=0)

    def scored(slot, start, g):
        block = query_ref[pl.ds(start, TALL), g * half : (g + 1) * half]
        spread = jnp.where(head_mask, block[None], jnp.zeros((), BF16))
        scores[slot, :, 0:count] = matmul(
            spread.reshape(half_heads * TALL, half), keys[g * half : (g + 1) * half, at]
        )

    def averaged(slot, start, g):
        table = scores[slot, :, 0:count]
        peak = jnp.max(table, axis=1, keepdims=True)
        weights = jnp.exp(table - peak).astype(BF16)
        summed = matmul(weights, values[g, at])
        finish(pl.ds(start, TALL), slice(g * half, (g + 1) * half), summed, peak, own_head)

    scored(0, 0, 0)
    scored(1, 0, 1)

    def step(i, carry):
        first = pl.multiple_of(i * 2 * TALL, 2 * TALL)
        second = pl.multiple_of(first + TALL, TALL)
        third = pl.multiple_of(second + TALL, TALL)
        scored(2, second, 0)
        averaged(0, first, 0)
        scored(3, second, 1)
        averaged(1, first, 1)
        scored(0, third, 0)
        averaged(2, second, 0)
        scored(1, third, 1)
        averaged(3, second, 1)
        return carry

    lax.fori_loop(0, (own + 2 * TALL - 1) // (2 * TALL), step, 0)


def early_body(plan, b, count_ref, row_ref, weight_ref, *refs):
    query_ref, sum_ref, total_ref, peak_ref, room, keys, values, scores = refs
    rows, half = plan.rows, plan.width // 2
    counts = [count_ref[j, 64 * b] for j in range(plan.lines)]
    room[...] = jnp.zeros(room.shape, room.dtype)
    own = pack_rows(plan, b == 0, 0, counts, row_ref, room)
    projected = matmul(room[0 : plan.held], weight_ref[b, :, : plan.width]).astype(BF16)
    query_ref[0 : plan.held] = (projected * ((plan.width // HEADS) ** -0.5)).astype(BF16)
    query_ref[plan.held :] = jnp.zeros((2 * TALL, plan.width), BF16)

    def finish(at, lanes, summed, peak, own_head):
        sum_ref[at, lanes] = own_head(summed[:, :half])
        total_ref[at, lanes] = own_head(summed[:, half:])
        peak_ref[at, lanes] = own_head(jnp.broadcast_to(peak, (peak.shape[0], half)))

    @pl.when(own >= rows)
    def _():
        some = slice(0, rows)
        project_pair(plan, b, room[some], weight_ref, some, keys, values)
        attention(plan, own, query_ref, keys, values, some, scores, finish)


def attend_body(plan, b, with_notes, count_ref, *refs):
    group, lines, held, cap, width = plan.group, plan.lines, plan.held, plan.cap, plan.width
    rows, half = plan.rows, width // 2
    part_refs, weight_ref, query_ref = refs[:group], refs[group], refs[group + 1]
    sum_ref, total_ref, peak_ref = refs[group + 2 : group + 5]
    refs = refs[group + 5 :]
    if with_notes:
        member_ref, refs = refs[0], refs[1:]
    out_refs, (all_rows, keys, values, mixed, scores) = refs[:lines], refs[lines:]
    offset = 0
    for k in range(group):
        counts = [count_ref[k * lines + j, 64 * b] for j in range(lines)]
        offset = pack_rows(plan, b == 0, offset, counts, part_refs[k], all_rows)
    mixed[...] = jnp.zeros(mixed.shape, mixed.dtype)
    own = 0
    offsets = []
    for j in range(lines):
        offsets.append(own)
        own = own + count_ref[j, 64 * b]
    first, others = slice(0, rows), slice(rows, PATCH)
    project_pair(plan, b, all_rows[others], weight_ref, others, keys, values)

    def joined(at, lanes, summed, peak, own_head):
        peak = own_head(jnp.broadcast_to(peak, (peak.shape[0], half)))
        most = jnp.maximum(peak, peak_ref[at, lanes])
        here, early = jnp.exp(peak - most), jnp.exp(peak_ref[at, lanes] - most)
        over = own_head(summed[:, :half]) * here + sum_ref[at, lanes] * early
        under = own_head(summed[:, half:]) * here + total_ref[at, lanes] * early
        mixed[at, lanes] = (over / under).astype(BF16)

    def alone(at, lanes, summed, peak, own_head):
        mixed[at, lanes] = own_head(summed[:, :half] / summed[:, half:]).astype(BF16)

    @pl.when(own >= rows)
    def _():
        attention(plan, own, query_ref, keys, values, others, scores, joined)

    @pl.when(own < rows)
    def _():
        project_pair(plan, b, all_rows[first], weight_ref, first, keys, values)
        attention(plan, own, query_ref, keys, values, slice(0, PATCH), scores, alone)

    for j in range(lines):
        out_refs[j][0:cap, :] = mixed[pl.ds(pl.multiple_of(offsets[j], 16), cap), :]
        if with_notes:
            entry = iota((16, 1), 0)
            now = member_ref[j : j + 1, :].astype(F32)
            later = member_ref[8 + j : 9 + j, :].astype(F32)
            note = jnp.where(entry == 0, now, jnp.where(entry == 1, later, 0.0))
            out_refs[j][cap : cap + 16, :] = note.astype(BF16)


def store_body(plan, b, last, *refs):
    lines, cap, rows = plan.lines, plan.cap, plan.rows
    piece_refs, refs = refs[:lines], refs[lines:]
    if b:
        note_refs, refs = refs[:lines], refs[lines:]
    else:
        note_refs = piece_refs
    state_ref, gain_ref, proj_ref, fc1_ref, fc2_ref = refs[:5]
    refs = refs[5:]
    state_out, send_refs = refs[0], refs[1:]
    notes = [r[cap : cap + 16, :].astype(F32) for r in note_refs]
    members = jnp.concatenate(notes, axis=0)
    ranks = matmul(members.astype(BF16), earlier_mask(rows))
    slot = iota((cap, 1), 0).astype(F32)

    def places(j, block):
        at = 16 * j + block
        where = jnp.where(members[at : at + 1] > 0.5, ranks[at : at + 1], -1.0)
        return ones_where(slot == where)

    where_from = jnp.concatenate([places(j, b) for j in range(lines)], axis=0)
    pieces = jnp.concatenate([r[0:cap, :] for r in piece_refs], axis=0)
    mixed = matmul(where_from, pieces, TN).astype(BF16)
    attended = state_ref[...] + matmul(mixed, proj_ref[b])
    normed_two = layer_norm(attended, gain_ref[b, 1:2, :]).astype(BF16)
    state = attended
    units = fc1_ref.shape[2]
    for start in range(0, units, units // 4):
        at = slice(start, start + units // 4)
        hidden = matmul(normed_two, fc1_ref[b, :, at])
        expanded = (0.5 * hidden * (1.0 + lax.erf(hidden * (0.5**0.5)))).astype(BF16)
        state = state + matmul(expanded, fc2_ref[b, at, :])
    state_out[...] = state
    if not last:
        normed = layer_norm(state, gain_ref[b + 1, 0:1, :]).astype(BF16)
        for j in range(lines):
            send_refs[j][...] = matmul(places(j, b + 1), normed).astype(BF16)


def move(block, peers, route):
    slabs = len(route)
    pairs = [
        (slabs * i + s, slabs * route[s](i) + s)
        for s in range(slabs)
        if route[s]
        for i in range(peers)
    ]
    return lax.ppermute(block, ("pts", "slab"), pairs)


def struct(shape, dtype):
    return jax.ShapeDtypeStruct(shape, dtype)


def by_lines(plan, features, orders, norm_gains, qkv_weight, proj_weight, fc1_weight, fc2_weight):
    rows, width, peers = plan.rows, plan.width, plan.peers
    group, lines, held, cap = plan.group, plan.lines, plan.held, plan.cap
    blocks = orders.shape[0]
    me = lax.axis_index("pts").astype(I32)
    slab = lax.axis_index("slab").astype(I32)
    shift = group.bit_length() - 1
    high, low = me >> shift, me & (group - 1)
    by_slab = lambda first, second: jnp.where(slab == 0, first, second)
    place = jnp.stack(
        [by_slab(high, low), by_slab(low, high), by_slab(group, 1), by_slab(1, group), slab]
    ).astype(I32)[None]

    def along_line(pieces):
        def far(j):
            return move(pieces[j], peers, [lambda i: i ^ (group * j), lambda i: i ^ j])

        return [pieces[0]] + [far(j) for j in range(1, lines)]

    def from_group(piece, k):
        return move(piece, peers, [lambda i: i ^ k, lambda i: i ^ (group * k)])

    turned = move(
        orders, peers, [None, lambda i: (i & (group - 1)) * group + (i >> shift)]
    )
    normed, own_orders = kernel_call(
        norm_body, [struct((rows, width), BF16), struct(orders.shape, I32)], [whole()] * 3
    )(features, norm_gains, orders)
    normed, kept, sent = kernel_call(
        functools.partial(note_body, plan),
        [struct((rows, width), BF16)] + [struct((64, width), BF16)] * 2,
        [whole()] * 4,
    )(place, normed, own_orders, turned)
    mine, sent, near = kernel_call(
        join_body, [struct((32, width), BF16)] * 2 + [struct((rows, width), BF16)], [whole()] * 3
    )(kept, from_group(sent, 1), normed)
    line_rows = along_line([normed, near] + [normed] * (lines - 2))
    notes = [mine, from_group(sent, 2)]
    packed, counts, members = kernel_call(
        functools.partial(first_pack_body, plan),
        [struct((held, width), BF16), struct((16, 128), I32), struct((16, width), BF16)],
        [whole()] * (lines + 2),
    )(*line_rows, *notes)
    state = features
    for b in range(blocks):
        last = b == blocks - 1
        tall = cap if b else cap + 16
        parts = [packed] + [from_group(packed, k) for k in range(1, group)]
        table = HEADS // 2 * TALL
        early = kernel_call(
            functools.partial(early_body, plan, b),
            [struct((held + 2 * TALL, width), BF16)] + [struct((held, width), F32)] * 3,
            [whole()] * 3,
            [
                pltpu.VMEM((held + cap, width), BF16),
                pltpu.VMEM((width, rows), BF16),
                pltpu.VMEM((2, rows, width), BF16),
                pltpu.VMEM((4, table, rows), F32),
            ],
        )(counts, packed, qkv_weight)
        extra = [] if b else [members]
        mixed = kernel_call(
            functools.partial(attend_body, plan, b, b == 0),
            [struct((tall, width), BF16)] * lines,
            [whole()] * (group + 6 + len(extra)),
            [
                pltpu.VMEM((PATCH + held, width), BF16),
                pltpu.VMEM((width, PATCH), BF16),
                pltpu.VMEM((2, PATCH, width), BF16),
                pltpu.VMEM((held + cap, width), BF16),
                pltpu.VMEM((4, table, PATCH), F32),
            ],
        )(counts, *parts, qkv_weight, *early, *extra)
        pieces = along_line(mixed)
        if b == 0:
            kept = pieces
        outs = [struct((rows, width), F32)]
        if not last:
            outs += [struct((cap, width), BF16)] * lines
        stored = kernel_call(
            functools.partial(store_body, plan, b, last),
            outs,
            [whole()] * (lines * (2 if b else 1) + 5),
        )(
            *pieces,
            *(kept if b else []),
            state,
            norm_gains,
            proj_weight,
            fc1_weight,
            fc2_weight,
        )
        state = stored[0]
        if not last:
            arrived = along_line(stored[1:])
            (packed,) = kernel_call(
                functools.partial(lay_body, plan), [struct((held, width), BF16)], [whole()] * lines
            )(*arrived)
    return state


def from_partner(block, axis, bit):
    count = lax.axis_size(axis)
    route = []
    for low in range(count):
        high = low | 1 << bit
        if high != low and high < count:
            route += [(low, high), (high, low)]
    return lax.ppermute(block, axis, route)


def routing(order_row, row_count, peers, capacity):
    owner_dev = order_row // row_count
    within = order_row % row_count
    onehot = (owner_dev[:, None] == jnp.arange(peers, dtype=jnp.int32)[None, :]).astype(jnp.int32)
    earlier = jnp.cumsum(onehot, axis=0) - onehot
    rank_pos = jnp.sum(onehot * earlier, axis=1)
    slot_pos = owner_dev * capacity + rank_pos
    request = jnp.full((peers * capacity,), row_count, jnp.int32).at[slot_pos].set(within)
    received = lax.all_to_all(request, "pts", split_axis=0, concat_axis=0, tiled=True)
    return (slot_pos, received)


def feed_forward(attended, gain_row, first_weight, second_weight):
    normed_two = layer_norm(attended, gain_row).astype(jnp.bfloat16)
    expanded = jax.nn.gelu(
        jnp.dot(normed_two, first_weight, preferred_element_type=jnp.float32), approximate=False
    ).astype(jnp.bfloat16)
    return jnp.dot(expanded, second_weight, preferred_element_type=jnp.float32)


def mix_heads(normed, in_weight):
    row_count, model_width = normed.shape
    projected_all = jnp.dot(normed, in_weight, preferred_element_type=jnp.float32).astype(
        jnp.bfloat16
    )
    queries = projected_all[:, :model_width]
    paired = projected_all[:, model_width:]
    doublings = (PATCH // row_count).bit_length() - 1
    gathered = paired
    for bit_index in range(doublings):
        gathered = jnp.concatenate((gathered, from_partner(gathered, "pts", bit_index)), axis=0)
    keys_all = gathered[:, :model_width]
    values_all = gathered[:, model_width:]
    head_size = model_width // HEADS
    per_group = min(4, HEADS)
    groups = HEADS // per_group
    score_scale = head_size ** (-0.5)

    def split_heads(matrix):
        return matrix.reshape(matrix.shape[0], groups, per_group, head_size).transpose(1, 0, 2, 3)

    def one_group(operands):
        query_part, key_part, value_part = operands
        scores = (
            jnp.einsum("qhd,khd->hqk", query_part, key_part, preferred_element_type=jnp.float32)
            * score_scale
        )
        row_peak = jnp.max(scores, axis=2, keepdims=True)
        weights = jnp.exp(scores - row_peak)
        probabilities = (weights / jnp.sum(weights, axis=2, keepdims=True)).astype(jnp.bfloat16)
        return jnp.einsum(
            "hqk,khd->qhd", probabilities, value_part, preferred_element_type=jnp.float32
        )

    mixed_heads = lax.map(
        one_group, (split_heads(queries), split_heads(keys_all), split_heads(values_all))
    )
    return mixed_heads.transpose(1, 0, 2, 3).reshape(row_count, model_width).astype(jnp.bfloat16)


def by_request(features, orders, norm_gains, qkv_weight, proj_weight, fc1_weight, fc2_weight):
    row_count, model_width = features.shape
    peers = lax.axis_size("pts")
    capacity = 3 * row_count // (2 * peers)
    state_rows = features
    for block_index in range(orders.shape[0]):
        slot_pos, received = routing(orders[block_index], row_count, peers, capacity)
        source_rows = jnp.minimum(received, row_count - 1)
        normed_local = layer_norm(state_rows, norm_gains[block_index, 0]).astype(jnp.bfloat16)
        arrived = lax.all_to_all(
            normed_local[source_rows], "pts", split_axis=0, concat_axis=0, tiled=True
        )
        mixed_heads = mix_heads(arrived[slot_pos], qkv_weight[block_index])
        returning = (
            jnp.zeros((peers * capacity, model_width), jnp.bfloat16).at[slot_pos].set(mixed_heads)
        )
        landed = lax.all_to_all(returning, "pts", split_axis=0, concat_axis=0, tiled=True)
        stored_mixed = (
            jnp.zeros((row_count, model_width), jnp.bfloat16).at[received].set(landed, mode="drop")
        )
        attended = state_rows + jnp.dot(
            stored_mixed, proj_weight[block_index], preferred_element_type=jnp.float32
        )
        state_rows = attended + feed_forward(
            attended, norm_gains[block_index, 1], fc1_weight[block_index], fc2_weight[block_index]
        )
    return state_rows


def local(*arrays):
    row_count, model_width = arrays[0].shape
    peers = lax.axis_size("pts")
    plan = Plan(row_count, peers, model_width)
    return by_lines(plan, *arrays) if plan.fits() else by_request(*arrays)


def solution(mesh):
    placed = (P(("slab", "pts"), None), P(None, ("slab", "pts")), P(), P(), P(), P(), P())
    return jax.shard_map(
        local, mesh=mesh, in_specs=placed, out_specs=P(("slab", "pts"), None), check_vma=False
    )
```

```python
import functools

import jax
import jax.numpy as jnp
from jax import lax
from jax.experimental import pallas as pl
from jax.experimental.pallas import tpu as pltpu
from jax.sharding import PartitionSpec as P

HEADS = 16
PATCH = 1024
TALL = 32
BF16, F32, I32 = jnp.bfloat16, jnp.float32, jnp.int32
NT = (((1,), (1,)), ((), ()))
TN = (((0,), (0,)), ((), ()))
VMEM = pltpu.VMEM


def layer_norm(values, gain_row):
    center = values - jnp.mean(values, axis=1, keepdims=True)
    spread = jnp.mean(center * center, axis=1, keepdims=True)
    return center * lax.rsqrt(spread + 1e-05) * gain_row


def matmul(a, b, dims=(((1,), (0,)), ((), ()))):
    return lax.dot_general(a, b, dims, preferred_element_type=F32)


def iota(shape, axis):
    return lax.broadcasted_iota(I32, shape, axis)


def ones_where(mask):
    return jnp.where(mask, 1.0, 0.0).astype(BF16)


def earlier_mask(count):
    return ones_where(iota((count, count), 0) < iota((count, count), 1))


def as_index(row):
    return row.astype(I32)


def slot_rows(members, ranks):
    return jnp.where(members > 0.5, ranks, -1.0)


class Plan:
    def __init__(self, row_count, peers, width):
        self.rows, self.peers, self.width = row_count, peers, width
        self.group = PATCH // row_count
        self.lines = peers // self.group
        self.base = row_count // (2 * peers)
        self.cap = 3 * self.base * self.group
        self.held = self.cap * self.lines

    def fits(self):
        return (
            self.group == 4
            and self.lines == 4
            and self.rows == self.width == 256
            and self.base % 8 == 0
        )


def kernel_call(body, outs, in_specs, scratch=()):
    return pl.pallas_call(
        body,
        out_shape=outs,
        in_specs=in_specs,
        out_specs=[pl.BlockSpec(memory_space=VMEM)] * len(outs),
        scratch_shapes=list(scratch),
        compiler_params=pltpu.CompilerParams(vmem_limit_bytes=40 * 2**20),
    )


def whole():
    return pl.BlockSpec(memory_space=VMEM)


def norm_body(feature_ref, gain_ref, order_ref, normed_ref, passed_ref):
    passed_ref[...] = order_ref[...]
    normed_ref[...] = layer_norm(feature_ref[...], gain_ref[0, 0:1, :]).astype(BF16)


def note_body(plan, place, row_ref, order_ref, turned_ref, passed_ref, kept_ref, sent_ref):
    passed_ref[...] = row_ref[...]
    line, column, line_step, column_step, slab = (place[0, i] for i in range(5))
    order = jnp.where(slab == 0, order_ref[...], turned_ref[...])
    bits = plan.rows.bit_length() - 1
    entry = iota((32, 1), 0)
    notes = None
    for b in range(order.shape[0]):
        order_row = order[b : b + 1, :]
        owner = order_row >> bits
        within = order_row & (plan.rows - 1)
        inside = ones_where(iota((plan.rows, 1), 0) == within)
        picks = []
        for k in range(plan.group):
            target = column ^ k
            member = entry - 8 * b
            stored = jnp.where(
                (member >= 0) & (member < plan.lines),
                (member ^ line) * line_step + target * column_step,
                -1,
            )
            other = entry - 16
            counted = ((other & 3) ^ line) * line_step + (target ^ (other >> 2)) * column_step
            picks.append(ones_where(owner == jnp.where(other >= 0, counted, stored)))
        pick = jnp.concatenate(picks, axis=0)
        found = matmul(pick, inside, NT)
        counts = jnp.sum(found, axis=1, keepdims=True)
        lane = iota((1, plan.width), 1)
        rowid = iota((32 * plan.group, 1), 0) & 31
        mine = (lane >= 128 * b) & (lane < 128 * (b + 1))
        part = jnp.where(rowid < 16, found, jnp.where(mine, counts, 0.0))
        notes = part if notes is None else notes + part
    for k in range(plan.group):
        half = (kept_ref, sent_ref)[k & 1]
        half[32 * (k >> 1) : 32 * (k >> 1) + 32] = notes[32 * k : 32 * (k + 1)].astype(BF16)


def join_body(kept_ref, got_ref, row_ref, mine_ref, sent_ref, passed_ref):
    passed_ref[...] = row_ref[...]
    total = (kept_ref[...].astype(F32) + got_ref[...].astype(F32)).astype(BF16)
    mine_ref[...] = total[:32]
    sent_ref[...] = total[32:]


def first_pack_body(plan, *refs):
    row_refs, note_refs = refs[:4], refs[4:6]
    packed_ref, count_ref, member_ref = refs[6:]
    total = sum(r[...].astype(F32) for r in note_refs)
    members = total[:16]
    member_ref[...] = members.astype(BF16)
    count_ref[...] = jnp.concatenate([total[16:, :64], total[16:, 128:192]], axis=1).astype(I32)
    ranks = matmul(members.astype(BF16), earlier_mask(plan.rows))
    slot = iota((plan.held, 1), 0).astype(F32)
    offset = jnp.zeros((1, 1), F32)
    out = jnp.zeros((plan.held, plan.width), F32)
    for j in range(plan.lines):
        row = members[j : j + 1]
        where = jnp.where(row > 0.5, ranks[j : j + 1] + offset, -1.0)
        out = out + matmul(ones_where(slot == where), row_refs[j][...])
        offset = offset + jnp.sum(row, axis=1, keepdims=True)
    packed_ref[...] = out.astype(BF16)


def lay_body(plan, *refs):
    piece_refs, laid_ref = refs[:-1], refs[-1]
    for j in range(plan.lines):
        laid_ref[j * plan.cap : (j + 1) * plan.cap] = piece_refs[j][...]


def pack_rows(plan, packed, offset, counts, piece_ref, room):
    if packed:
        room[pl.ds(pl.multiple_of(offset, 16), plan.held), :] = piece_ref[...]
    for j in range(plan.lines):
        if not packed:
            piece = piece_ref[j * plan.cap : (j + 1) * plan.cap, :]
            room[pl.ds(pl.multiple_of(offset, 16), plan.cap), :] = piece
        offset = offset + counts[j]
    return offset


def project_pair(plan, b, rows, weight_ref, at, keys, values):
    width = plan.width
    half = width // 2
    keys[:, at] = matmul(
        weight_ref[b, :, width : 2 * width], rows, (((0,), (1,)), ((), ()))
    ).astype(BF16)
    projected = matmul(rows, weight_ref[b, :, 2 * width :]).astype(BF16)
    ones = jnp.ones((rows.shape[0], half), BF16)
    for g in range(2):
        values[g, at] = jnp.concatenate([projected[:, g * half : (g + 1) * half], ones], axis=1)


def attention(plan, own, query_ref, keys, values, at, scores, finish):
    width = plan.width
    half = width // 2
    half_heads = HEADS // 2
    shape = (half_heads, 1, half)
    head_mask = iota(shape, 0) == iota(shape, 2) // (width // HEADS)
    count = at.stop - at.start

    def own_head(table):
        kept = jnp.where(head_mask, table.reshape(half_heads, TALL, half), 0.0)
        return jnp.sum(kept, axis=0)

    def scored(slot, start, g):
        block = query_ref[pl.ds(start, TALL), g * half : (g + 1) * half]
        spread = jnp.where(head_mask, block[None], jnp.zeros((), BF16))
        scores[slot, :, 0:count] = matmul(
            spread.reshape(half_heads * TALL, half), keys[g * half : (g + 1) * half, at]
        )

    def averaged(slot, start, g):
        table = scores[slot, :, 0:count]
        peak = jnp.max(table, axis=1, keepdims=True)
        weights = jnp.exp(table - peak).astype(BF16)
        summed = matmul(weights, values[g, at])
        finish(pl.ds(start, TALL), slice(g * half, (g + 1) * half), summed, peak, own_head)

    scored(0, 0, 0)
    scored(1, 0, 1)

    def step(i, carry):
        first = pl.multiple_of(i * 2 * TALL, 2 * TALL)
        second = pl.multiple_of(first + TALL, TALL)
        third = pl.multiple_of(second + TALL, TALL)
        scored(2, second, 0)
        averaged(0, first, 0)
        scored(3, second, 1)
        averaged(1, first, 1)
        scored(0, third, 0)
        averaged(2, second, 0)
        scored(1, third, 1)
        averaged(3, second, 1)
        return carry

    full = own // (2 * TALL)
    lax.fori_loop(0, full, step, 0)
    rest = own - full * 2 * TALL
    first = pl.multiple_of(full * 2 * TALL, 2 * TALL)
    second = pl.multiple_of(first + TALL, TALL)

    @pl.when((rest > 0) & (rest <= TALL))
    def _():
        averaged(0, first, 0)
        averaged(1, first, 1)

    @pl.when(rest > TALL)
    def _():
        scored(2, second, 0)
        averaged(0, first, 0)
        scored(3, second, 1)
        averaged(1, first, 1)
        averaged(2, second, 0)
        averaged(3, second, 1)


def early_body(plan, b, count_ref, row_ref, weight_ref, *refs):
    query_ref, sum_ref, total_ref, peak_ref, room, keys, values, scores = refs
    rows, half = plan.rows, plan.width // 2
    counts = [count_ref[j, 64 * b] for j in range(plan.lines)]
    room[...] = jnp.zeros(room.shape, room.dtype)
    own = pack_rows(plan, b == 0, 0, counts, row_ref, room)
    projected = matmul(room[0 : plan.held], weight_ref[b, :, : plan.width]).astype(BF16)
    query_ref[0 : plan.held] = (projected * ((plan.width // HEADS) ** -0.5)).astype(BF16)
    query_ref[plan.held :] = jnp.zeros((2 * TALL, plan.width), BF16)

    def finish(at, lanes, summed, peak, own_head):
        sum_ref[at, lanes] = own_head(summed[:, :half])
        total_ref[at, lanes] = own_head(summed[:, half:])
        peak_ref[at, lanes] = own_head(jnp.broadcast_to(peak, (peak.shape[0], half)))

    @pl.when(own >= rows)
    def _():
        some = slice(0, rows)
        project_pair(plan, b, room[some], weight_ref, some, keys, values)
        attention(plan, own, query_ref, keys, values, some, scores, finish)


def attend_body(plan, b, with_notes, count_ref, *refs):
    group, lines, held, cap, width = plan.group, plan.lines, plan.held, plan.cap, plan.width
    rows, half = plan.rows, width // 2
    part_refs, weight_ref, query_ref = refs[:group], refs[group], refs[group + 1]
    sum_ref, total_ref, peak_ref = refs[group + 2 : group + 5]
    refs = refs[group + 5 :]
    if with_notes:
        member_ref, refs = refs[0], refs[1:]
    out_refs, (all_rows, keys, values, mixed, scores) = refs[:lines], refs[lines:]
    offset = 0
    for k in range(group):
        counts = [count_ref[k * lines + j, 64 * b] for j in range(lines)]
        offset = pack_rows(plan, b == 0, offset, counts, part_refs[k], all_rows)
    mixed[...] = jnp.zeros(mixed.shape, mixed.dtype)
    own = 0
    offsets = []
    for j in range(lines):
        offsets.append(own)
        own = own + count_ref[j, 64 * b]
    first, others = slice(0, rows), slice(rows, PATCH)
    project_pair(plan, b, all_rows[others], weight_ref, others, keys, values)

    def joined(at, lanes, summed, peak, own_head):
        peak = own_head(jnp.broadcast_to(peak, (peak.shape[0], half)))
        most = jnp.maximum(peak, peak_ref[at, lanes])
        here, early = jnp.exp(peak - most), jnp.exp(peak_ref[at, lanes] - most)
        over = own_head(summed[:, :half]) * here + sum_ref[at, lanes] * early
        under = own_head(summed[:, half:]) * here + total_ref[at, lanes] * early
        mixed[at, lanes] = (over / under).astype(BF16)

    def alone(at, lanes, summed, peak, own_head):
        mixed[at, lanes] = own_head(summed[:, :half] / summed[:, half:]).astype(BF16)

    @pl.when(own >= rows)
    def _():
        attention(plan, own, query_ref, keys, values, others, scores, joined)

    @pl.when(own < rows)
    def _():
        project_pair(plan, b, all_rows[first], weight_ref, first, keys, values)
        attention(plan, own, query_ref, keys, values, slice(0, PATCH), scores, alone)

    for j in range(lines):
        out_refs[j][0:cap, :] = mixed[pl.ds(pl.multiple_of(offsets[j], 16), cap), :]
        if with_notes:
            entry = iota((16, 1), 0)
            now = member_ref[j : j + 1, :].astype(F32)
            later = member_ref[8 + j : 9 + j, :].astype(F32)
            note = jnp.where(entry == 0, now, jnp.where(entry == 1, later, 0.0))
            out_refs[j][cap : cap + 16, :] = note.astype(BF16)


def slots_of(plan, note_refs):
    cap = plan.cap
    notes = [r[cap : cap + 16, :].astype(F32) for r in note_refs]
    members = jnp.concatenate(notes, axis=0)
    ranks = matmul(members.astype(BF16), earlier_mask(plan.rows))
    slot = iota((cap, 1), 0).astype(F32)

    def places(j, block):
        at = 16 * j + block
        where = jnp.where(members[at : at + 1] > 0.5, ranks[at : at + 1], -1.0)
        return ones_where(slot == where)

    return places


def place_body(plan, b, *refs):
    note_refs, where_ref = refs[:-1], refs[-1]
    places = slots_of(plan, note_refs)
    found = jnp.concatenate([places(j, b) for j in range(plan.lines)], axis=0)
    same = ones_where(iota((plan.rows, plan.rows), 0) == iota((plan.rows, plan.rows), 1))
    where_ref[...] = matmul(same, found, NT).astype(BF16)


def store_body(plan, b, last, *refs):
    lines, cap, rows = plan.lines, plan.cap, plan.rows
    piece_refs, refs = refs[:lines], refs[lines:]
    note_refs = piece_refs
    if b:
        where_ref, refs = refs[0], refs[1:]
        if not last:
            note_refs, refs = refs[:lines], refs[lines:]
    state_ref, gain_ref, proj_ref, fc1_ref, fc2_ref = refs[:5]
    refs = refs[5:]
    state_out, send_refs = refs[0], refs[1:]
    if not b or not last:
        places = slots_of(plan, note_refs)
    pieces = jnp.concatenate([r[0:cap, :] for r in piece_refs], axis=0)
    if b:
        mixed = matmul(where_ref[...], pieces).astype(BF16)
    else:
        where_from = jnp.concatenate([places(j, b) for j in range(lines)], axis=0)
        mixed = matmul(where_from, pieces, TN).astype(BF16)
    attended = state_ref[...] + matmul(mixed, proj_ref[b])
    normed_two = layer_norm(attended, gain_ref[b, 1:2, :]).astype(BF16)
    state = attended
    units = fc1_ref.shape[2]
    for start in range(0, units, units // 4):
        at = slice(start, start + units // 4)
        hidden = matmul(normed_two, fc1_ref[b, :, at])
        expanded = (0.5 * hidden * (1.0 + lax.erf(hidden * (0.5**0.5)))).astype(BF16)
        state = state + matmul(expanded, fc2_ref[b, at, :])
    state_out[...] = state
    if not last:
        normed = layer_norm(state, gain_ref[b + 1, 0:1, :]).astype(BF16)
        for j in range(lines):
            send_refs[j][...] = matmul(places(j, b + 1), normed).astype(BF16)


def move(block, peers, route):
    slabs = len(route)
    pairs = [
        (slabs * i + s, slabs * route[s](i) + s)
        for s in range(slabs)
        if route[s]
        for i in range(peers)
    ]
    return lax.ppermute(block, ("pts", "slab"), pairs)


def struct(shape, dtype):
    return jax.ShapeDtypeStruct(shape, dtype)


def by_lines(plan, features, orders, norm_gains, qkv_weight, proj_weight, fc1_weight, fc2_weight):
    rows, width, peers = plan.rows, plan.width, plan.peers
    group, lines, held, cap = plan.group, plan.lines, plan.held, plan.cap
    blocks = orders.shape[0]
    me = lax.axis_index("pts").astype(I32)
    slab = lax.axis_index("slab").astype(I32)
    shift = group.bit_length() - 1
    high, low = me >> shift, me & (group - 1)
    by_slab = lambda first, second: jnp.where(slab == 0, first, second)
    place = jnp.stack(
        [by_slab(high, low), by_slab(low, high), by_slab(group, 1), by_slab(1, group), slab]
    ).astype(I32)[None]

    def along_line(pieces):
        def far(j):
            return move(pieces[j], peers, [lambda i: i ^ (group * j), lambda i: i ^ j])

        return [pieces[0]] + [far(j) for j in range(1, lines)]

    def from_group(piece, k):
        return move(piece, peers, [lambda i: i ^ k, lambda i: i ^ (group * k)])

    turned = move(
        orders, peers, [None, lambda i: (i & (group - 1)) * group + (i >> shift)]
    )
    normed, own_orders = kernel_call(
        norm_body, [struct((rows, width), BF16), struct(orders.shape, I32)], [whole()] * 3
    )(features, norm_gains, orders)
    normed, kept, sent = kernel_call(
        functools.partial(note_body, plan),
        [struct((rows, width), BF16)] + [struct((64, width), BF16)] * 2,
        [whole()] * 4,
    )(place, normed, own_orders, turned)
    mine, sent, near = kernel_call(
        join_body, [struct((32, width), BF16)] * 2 + [struct((rows, width), BF16)], [whole()] * 3
    )(kept, from_group(sent, 1), normed)
    line_rows = along_line([normed, near] + [normed] * (lines - 2))
    notes = [mine, from_group(sent, 2)]
    packed, counts, members = kernel_call(
        functools.partial(first_pack_body, plan),
        [struct((held, width), BF16), struct((16, 128), I32), struct((16, width), BF16)],
        [whole()] * (lines + 2),
    )(*line_rows, *notes)
    state = features
    for b in range(blocks):
        last = b == blocks - 1
        tall = cap if b else cap + 16
        parts = [packed] + [from_group(packed, k) for k in range(1, group)]
        table = HEADS // 2 * TALL
        early = kernel_call(
            functools.partial(early_body, plan, b),
            [struct((held + 2 * TALL, width), BF16)] + [struct((held, width), F32)] * 3,
            [whole()] * 3,
            [
                pltpu.VMEM((held + cap, width), BF16),
                pltpu.VMEM((width, rows), BF16),
                pltpu.VMEM((2, rows, width), BF16),
                pltpu.VMEM((4, table, rows), F32),
            ],
        )(counts, packed, qkv_weight)
        extra = [] if b else [members]
        mixed = kernel_call(
            functools.partial(attend_body, plan, b, b == 0),
            [struct((tall, width), BF16)] * lines,
            [whole()] * (group + 6 + len(extra)),
            [
                pltpu.VMEM((PATCH + held, width), BF16),
                pltpu.VMEM((width, PATCH), BF16),
                pltpu.VMEM((2, PATCH, width), BF16),
                pltpu.VMEM((held + cap, width), BF16),
                pltpu.VMEM((4, table, PATCH), F32),
            ],
        )(counts, *parts, qkv_weight, *early, *extra)
        pieces = along_line(mixed)
        if b == 0:
            kept_notes, told = pieces, []
        else:
            told = kernel_call(
                functools.partial(place_body, plan, b),
                [struct((rows, held), BF16)],
                [whole()] * lines,
            )(*kept_notes)
            told = list(told) + ([] if last else kept_notes)
        outs = [struct((rows, width), F32)]
        if not last:
            outs += [struct((cap, width), BF16)] * lines
        stored = kernel_call(
            functools.partial(store_body, plan, b, last), outs, [whole()] * (lines + len(told) + 5)
        )(*pieces, *told, state, norm_gains, proj_weight, fc1_weight, fc2_weight)
        state = stored[0]
        if not last:
            arrived = along_line(stored[1:])
            (packed,) = kernel_call(
                functools.partial(lay_body, plan), [struct((held, width), BF16)], [whole()] * lines
            )(*arrived)
    return state


def from_partner(block, axis, bit):
    count = lax.axis_size(axis)
    route = []
    for low in range(count):
        high = low | 1 << bit
        if high != low and high < count:
            route += [(low, high), (high, low)]
    return lax.ppermute(block, axis, route)


def routing(order_row, row_count, peers, capacity):
    owner_dev = order_row // row_count
    within = order_row % row_count
    onehot = (owner_dev[:, None] == jnp.arange(peers, dtype=jnp.int32)[None, :]).astype(jnp.int32)
    earlier = jnp.cumsum(onehot, axis=0) - onehot
    rank_pos = jnp.sum(onehot * earlier, axis=1)
    slot_pos = owner_dev * capacity + rank_pos
    request = jnp.full((peers * capacity,), row_count, jnp.int32).at[slot_pos].set(within)
    received = lax.all_to_all(request, "pts", split_axis=0, concat_axis=0, tiled=True)
    return (slot_pos, received)


def feed_forward(attended, gain_row, first_weight, second_weight):
    normed_two = layer_norm(attended, gain_row).astype(jnp.bfloat16)
    expanded = jax.nn.gelu(
        jnp.dot(normed_two, first_weight, preferred_element_type=jnp.float32), approximate=False
    ).astype(jnp.bfloat16)
    return jnp.dot(expanded, second_weight, preferred_element_type=jnp.float32)


def mix_heads(normed, in_weight):
    row_count, model_width = normed.shape
    projected_all = jnp.dot(normed, in_weight, preferred_element_type=jnp.float32).astype(
        jnp.bfloat16
    )
    queries = projected_all[:, :model_width]
    paired = projected_all[:, model_width:]
    doublings = (PATCH // row_count).bit_length() - 1
    gathered = paired
    for bit_index in range(doublings):
        gathered = jnp.concatenate((gathered, from_partner(gathered, "pts", bit_index)), axis=0)
    keys_all = gathered[:, :model_width]
    values_all = gathered[:, model_width:]
    head_size = model_width // HEADS
    per_group = min(4, HEADS)
    groups = HEADS // per_group
    score_scale = head_size ** (-0.5)

    def split_heads(matrix):
        return matrix.reshape(matrix.shape[0], groups, per_group, head_size).transpose(1, 0, 2, 3)

    def one_group(operands):
        query_part, key_part, value_part = operands
        scores = (
            jnp.einsum("qhd,khd->hqk", query_part, key_part, preferred_element_type=jnp.float32)
            * score_scale
        )
        row_peak = jnp.max(scores, axis=2, keepdims=True)
        weights = jnp.exp(scores - row_peak)
        probabilities = (weights / jnp.sum(weights, axis=2, keepdims=True)).astype(jnp.bfloat16)
        return jnp.einsum(
            "hqk,khd->qhd", probabilities, value_part, preferred_element_type=jnp.float32
        )

    mixed_heads = lax.map(
        one_group, (split_heads(queries), split_heads(keys_all), split_heads(values_all))
    )
    return mixed_heads.transpose(1, 0, 2, 3).reshape(row_count, model_width).astype(jnp.bfloat16)


def by_request(features, orders, norm_gains, qkv_weight, proj_weight, fc1_weight, fc2_weight):
    row_count, model_width = features.shape
    peers = lax.axis_size("pts")
    capacity = 3 * row_count // (2 * peers)
    state_rows = features
    for block_index in range(orders.shape[0]):
        slot_pos, received = routing(orders[block_index], row_count, peers, capacity)
        source_rows = jnp.minimum(received, row_count - 1)
        normed_local = layer_norm(state_rows, norm_gains[block_index, 0]).astype(jnp.bfloat16)
        arrived = lax.all_to_all(
            normed_local[source_rows], "pts", split_axis=0, concat_axis=0, tiled=True
        )
        mixed_heads = mix_heads(arrived[slot_pos], qkv_weight[block_index])
        returning = (
            jnp.zeros((peers * capacity, model_width), jnp.bfloat16).at[slot_pos].set(mixed_heads)
        )
        landed = lax.all_to_all(returning, "pts", split_axis=0, concat_axis=0, tiled=True)
        stored_mixed = (
            jnp.zeros((row_count, model_width), jnp.bfloat16).at[received].set(landed, mode="drop")
        )
        attended = state_rows + jnp.dot(
            stored_mixed, proj_weight[block_index], preferred_element_type=jnp.float32
        )
        state_rows = attended + feed_forward(
            attended, norm_gains[block_index, 1], fc1_weight[block_index], fc2_weight[block_index]
        )
    return state_rows


def local(*arrays):
    row_count, model_width = arrays[0].shape
    peers = lax.axis_size("pts")
    plan = Plan(row_count, peers, model_width)
    return by_lines(plan, *arrays) if plan.fits() else by_request(*arrays)


def solution(mesh):
    placed = (P(("slab", "pts"), None), P(None, ("slab", "pts")), P(), P(), P(), P(), P())
    return jax.shard_map(
        local, mesh=mesh, in_specs=placed, out_specs=P(("slab", "pts"), None), check_vma=False
    )
```

```python
import functools

import jax
import jax.numpy as jnp
from jax import lax
from jax.experimental import pallas as pl
from jax.experimental.pallas import tpu as pltpu
from jax.sharding import PartitionSpec as P

HEADS = 16
PATCH = 1024
TALL = 32
BF16, F32, I32 = jnp.bfloat16, jnp.float32, jnp.int32
NT = (((1,), (1,)), ((), ()))
TN = (((0,), (0,)), ((), ()))
VMEM = pltpu.VMEM


def layer_norm(values, gain_row):
    center = values - jnp.mean(values, axis=1, keepdims=True)
    spread = jnp.mean(center * center, axis=1, keepdims=True)
    return center * lax.rsqrt(spread + 1e-05) * gain_row


def matmul(a, b, dims=(((1,), (0,)), ((), ()))):
    return lax.dot_general(a, b, dims, preferred_element_type=F32)


def iota(shape, axis):
    return lax.broadcasted_iota(I32, shape, axis)


def ones_where(mask):
    return jnp.where(mask, 1.0, 0.0).astype(BF16)


def earlier_mask(count):
    return ones_where(iota((count, count), 0) < iota((count, count), 1))


def as_index(row):
    return row.astype(I32)


def slot_rows(members, ranks):
    return jnp.where(members > 0.5, ranks, -1.0)


class Plan:
    def __init__(self, row_count, peers, width):
        self.rows, self.peers, self.width = row_count, peers, width
        self.group = PATCH // row_count
        self.lines = peers // self.group
        self.base = row_count // (2 * peers)
        self.cap = 3 * self.base * self.group
        self.held = self.cap * self.lines

    def fits(self):
        return (
            self.group == 4
            and self.lines == 4
            and self.rows == self.width == 256
            and self.base % 8 == 0
        )


def kernel_call(body, outs, in_specs, scratch=()):
    return pl.pallas_call(
        body,
        out_shape=outs,
        in_specs=in_specs,
        out_specs=[pl.BlockSpec(memory_space=VMEM)] * len(outs),
        scratch_shapes=list(scratch),
        compiler_params=pltpu.CompilerParams(vmem_limit_bytes=40 * 2**20),
    )


def whole():
    return pl.BlockSpec(memory_space=VMEM)


def norm_body(feature_ref, gain_ref, order_ref, normed_ref, passed_ref):
    passed_ref[...] = order_ref[...]
    normed_ref[...] = layer_norm(feature_ref[...], gain_ref[0, 0:1, :]).astype(BF16)


def note_body(plan, place, row_ref, order_ref, turned_ref, passed_ref, kept_ref, sent_ref):
    passed_ref[...] = row_ref[...]
    line, column, line_step, column_step, slab = (place[0, i] for i in range(5))
    order = jnp.where(slab == 0, order_ref[...], turned_ref[...])
    bits = plan.rows.bit_length() - 1
    entry = iota((32, 1), 0)
    notes = None
    for b in range(order.shape[0]):
        order_row = order[b : b + 1, :]
        owner = order_row >> bits
        within = order_row & (plan.rows - 1)
        inside = ones_where(iota((plan.rows, 1), 0) == within)
        picks = []
        for k in range(plan.group):
            target = column ^ k
            member = entry - 8 * b
            stored = jnp.where(
                (member >= 0) & (member < plan.lines),
                (member ^ line) * line_step + target * column_step,
                -1,
            )
            other = entry - 16
            counted = ((other & 3) ^ line) * line_step + (target ^ (other >> 2)) * column_step
            picks.append(ones_where(owner == jnp.where(other >= 0, counted, stored)))
        pick = jnp.concatenate(picks, axis=0)
        found = matmul(pick, inside, NT)
        counts = jnp.sum(found, axis=1, keepdims=True)
        lane = iota((1, plan.width), 1)
        rowid = iota((32 * plan.group, 1), 0) & 31
        mine = (lane >= 128 * b) & (lane < 128 * (b + 1))
        part = jnp.where(rowid < 16, found, jnp.where(mine, counts, 0.0))
        notes = part if notes is None else notes + part
    for k in range(plan.group):
        half = (kept_ref, sent_ref)[k & 1]
        half[32 * (k >> 1) : 32 * (k >> 1) + 32] = notes[32 * k : 32 * (k + 1)].astype(BF16)


def join_body(kept_ref, got_ref, row_ref, mine_ref, sent_ref, passed_ref):
    passed_ref[...] = row_ref[...]
    total = (kept_ref[...].astype(F32) + got_ref[...].astype(F32)).astype(BF16)
    mine_ref[...] = total[:32]
    sent_ref[...] = total[32:]


def first_pack_body(plan, *refs):
    row_refs, note_refs = refs[:4], refs[4:6]
    packed_ref, count_ref, member_ref = refs[6:]
    total = sum(r[...].astype(F32) for r in note_refs)
    members = total[:16]
    member_ref[...] = members.astype(BF16)
    count_ref[...] = jnp.concatenate([total[16:, :64], total[16:, 128:192]], axis=1).astype(I32)
    ranks = matmul(members.astype(BF16), earlier_mask(plan.rows))
    slot = iota((plan.held, 1), 0).astype(F32)
    offset = jnp.zeros((1, 1), F32)
    out = jnp.zeros((plan.held, plan.width), F32)
    for j in range(plan.lines):
        row = members[j : j + 1]
        where = jnp.where(row > 0.5, ranks[j : j + 1] + offset, -1.0)
        out = out + matmul(ones_where(slot == where), row_refs[j][...])
        offset = offset + jnp.sum(row, axis=1, keepdims=True)
    packed_ref[...] = out.astype(BF16)


def far_first(pieces):
    return list(pieces[:1]) + list(pieces[:0:-1])


def lay_body(plan, *refs):
    piece_refs, laid_ref = far_first(refs[:-1]), refs[-1]
    for j in range(plan.lines):
        laid_ref[j * plan.cap : (j + 1) * plan.cap] = piece_refs[j][...]


def pack_rows(plan, packed, offset, counts, piece_ref, room):
    if packed:
        room[pl.ds(pl.multiple_of(offset, 16), plan.held), :] = piece_ref[...]
    for j in range(plan.lines):
        if not packed:
            piece = piece_ref[j * plan.cap : (j + 1) * plan.cap, :]
            room[pl.ds(pl.multiple_of(offset, 16), plan.cap), :] = piece
        offset = offset + counts[j]
    return offset


def project_pair(plan, b, rows, weight_ref, at, keys, values):
    width = plan.width
    half = width // 2
    keys[:, at] = matmul(
        weight_ref[b, :, width : 2 * width], rows, (((0,), (1,)), ((), ()))
    ).astype(BF16)
    projected = matmul(rows, weight_ref[b, :, 2 * width :]).astype(BF16)
    ones = jnp.ones((rows.shape[0], half), BF16)
    for g in range(2):
        values[g, at] = jnp.concatenate([projected[:, g * half : (g + 1) * half], ones], axis=1)


def attention(plan, own, query_ref, keys, values, at, scores, finish):
    width = plan.width
    half = width // 2
    half_heads = HEADS // 2
    shape = (half_heads, 1, half)
    head_mask = iota(shape, 0) == iota(shape, 2) // (width // HEADS)
    count = at.stop - at.start

    def own_head(table):
        kept = jnp.where(head_mask, table.reshape(half_heads, TALL, half), 0.0)
        return jnp.sum(kept, axis=0)

    def scored(slot, start, g):
        block = query_ref[pl.ds(start, TALL), g * half : (g + 1) * half]
        spread = jnp.where(head_mask, block[None], jnp.zeros((), BF16))
        scores[slot, :, 0:count] = matmul(
            spread.reshape(half_heads * TALL, half), keys[g * half : (g + 1) * half, at]
        )

    def averaged(slot, start, g):
        table = scores[slot, :, 0:count]
        peak = jnp.max(table, axis=1, keepdims=True)
        weights = jnp.exp(table - peak).astype(BF16)
        summed = matmul(weights, values[g, at])
        finish(pl.ds(start, TALL), slice(g * half, (g + 1) * half), summed, peak, own_head)

    scored(0, 0, 0)
    scored(1, 0, 1)

    def step(i, carry):
        first = pl.multiple_of(i * 2 * TALL, 2 * TALL)
        second = pl.multiple_of(first + TALL, TALL)
        third = pl.multiple_of(second + TALL, TALL)
        scored(2, second, 0)
        averaged(0, first, 0)
        scored(3, second, 1)
        averaged(1, first, 1)
        scored(0, third, 0)
        averaged(2, second, 0)
        scored(1, third, 1)
        averaged(3, second, 1)
        return carry

    full = own // (2 * TALL)
    lax.fori_loop(0, full, step, 0)
    rest = own - full * 2 * TALL
    first = pl.multiple_of(full * 2 * TALL, 2 * TALL)
    second = pl.multiple_of(first + TALL, TALL)

    @pl.when((rest > 0) & (rest <= TALL))
    def _():
        averaged(0, first, 0)
        averaged(1, first, 1)

    @pl.when(rest > TALL)
    def _():
        scored(2, second, 0)
        averaged(0, first, 0)
        scored(3, second, 1)
        averaged(1, first, 1)
        averaged(2, second, 0)
        averaged(3, second, 1)


def early_body(plan, b, count_ref, row_ref, weight_ref, *refs):
    query_ref, sum_ref, total_ref, peak_ref, room, keys, values, scores = refs
    rows, half = plan.rows, plan.width // 2
    counts = [count_ref[j, 64 * b] for j in range(plan.lines)]
    room[...] = jnp.zeros(room.shape, room.dtype)
    own = pack_rows(plan, b == 0, 0, counts, row_ref, room)
    projected = matmul(room[0 : plan.held], weight_ref[b, :, : plan.width]).astype(BF16)
    query_ref[0 : plan.held] = (projected * ((plan.width // HEADS) ** -0.5)).astype(BF16)
    query_ref[plan.held :] = jnp.zeros((2 * TALL, plan.width), BF16)

    def finish(at, lanes, summed, peak, own_head):
        sum_ref[at, lanes] = own_head(summed[:, :half])
        total_ref[at, lanes] = own_head(summed[:, half:])
        peak_ref[at, lanes] = own_head(jnp.broadcast_to(peak, (peak.shape[0], half)))

    @pl.when(own >= rows)
    def _():
        some = slice(0, rows)
        project_pair(plan, b, room[some], weight_ref, some, keys, values)
        attention(plan, own, query_ref, keys, values, some, scores, finish)


def attend_body(plan, b, with_notes, count_ref, *refs):
    group, lines, held, cap, width = plan.group, plan.lines, plan.held, plan.cap, plan.width
    rows, half = plan.rows, width // 2
    part_refs, weight_ref, query_ref = refs[:group], refs[group], refs[group + 1]
    sum_ref, total_ref, peak_ref = refs[group + 2 : group + 5]
    refs = refs[group + 5 :]
    if with_notes:
        member_ref, refs = refs[0], refs[1:]
    out_refs, (all_rows, keys, values, mixed, scores) = refs[:lines], refs[lines:]
    offset = 0
    for k in range(group):
        counts = [count_ref[k * lines + j, 64 * b] for j in range(lines)]
        offset = pack_rows(plan, b == 0, offset, counts, part_refs[k], all_rows)
    mixed[...] = jnp.zeros(mixed.shape, mixed.dtype)
    own = 0
    offsets = []
    for j in range(lines):
        offsets.append(own)
        own = own + count_ref[j, 64 * b]
    first, others = slice(0, rows), slice(rows, PATCH)
    project_pair(plan, b, all_rows[others], weight_ref, others, keys, values)

    def joined(at, lanes, summed, peak, own_head):
        peak = own_head(jnp.broadcast_to(peak, (peak.shape[0], half)))
        most = jnp.maximum(peak, peak_ref[at, lanes])
        here, early = jnp.exp(peak - most), jnp.exp(peak_ref[at, lanes] - most)
        over = own_head(summed[:, :half]) * here + sum_ref[at, lanes] * early
        under = own_head(summed[:, half:]) * here + total_ref[at, lanes] * early
        mixed[at, lanes] = (over / under).astype(BF16)

    def alone(at, lanes, summed, peak, own_head):
        mixed[at, lanes] = own_head(summed[:, :half] / summed[:, half:]).astype(BF16)

    @pl.when(own >= rows)
    def _():
        attention(plan, own, query_ref, keys, values, others, scores, joined)

    @pl.when(own < rows)
    def _():
        project_pair(plan, b, all_rows[first], weight_ref, first, keys, values)
        attention(plan, own, query_ref, keys, values, slice(0, PATCH), scores, alone)

    for j in range(lines):
        out_refs[j][0:cap, :] = mixed[pl.ds(pl.multiple_of(offsets[j], 16), cap), :]
        if with_notes:
            entry = iota((16, 1), 0)
            now = member_ref[j : j + 1, :].astype(F32)
            later = member_ref[8 + j : 9 + j, :].astype(F32)
            note = jnp.where(entry == 0, now, jnp.where(entry == 1, later, 0.0))
            out_refs[j][cap : cap + 16, :] = note.astype(BF16)


def slots_of(plan, note_refs):
    cap = plan.cap
    notes = [r[cap : cap + 16, :].astype(F32) for r in note_refs]
    members = jnp.concatenate(notes, axis=0)
    ranks = matmul(members.astype(BF16), earlier_mask(plan.rows))
    slot = iota((cap, 1), 0).astype(F32)

    def places(j, block):
        at = 16 * j + block
        where = jnp.where(members[at : at + 1] > 0.5, ranks[at : at + 1], -1.0)
        return ones_where(slot == where)

    return places


def place_body(plan, b, *refs):
    note_refs, where_ref = refs[:-1], refs[-1]
    places = slots_of(plan, note_refs)
    found = jnp.concatenate([places(j, b) for j in range(plan.lines)], axis=0)
    same = ones_where(iota((plan.rows, plan.rows), 0) == iota((plan.rows, plan.rows), 1))
    where_ref[...] = matmul(same, found, NT).astype(BF16)


def store_body(plan, b, last, *refs):
    lines, cap, rows = plan.lines, plan.cap, plan.rows
    piece_refs, refs = far_first(refs[:lines]), refs[lines:]
    note_refs = piece_refs
    if b:
        where_ref, refs = refs[0], refs[1:]
        if not last:
            note_refs, refs = refs[:lines], refs[lines:]
    state_ref, gain_ref, proj_ref, fc1_ref, fc2_ref = refs[:5]
    refs = refs[5:]
    state_out, send_refs = refs[0], refs[1:]
    if not b or not last:
        places = slots_of(plan, note_refs)
    pieces = jnp.concatenate([r[0:cap, :] for r in piece_refs], axis=0)
    if b:
        mixed = matmul(where_ref[...], pieces).astype(BF16)
    else:
        where_from = jnp.concatenate([places(j, b) for j in range(lines)], axis=0)
        mixed = matmul(where_from, pieces, TN).astype(BF16)
    attended = state_ref[...] + matmul(mixed, proj_ref[b])
    normed_two = layer_norm(attended, gain_ref[b, 1:2, :]).astype(BF16)
    state = attended
    units = fc1_ref.shape[2]
    for start in range(0, units, units // 4):
        at = slice(start, start + units // 4)
        hidden = matmul(normed_two, fc1_ref[b, :, at])
        expanded = (0.5 * hidden * (1.0 + lax.erf(hidden * (0.5**0.5)))).astype(BF16)
        state = state + matmul(expanded, fc2_ref[b, at, :])
    state_out[...] = state
    if not last:
        normed = layer_norm(state, gain_ref[b + 1, 0:1, :]).astype(BF16)
        for j in range(lines):
            send_refs[j][...] = matmul(places(j, b + 1), normed).astype(BF16)


def move(block, peers, route):
    slabs = len(route)
    pairs = [
        (slabs * i + s, slabs * route[s](i) + s)
        for s in range(slabs)
        if route[s]
        for i in range(peers)
    ]
    return lax.ppermute(block, ("pts", "slab"), pairs)


def struct(shape, dtype):
    return jax.ShapeDtypeStruct(shape, dtype)


def by_lines(plan, features, orders, norm_gains, qkv_weight, proj_weight, fc1_weight, fc2_weight):
    rows, width, peers = plan.rows, plan.width, plan.peers
    group, lines, held, cap = plan.group, plan.lines, plan.held, plan.cap
    blocks = orders.shape[0]
    me = lax.axis_index("pts").astype(I32)
    slab = lax.axis_index("slab").astype(I32)
    shift = group.bit_length() - 1
    high, low = me >> shift, me & (group - 1)
    by_slab = lambda first, second: jnp.where(slab == 0, first, second)
    place = jnp.stack(
        [by_slab(high, low), by_slab(low, high), by_slab(group, 1), by_slab(1, group), slab]
    ).astype(I32)[None]

    def along_line(pieces):
        def far(j):
            return move(pieces[j], peers, [lambda i: i ^ (group * j), lambda i: i ^ j])

        return [pieces[0]] + [far(j) for j in range(1, lines)]

    def from_group(piece, k):
        return move(piece, peers, [lambda i: i ^ k, lambda i: i ^ (group * k)])

    turned = move(
        orders, peers, [None, lambda i: (i & (group - 1)) * group + (i >> shift)]
    )
    normed, own_orders = kernel_call(
        norm_body, [struct((rows, width), BF16), struct(orders.shape, I32)], [whole()] * 3
    )(features, norm_gains, orders)
    normed, kept, sent = kernel_call(
        functools.partial(note_body, plan),
        [struct((rows, width), BF16)] + [struct((64, width), BF16)] * 2,
        [whole()] * 4,
    )(place, normed, own_orders, turned)
    mine, sent, near = kernel_call(
        join_body, [struct((32, width), BF16)] * 2 + [struct((rows, width), BF16)], [whole()] * 3
    )(kept, from_group(sent, 1), normed)
    line_rows = along_line([normed, near] + [normed] * (lines - 2))
    notes = [mine, from_group(sent, 2)]
    packed, counts, members = kernel_call(
        functools.partial(first_pack_body, plan),
        [struct((held, width), BF16), struct((16, 128), I32), struct((16, width), BF16)],
        [whole()] * (lines + 2),
    )(*line_rows, *notes)
    state = features
    for b in range(blocks):
        last = b == blocks - 1
        tall = cap if b else cap + 16
        parts = [packed] + [from_group(packed, k) for k in range(1, group)]
        table = HEADS // 2 * TALL
        early = kernel_call(
            functools.partial(early_body, plan, b),
            [struct((held + 2 * TALL, width), BF16)] + [struct((held, width), F32)] * 3,
            [whole()] * 3,
            [
                pltpu.VMEM((held + cap, width), BF16),
                pltpu.VMEM((width, rows), BF16),
                pltpu.VMEM((2, rows, width), BF16),
                pltpu.VMEM((4, table, rows), F32),
            ],
        )(counts, packed, qkv_weight)
        extra = [] if b else [members]
        mixed = kernel_call(
            functools.partial(attend_body, plan, b, b == 0),
            [struct((tall, width), BF16)] * lines,
            [whole()] * (group + 6 + len(extra)),
            [
                pltpu.VMEM((PATCH + held, width), BF16),
                pltpu.VMEM((width, PATCH), BF16),
                pltpu.VMEM((2, PATCH, width), BF16),
                pltpu.VMEM((held + cap, width), BF16),
                pltpu.VMEM((4, table, PATCH), F32),
            ],
        )(counts, *parts, qkv_weight, *early, *extra)
        pieces = along_line(mixed)
        if b == 0:
            kept_notes, told = pieces, []
        else:
            told = kernel_call(
                functools.partial(place_body, plan, b),
                [struct((rows, held), BF16)],
                [whole()] * lines,
            )(*kept_notes)
            told = list(told) + ([] if last else kept_notes)
        outs = [struct((rows, width), F32)]
        if not last:
            outs += [struct((cap, width), BF16)] * lines
        stored = kernel_call(
            functools.partial(store_body, plan, b, last), outs, [whole()] * (lines + len(told) + 5)
        )(*far_first(pieces), *told, state, norm_gains, proj_weight, fc1_weight, fc2_weight)
        state = stored[0]
        if not last:
            arrived = along_line(stored[1:])
            (packed,) = kernel_call(
                functools.partial(lay_body, plan), [struct((held, width), BF16)], [whole()] * lines
            )(*far_first(arrived))
    return state


def from_partner(block, axis, bit):
    count = lax.axis_size(axis)
    route = []
    for low in range(count):
        high = low | 1 << bit
        if high != low and high < count:
            route += [(low, high), (high, low)]
    return lax.ppermute(block, axis, route)


def routing(order_row, row_count, peers, capacity):
    owner_dev = order_row // row_count
    within = order_row % row_count
    onehot = (owner_dev[:, None] == jnp.arange(peers, dtype=jnp.int32)[None, :]).astype(jnp.int32)
    earlier = jnp.cumsum(onehot, axis=0) - onehot
    rank_pos = jnp.sum(onehot * earlier, axis=1)
    slot_pos = owner_dev * capacity + rank_pos
    request = jnp.full((peers * capacity,), row_count, jnp.int32).at[slot_pos].set(within)
    received = lax.all_to_all(request, "pts", split_axis=0, concat_axis=0, tiled=True)
    return (slot_pos, received)


def feed_forward(attended, gain_row, first_weight, second_weight):
    normed_two = layer_norm(attended, gain_row).astype(jnp.bfloat16)
    expanded = jax.nn.gelu(
        jnp.dot(normed_two, first_weight, preferred_element_type=jnp.float32), approximate=False
    ).astype(jnp.bfloat16)
    return jnp.dot(expanded, second_weight, preferred_element_type=jnp.float32)


def mix_heads(normed, in_weight):
    row_count, model_width = normed.shape
    projected_all = jnp.dot(normed, in_weight, preferred_element_type=jnp.float32).astype(
        jnp.bfloat16
    )
    queries = projected_all[:, :model_width]
    paired = projected_all[:, model_width:]
    doublings = (PATCH // row_count).bit_length() - 1
    gathered = paired
    for bit_index in range(doublings):
        gathered = jnp.concatenate((gathered, from_partner(gathered, "pts", bit_index)), axis=0)
    keys_all = gathered[:, :model_width]
    values_all = gathered[:, model_width:]
    head_size = model_width // HEADS
    per_group = min(4, HEADS)
    groups = HEADS // per_group
    score_scale = head_size ** (-0.5)

    def split_heads(matrix):
        return matrix.reshape(matrix.shape[0], groups, per_group, head_size).transpose(1, 0, 2, 3)

    def one_group(operands):
        query_part, key_part, value_part = operands
        scores = (
            jnp.einsum("qhd,khd->hqk", query_part, key_part, preferred_element_type=jnp.float32)
            * score_scale
        )
        row_peak = jnp.max(scores, axis=2, keepdims=True)
        weights = jnp.exp(scores - row_peak)
        probabilities = (weights / jnp.sum(weights, axis=2, keepdims=True)).astype(jnp.bfloat16)
        return jnp.einsum(
            "hqk,khd->qhd", probabilities, value_part, preferred_element_type=jnp.float32
        )

    mixed_heads = lax.map(
        one_group, (split_heads(queries), split_heads(keys_all), split_heads(values_all))
    )
    return mixed_heads.transpose(1, 0, 2, 3).reshape(row_count, model_width).astype(jnp.bfloat16)


def by_request(features, orders, norm_gains, qkv_weight, proj_weight, fc1_weight, fc2_weight):
    row_count, model_width = features.shape
    peers = lax.axis_size("pts")
    capacity = 3 * row_count // (2 * peers)
    state_rows = features
    for block_index in range(orders.shape[0]):
        slot_pos, received = routing(orders[block_index], row_count, peers, capacity)
        source_rows = jnp.minimum(received, row_count - 1)
        normed_local = layer_norm(state_rows, norm_gains[block_index, 0]).astype(jnp.bfloat16)
        arrived = lax.all_to_all(
            normed_local[source_rows], "pts", split_axis=0, concat_axis=0, tiled=True
        )
        mixed_heads = mix_heads(arrived[slot_pos], qkv_weight[block_index])
        returning = (
            jnp.zeros((peers * capacity, model_width), jnp.bfloat16).at[slot_pos].set(mixed_heads)
        )
        landed = lax.all_to_all(returning, "pts", split_axis=0, concat_axis=0, tiled=True)
        stored_mixed = (
            jnp.zeros((row_count, model_width), jnp.bfloat16).at[received].set(landed, mode="drop")
        )
        attended = state_rows + jnp.dot(
            stored_mixed, proj_weight[block_index], preferred_element_type=jnp.float32
        )
        state_rows = attended + feed_forward(
            attended, norm_gains[block_index, 1], fc1_weight[block_index], fc2_weight[block_index]
        )
    return state_rows


def local(*arrays):
    row_count, model_width = arrays[0].shape
    peers = lax.axis_size("pts")
    plan = Plan(row_count, peers, model_width)
    return by_lines(plan, *arrays) if plan.fits() else by_request(*arrays)


def solution(mesh):
    placed = (P(("slab", "pts"), None), P(None, ("slab", "pts")), P(), P(), P(), P(), P())
    return jax.shard_map(
        local, mesh=mesh, in_specs=placed, out_specs=P(("slab", "pts"), None), check_vma=False
    )
```

```python
import functools

import jax
import jax.numpy as jnp
from jax import lax
from jax.experimental import pallas as pl
from jax.experimental.pallas import tpu as pltpu
from jax.sharding import PartitionSpec as P

HEADS = 16
PATCH = 1024
TALL = 32
BF16, F32, I32 = jnp.bfloat16, jnp.float32, jnp.int32
NT = (((1,), (1,)), ((), ()))
TN = (((0,), (0,)), ((), ()))
VMEM = pltpu.VMEM


def layer_norm(values, gain_row):
    center = values - jnp.mean(values, axis=1, keepdims=True)
    spread = jnp.mean(center * center, axis=1, keepdims=True)
    return center * lax.rsqrt(spread + 1e-05) * gain_row


def matmul(a, b, dims=(((1,), (0,)), ((), ()))):
    return lax.dot_general(a, b, dims, preferred_element_type=F32)


def iota(shape, axis):
    return lax.broadcasted_iota(I32, shape, axis)


def ones_where(mask):
    return jnp.where(mask, 1.0, 0.0).astype(BF16)


def earlier_mask(count):
    return ones_where(iota((count, count), 0) < iota((count, count), 1))


def as_index(row):
    return row.astype(I32)


def slot_rows(members, ranks):
    return jnp.where(members > 0.5, ranks, -1.0)


class Plan:
    def __init__(self, row_count, peers, width):
        self.rows, self.peers, self.width = row_count, peers, width
        self.group = PATCH // row_count
        self.lines = peers // self.group
        self.base = row_count // (2 * peers)
        self.cap = 3 * self.base * self.group
        self.held = self.cap * self.lines

    def fits(self):
        return (
            self.group == 4
            and self.lines == 4
            and self.rows == self.width == 256
            and self.base % 8 == 0
        )


def kernel_call(body, outs, in_specs, scratch=()):
    return pl.pallas_call(
        body,
        out_shape=outs,
        in_specs=in_specs,
        out_specs=[pl.BlockSpec(memory_space=VMEM)] * len(outs),
        scratch_shapes=list(scratch),
        compiler_params=pltpu.CompilerParams(vmem_limit_bytes=40 * 2**20),
    )


def whole():
    return pl.BlockSpec(memory_space=VMEM)


def norm_body(feature_ref, gain_ref, order_ref, normed_ref, passed_ref):
    passed_ref[...] = order_ref[...]
    normed_ref[...] = layer_norm(feature_ref[...], gain_ref[0, 0:1, :]).astype(BF16)


def note_body(plan, place, row_ref, order_ref, turned_ref, passed_ref, kept_ref, sent_ref):
    passed_ref[...] = row_ref[...]
    line, column, line_step, column_step, slab = (place[0, i] for i in range(5))
    order = jnp.where(slab == 0, order_ref[...], turned_ref[...])
    bits = plan.rows.bit_length() - 1
    entry = iota((32, 1), 0)
    notes = None
    for b in range(order.shape[0]):
        order_row = order[b : b + 1, :]
        owner = order_row >> bits
        within = order_row & (plan.rows - 1)
        inside = ones_where(iota((plan.rows, 1), 0) == within)
        picks = []
        for k in range(plan.group):
            target = column ^ k
            member = entry - 8 * b
            stored = jnp.where(
                (member >= 0) & (member < plan.lines),
                (member ^ line) * line_step + target * column_step,
                -1,
            )
            other = entry - 16
            counted = ((other & 3) ^ line) * line_step + (target ^ (other >> 2)) * column_step
            picks.append(ones_where(owner == jnp.where(other >= 0, counted, stored)))
        pick = jnp.concatenate(picks, axis=0)
        found = matmul(pick, inside, NT)
        counts = jnp.sum(found, axis=1, keepdims=True)
        lane = iota((1, plan.width), 1)
        rowid = iota((32 * plan.group, 1), 0) & 31
        mine = (lane >= 128 * b) & (lane < 128 * (b + 1))
        part = jnp.where(rowid < 16, found, jnp.where(mine, counts, 0.0))
        notes = part if notes is None else notes + part
    for k in range(plan.group):
        half = (kept_ref, sent_ref)[k & 1]
        half[32 * (k >> 1) : 32 * (k >> 1) + 32] = notes[32 * k : 32 * (k + 1)].astype(BF16)


def join_body(kept_ref, got_ref, row_ref, mine_ref, sent_ref, passed_ref):
    passed_ref[...] = row_ref[...]
    total = (kept_ref[...].astype(F32) + got_ref[...].astype(F32)).astype(BF16)
    mine_ref[...] = total[:32]
    sent_ref[...] = total[32:]


def first_pack_body(plan, *refs):
    row_refs, note_refs = refs[:4], refs[4:6]
    packed_ref, count_ref, member_ref = refs[6:]
    total = sum(r[...].astype(F32) for r in note_refs)
    members = total[:16]
    member_ref[...] = members.astype(BF16)
    count_ref[...] = jnp.concatenate([total[16:, :64], total[16:, 128:192]], axis=1).astype(I32)
    ranks = matmul(members.astype(BF16), earlier_mask(plan.rows))
    slot = iota((plan.held, 1), 0).astype(F32)
    offset = jnp.zeros((1, 1), F32)
    out = jnp.zeros((plan.held, plan.width), F32)
    for j in range(plan.lines):
        row = members[j : j + 1]
        where = jnp.where(row > 0.5, ranks[j : j + 1] + offset, -1.0)
        out = out + matmul(ones_where(slot == where), row_refs[j][...])
        offset = offset + jnp.sum(row, axis=1, keepdims=True)
    packed_ref[...] = out.astype(BF16)


def far_first(pieces):
    return list(pieces[:1]) + list(pieces[:0:-1])


def lay_body(plan, *refs):
    piece_refs, laid_ref = far_first(refs[:-1]), refs[-1]
    for j in range(plan.lines):
        laid_ref[j * plan.cap : (j + 1) * plan.cap] = piece_refs[j][...]


def pack_rows(plan, packed, offset, counts, piece_ref, room):
    if packed:
        room[pl.ds(pl.multiple_of(offset, 16), plan.held), :] = piece_ref[...]
    for j in range(plan.lines):
        if not packed:
            piece = piece_ref[j * plan.cap : (j + 1) * plan.cap, :]
            room[pl.ds(pl.multiple_of(offset, 16), plan.cap), :] = piece
        offset = offset + counts[j]
    return offset


def project_pair(plan, b, rows, weight_ref, at, keys, values):
    width = plan.width
    half = width // 2
    keys[:, at] = matmul(
        weight_ref[b, :, width : 2 * width], rows, (((0,), (1,)), ((), ()))
    ).astype(BF16)
    projected = matmul(rows, weight_ref[b, :, 2 * width :]).astype(BF16)
    ones = jnp.ones((rows.shape[0], half), BF16)
    for g in range(2):
        values[g, at] = jnp.concatenate([projected[:, g * half : (g + 1) * half], ones], axis=1)


def attention(plan, own, query_ref, keys, values, at, scores, finish):
    width = plan.width
    half = width // 2
    half_heads = HEADS // 2
    shape = (half_heads, 1, half)
    head_mask = iota(shape, 0) == iota(shape, 2) // (width // HEADS)
    count = at.stop - at.start

    def own_head(table):
        kept = jnp.where(head_mask, table.reshape(half_heads, TALL, half), 0.0)
        return jnp.sum(kept, axis=0)

    def scored(slot, start, g):
        block = query_ref[pl.ds(start, TALL), g * half : (g + 1) * half]
        spread = jnp.where(head_mask, block[None], jnp.zeros((), BF16))
        scores[slot, :, 0:count] = matmul(
            spread.reshape(half_heads * TALL, half), keys[g * half : (g + 1) * half, at]
        )

    def averaged(slot, start, g):
        table = scores[slot, :, 0:count]
        peak = jnp.max(table, axis=1, keepdims=True)
        weights = jnp.exp(table - peak).astype(BF16)
        summed = matmul(weights, values[g, at])
        finish(pl.ds(start, TALL), slice(g * half, (g + 1) * half), summed, peak, own_head)

    scored(0, 0, 0)
    scored(1, 0, 1)

    def step(i, carry):
        first = pl.multiple_of(i * 2 * TALL, 2 * TALL)
        second = pl.multiple_of(first + TALL, TALL)
        third = pl.multiple_of(second + TALL, TALL)
        scored(2, second, 0)
        averaged(0, first, 0)
        scored(3, second, 1)
        averaged(1, first, 1)
        scored(0, third, 0)
        averaged(2, second, 0)
        scored(1, third, 1)
        averaged(3, second, 1)
        return carry

    full = own // (2 * TALL)
    lax.fori_loop(0, full, step, 0)
    rest = own - full * 2 * TALL
    first = pl.multiple_of(full * 2 * TALL, 2 * TALL)
    second = pl.multiple_of(first + TALL, TALL)

    @pl.when((rest > 0) & (rest <= TALL))
    def _():
        averaged(0, first, 0)
        averaged(1, first, 1)

    @pl.when(rest > TALL)
    def _():
        scored(2, second, 0)
        averaged(0, first, 0)
        scored(3, second, 1)
        averaged(1, first, 1)
        averaged(2, second, 0)
        averaged(3, second, 1)


def early_body(plan, b, count_ref, row_ref, weight_ref, *refs):
    query_ref, sum_ref, total_ref, peak_ref, room, keys, values, scores = refs
    rows, half = plan.rows, plan.width // 2
    counts = [count_ref[j, 64 * b] for j in range(plan.lines)]
    room[...] = jnp.zeros(room.shape, room.dtype)
    own = pack_rows(plan, b == 0, 0, counts, row_ref, room)
    projected = matmul(room[0 : plan.held], weight_ref[b, :, : plan.width]).astype(BF16)
    query_ref[0 : plan.held] = (projected * ((plan.width // HEADS) ** -0.5)).astype(BF16)
    query_ref[plan.held :] = jnp.zeros((2 * TALL, plan.width), BF16)

    def finish(at, lanes, summed, peak, own_head):
        sum_ref[at, lanes] = own_head(summed[:, :half])
        total_ref[at, lanes] = own_head(summed[:, half:])
        peak_ref[at, lanes] = own_head(jnp.broadcast_to(peak, (peak.shape[0], half)))

    @pl.when(own >= rows)
    def _():
        some = slice(0, rows)
        project_pair(plan, b, room[some], weight_ref, some, keys, values)
        attention(plan, own, query_ref, keys, values, some, scores, finish)


def attend_body(plan, b, with_notes, count_ref, *refs):
    group, lines, held, cap, width = plan.group, plan.lines, plan.held, plan.cap, plan.width
    rows, half = plan.rows, width // 2
    part_refs, weight_ref, query_ref = refs[:group], refs[group], refs[group + 1]
    sum_ref, total_ref, peak_ref = refs[group + 2 : group + 5]
    refs = refs[group + 5 :]
    if with_notes:
        member_ref, refs = refs[0], refs[1:]
    out_refs, (all_rows, keys, values, mixed, scores) = refs[:lines], refs[lines:]
    offset = 0
    for k in range(group):
        counts = [count_ref[k * lines + j, 64 * b] for j in range(lines)]
        offset = pack_rows(plan, b == 0, offset, counts, part_refs[k], all_rows)
    mixed[...] = jnp.zeros(mixed.shape, mixed.dtype)
    own = 0
    offsets = []
    for j in range(lines):
        offsets.append(own)
        own = own + count_ref[j, 64 * b]
    first, others = slice(0, rows), slice(rows, PATCH)
    project_pair(plan, b, all_rows[others], weight_ref, others, keys, values)

    def joined(at, lanes, summed, peak, own_head):
        peak = own_head(jnp.broadcast_to(peak, (peak.shape[0], half)))
        most = jnp.maximum(peak, peak_ref[at, lanes])
        here, early = jnp.exp(peak - most), jnp.exp(peak_ref[at, lanes] - most)
        over = own_head(summed[:, :half]) * here + sum_ref[at, lanes] * early
        under = own_head(summed[:, half:]) * here + total_ref[at, lanes] * early
        mixed[at, lanes] = (over / under).astype(BF16)

    def alone(at, lanes, summed, peak, own_head):
        mixed[at, lanes] = own_head(summed[:, :half] / summed[:, half:]).astype(BF16)

    @pl.when(own >= rows)
    def _():
        attention(plan, own, query_ref, keys, values, others, scores, joined)

    @pl.when(own < rows)
    def _():
        project_pair(plan, b, all_rows[first], weight_ref, first, keys, values)
        attention(plan, own, query_ref, keys, values, slice(0, PATCH), scores, alone)

    if with_notes:
        members = member_ref[...].astype(F32)
    for j in range(lines):
        out_refs[j][0:cap, :] = mixed[pl.ds(pl.multiple_of(offsets[j], 16), cap), :]
        if with_notes:
            entry = iota((16, 1), 0)
            now, later = members[j : j + 1], members[8 + j : 9 + j]
            note = jnp.where(entry == 0, now, jnp.where(entry == 1, later, 0.0))
            out_refs[j][cap : cap + 16, :] = note.astype(BF16)


def slots_of(plan, note_refs):
    cap = plan.cap
    notes = [r[cap : cap + 16, :].astype(F32) for r in note_refs]
    members = jnp.concatenate(notes, axis=0)
    ranks = matmul(members.astype(BF16), earlier_mask(plan.rows))
    slot = iota((cap, 1), 0).astype(F32)

    def places(j, block):
        at = 16 * j + block
        where = jnp.where(members[at : at + 1] > 0.5, ranks[at : at + 1], -1.0)
        return ones_where(slot == where)

    return places


def place_body(plan, b, *refs):
    note_refs, where_ref = refs[:-1], refs[-1]
    places = slots_of(plan, note_refs)
    found = jnp.concatenate([places(j, b) for j in range(plan.lines)], axis=0)
    same = ones_where(iota((plan.rows, plan.rows), 0) == iota((plan.rows, plan.rows), 1))
    where_ref[...] = matmul(same, found, NT).astype(BF16)


def store_body(plan, b, last, *refs):
    lines, cap, rows = plan.lines, plan.cap, plan.rows
    piece_refs, refs = far_first(refs[:lines]), refs[lines:]
    note_refs = piece_refs
    if b:
        where_ref, refs = refs[0], refs[1:]
        if not last:
            note_refs, refs = refs[:lines], refs[lines:]
    state_ref, gain_ref, proj_ref, fc1_ref, fc2_ref = refs[:5]
    refs = refs[5:]
    state_out, send_refs = refs[0], refs[1:]
    if not b or not last:
        places = slots_of(plan, note_refs)
    pieces = jnp.concatenate([r[0:cap, :] for r in piece_refs], axis=0)
    if b:
        mixed = matmul(where_ref[...], pieces).astype(BF16)
    else:
        where_from = jnp.concatenate([places(j, b) for j in range(lines)], axis=0)
        mixed = matmul(where_from, pieces, TN).astype(BF16)
    attended = state_ref[...] + matmul(mixed, proj_ref[b])
    normed_two = layer_norm(attended, gain_ref[b, 1:2, :]).astype(BF16)
    state = attended
    units = fc1_ref.shape[2]
    for start in range(0, units, units // 4):
        at = slice(start, start + units // 4)
        hidden = matmul(normed_two, fc1_ref[b, :, at])
        expanded = (0.5 * hidden * (1.0 + lax.erf(hidden * (0.5**0.5)))).astype(BF16)
        state = state + matmul(expanded, fc2_ref[b, at, :])
    state_out[...] = state
    if not last:
        normed = layer_norm(state, gain_ref[b + 1, 0:1, :]).astype(BF16)
        for j in range(lines):
            send_refs[j][...] = matmul(places(j, b + 1), normed).astype(BF16)


def move(block, peers, route):
    slabs = len(route)
    pairs = [
        (slabs * i + s, slabs * route[s](i) + s)
        for s in range(slabs)
        if route[s]
        for i in range(peers)
    ]
    return lax.ppermute(block, ("pts", "slab"), pairs)


def struct(shape, dtype):
    return jax.ShapeDtypeStruct(shape, dtype)


def by_lines(plan, features, orders, norm_gains, qkv_weight, proj_weight, fc1_weight, fc2_weight):
    rows, width, peers = plan.rows, plan.width, plan.peers
    group, lines, held, cap = plan.group, plan.lines, plan.held, plan.cap
    blocks = orders.shape[0]
    me = lax.axis_index("pts").astype(I32)
    slab = lax.axis_index("slab").astype(I32)
    shift = group.bit_length() - 1
    high, low = me >> shift, me & (group - 1)
    by_slab = lambda first, second: jnp.where(slab == 0, first, second)
    place = jnp.stack(
        [by_slab(high, low), by_slab(low, high), by_slab(group, 1), by_slab(1, group), slab]
    ).astype(I32)[None]

    def along_line(pieces):
        def far(j):
            return move(pieces[j], peers, [lambda i: i ^ (group * j), lambda i: i ^ j])

        return [pieces[0]] + [far(j) for j in range(1, lines)]

    def from_group(piece, k):
        return move(piece, peers, [lambda i: i ^ k, lambda i: i ^ (group * k)])

    turned = move(
        orders, peers, [None, lambda i: (i & (group - 1)) * group + (i >> shift)]
    )
    normed, own_orders = kernel_call(
        norm_body, [struct((rows, width), BF16), struct(orders.shape, I32)], [whole()] * 3
    )(features, norm_gains, orders)
    normed, kept, sent = kernel_call(
        functools.partial(note_body, plan),
        [struct((rows, width), BF16)] + [struct((64, width), BF16)] * 2,
        [whole()] * 4,
    )(place, normed, own_orders, turned)
    mine, sent, near = kernel_call(
        join_body, [struct((32, width), BF16)] * 2 + [struct((rows, width), BF16)], [whole()] * 3
    )(kept, from_group(sent, 1), normed)
    line_rows = along_line([normed, near] + [normed] * (lines - 2))
    notes = [mine, from_group(sent, 2)]
    packed, counts, members = kernel_call(
        functools.partial(first_pack_body, plan),
        [struct((held, width), BF16), struct((16, 128), I32), struct((16, width), BF16)],
        [whole()] * (lines + 2),
    )(*line_rows, *notes)
    state = features
    for b in range(blocks):
        last = b == blocks - 1
        tall = cap if b else cap + 16
        parts = [packed] + [from_group(packed, k) for k in range(1, group)]
        table = HEADS // 2 * TALL
        early = kernel_call(
            functools.partial(early_body, plan, b),
            [struct((held + 2 * TALL, width), BF16)] + [struct((held, width), F32)] * 3,
            [whole()] * 3,
            [
                pltpu.VMEM((held + cap, width), BF16),
                pltpu.VMEM((width, rows), BF16),
                pltpu.VMEM((2, rows, width), BF16),
                pltpu.VMEM((4, table, rows), F32),
            ],
        )(counts, packed, qkv_weight)
        extra = [] if b else [members]
        mixed = kernel_call(
            functools.partial(attend_body, plan, b, b == 0),
            [struct((tall, width), BF16)] * lines,
            [whole()] * (group + 6 + len(extra)),
            [
                pltpu.VMEM((PATCH + held, width), BF16),
                pltpu.VMEM((width, PATCH), BF16),
                pltpu.VMEM((2, PATCH, width), BF16),
                pltpu.VMEM((held + cap, width), BF16),
                pltpu.VMEM((4, table, PATCH), F32),
            ],
        )(counts, *parts, qkv_weight, *early, *extra)
        pieces = along_line(mixed)
        if b == 0:
            kept_notes, told = pieces, []
        else:
            told = kernel_call(
                functools.partial(place_body, plan, b),
                [struct((rows, held), BF16)],
                [whole()] * lines,
            )(*kept_notes)
            told = list(told) + ([] if last else kept_notes)
        outs = [struct((rows, width), F32)]
        if not last:
            outs += [struct((cap, width), BF16)] * lines
        stored = kernel_call(
            functools.partial(store_body, plan, b, last), outs, [whole()] * (lines + len(told) + 5)
        )(*far_first(pieces), *told, state, norm_gains, proj_weight, fc1_weight, fc2_weight)
        state = stored[0]
        if not last:
            arrived = along_line(stored[1:])
            (packed,) = kernel_call(
                functools.partial(lay_body, plan), [struct((held, width), BF16)], [whole()] * lines
            )(*far_first(arrived))
    return state


def from_partner(block, axis, bit):
    count = lax.axis_size(axis)
    route = []
    for low in range(count):
        high = low | 1 << bit
        if high != low and high < count:
            route += [(low, high), (high, low)]
    return lax.ppermute(block, axis, route)


def routing(order_row, row_count, peers, capacity):
    owner_dev = order_row // row_count
    within = order_row % row_count
    onehot = (owner_dev[:, None] == jnp.arange(peers, dtype=jnp.int32)[None, :]).astype(jnp.int32)
    earlier = jnp.cumsum(onehot, axis=0) - onehot
    rank_pos = jnp.sum(onehot * earlier, axis=1)
    slot_pos = owner_dev * capacity + rank_pos
    request = jnp.full((peers * capacity,), row_count, jnp.int32).at[slot_pos].set(within)
    received = lax.all_to_all(request, "pts", split_axis=0, concat_axis=0, tiled=True)
    return (slot_pos, received)


def feed_forward(attended, gain_row, first_weight, second_weight):
    normed_two = layer_norm(attended, gain_row).astype(jnp.bfloat16)
    expanded = jax.nn.gelu(
        jnp.dot(normed_two, first_weight, preferred_element_type=jnp.float32), approximate=False
    ).astype(jnp.bfloat16)
    return jnp.dot(expanded, second_weight, preferred_element_type=jnp.float32)


def mix_heads(normed, in_weight):
    row_count, model_width = normed.shape
    projected_all = jnp.dot(normed, in_weight, preferred_element_type=jnp.float32).astype(
        jnp.bfloat16
    )
    queries = projected_all[:, :model_width]
    paired = projected_all[:, model_width:]
    doublings = (PATCH // row_count).bit_length() - 1
    gathered = paired
    for bit_index in range(doublings):
        gathered = jnp.concatenate((gathered, from_partner(gathered, "pts", bit_index)), axis=0)
    keys_all = gathered[:, :model_width]
    values_all = gathered[:, model_width:]
    head_size = model_width // HEADS
    per_group = min(4, HEADS)
    groups = HEADS // per_group
    score_scale = head_size ** (-0.5)

    def split_heads(matrix):
        return matrix.reshape(matrix.shape[0], groups, per_group, head_size).transpose(1, 0, 2, 3)

    def one_group(operands):
        query_part, key_part, value_part = operands
        scores = (
            jnp.einsum("qhd,khd->hqk", query_part, key_part, preferred_element_type=jnp.float32)
            * score_scale
        )
        row_peak = jnp.max(scores, axis=2, keepdims=True)
        weights = jnp.exp(scores - row_peak)
        probabilities = (weights / jnp.sum(weights, axis=2, keepdims=True)).astype(jnp.bfloat16)
        return jnp.einsum(
            "hqk,khd->qhd", probabilities, value_part, preferred_element_type=jnp.float32
        )

    mixed_heads = lax.map(
        one_group, (split_heads(queries), split_heads(keys_all), split_heads(values_all))
    )
    return mixed_heads.transpose(1, 0, 2, 3).reshape(row_count, model_width).astype(jnp.bfloat16)


def by_request(features, orders, norm_gains, qkv_weight, proj_weight, fc1_weight, fc2_weight):
    row_count, model_width = features.shape
    peers = lax.axis_size("pts")
    capacity = 3 * row_count // (2 * peers)
    state_rows = features
    for block_index in range(orders.shape[0]):
        slot_pos, received = routing(orders[block_index], row_count, peers, capacity)
        source_rows = jnp.minimum(received, row_count - 1)
        normed_local = layer_norm(state_rows, norm_gains[block_index, 0]).astype(jnp.bfloat16)
        arrived = lax.all_to_all(
            normed_local[source_rows], "pts", split_axis=0, concat_axis=0, tiled=True
        )
        mixed_heads = mix_heads(arrived[slot_pos], qkv_weight[block_index])
        returning = (
            jnp.zeros((peers * capacity, model_width), jnp.bfloat16).at[slot_pos].set(mixed_heads)
        )
        landed = lax.all_to_all(returning, "pts", split_axis=0, concat_axis=0, tiled=True)
        stored_mixed = (
            jnp.zeros((row_count, model_width), jnp.bfloat16).at[received].set(landed, mode="drop")
        )
        attended = state_rows + jnp.dot(
            stored_mixed, proj_weight[block_index], preferred_element_type=jnp.float32
        )
        state_rows = attended + feed_forward(
            attended, norm_gains[block_index, 1], fc1_weight[block_index], fc2_weight[block_index]
        )
    return state_rows


def local(*arrays):
    row_count, model_width = arrays[0].shape
    peers = lax.axis_size("pts")
    plan = Plan(row_count, peers, model_width)
    return by_lines(plan, *arrays) if plan.fits() else by_request(*arrays)


def solution(mesh):
    placed = (P(("slab", "pts"), None), P(None, ("slab", "pts")), P(), P(), P(), P(), P())
    return jax.shard_map(
        local, mesh=mesh, in_specs=placed, out_specs=P(("slab", "pts"), None), check_vma=False
    )
```

```python
import functools

import jax
import jax.numpy as jnp
from jax import lax
from jax.experimental import pallas as pl
from jax.experimental.pallas import tpu as pltpu
from jax.sharding import PartitionSpec as P

HEADS = 16
PATCH = 1024
TALL = 32
BF16, F32, I32 = jnp.bfloat16, jnp.float32, jnp.int32
NT = (((1,), (1,)), ((), ()))
TN = (((0,), (0,)), ((), ()))
VMEM = pltpu.VMEM


def layer_norm(values, gain_row):
    center = values - jnp.mean(values, axis=1, keepdims=True)
    spread = jnp.mean(center * center, axis=1, keepdims=True)
    return center * lax.rsqrt(spread + 1e-05) * gain_row


def matmul(a, b, dims=(((1,), (0,)), ((), ()))):
    return lax.dot_general(a, b, dims, preferred_element_type=F32)


def iota(shape, axis):
    return lax.broadcasted_iota(I32, shape, axis)


def ones_where(mask):
    return jnp.where(mask, 1.0, 0.0).astype(BF16)


def earlier_mask(count):
    return ones_where(iota((count, count), 0) < iota((count, count), 1))


def as_index(row):
    return row.astype(I32)


def slot_rows(members, ranks):
    return jnp.where(members > 0.5, ranks, -1.0)


class Plan:
    def __init__(self, row_count, peers, width):
        self.rows, self.peers, self.width = row_count, peers, width
        self.group = PATCH // row_count
        self.lines = peers // self.group
        self.base = row_count // (2 * peers)
        self.cap = 3 * self.base * self.group
        self.held = self.cap * self.lines

    def fits(self):
        return (
            self.group == 4
            and self.lines == 4
            and self.rows == self.width == 256
            and self.base % 8 == 0
        )


def kernel_call(body, outs, in_specs, scratch=()):
    return pl.pallas_call(
        body,
        out_shape=outs,
        in_specs=in_specs,
        out_specs=[pl.BlockSpec(memory_space=VMEM)] * len(outs),
        scratch_shapes=list(scratch),
        compiler_params=pltpu.CompilerParams(vmem_limit_bytes=40 * 2**20),
    )


def whole():
    return pl.BlockSpec(memory_space=VMEM)


def norm_body(feature_ref, gain_ref, normed_ref):
    normed_ref[...] = layer_norm(feature_ref[...], gain_ref[0, 0:1, :]).astype(BF16)


def note_body(plan, place, row_ref, turned_ref, passed_ref, kept_ref, sent_ref):
    passed_ref[...] = row_ref[...]
    line, column, line_step, column_step = (place[0, i] for i in range(4))
    order = turned_ref[...]
    bits = plan.rows.bit_length() - 1
    entry = iota((32, 1), 0)
    notes = None
    for b in range(order.shape[0]):
        order_row = order[b : b + 1, :]
        owner = order_row >> bits
        within = order_row & (plan.rows - 1)
        inside = ones_where(iota((plan.rows, 1), 0) == within)
        picks = []
        for k in range(plan.group):
            target = column ^ k
            member = entry - 8 * b
            stored = jnp.where(
                (member >= 0) & (member < plan.lines),
                (member ^ line) * line_step + target * column_step,
                -1,
            )
            other = entry - 16
            counted = ((other & 3) ^ line) * line_step + (target ^ (other >> 2)) * column_step
            picks.append(ones_where(owner == jnp.where(other >= 0, counted, stored)))
        pick = jnp.concatenate(picks, axis=0)
        found = matmul(pick, inside, NT)
        counts = jnp.sum(found, axis=1, keepdims=True)
        lane = iota((1, plan.width), 1)
        rowid = iota((32 * plan.group, 1), 0) & 31
        mine = (lane >= 128 * b) & (lane < 128 * (b + 1))
        part = jnp.where(rowid < 16, found, jnp.where(mine, counts, 0.0))
        notes = part if notes is None else notes + part
    for k in range(plan.group):
        half = (kept_ref, sent_ref)[k & 1]
        half[32 * (k >> 1) : 32 * (k >> 1) + 32] = notes[32 * k : 32 * (k + 1)].astype(BF16)


def join_body(kept_ref, got_ref, row_ref, mine_ref, sent_ref, passed_ref):
    passed_ref[...] = row_ref[...]
    total = (kept_ref[...].astype(F32) + got_ref[...].astype(F32)).astype(BF16)
    mine_ref[...] = total[:32]
    sent_ref[...] = total[32:]


def first_pack_body(plan, *refs):
    row_refs, note_refs = refs[:4], refs[4:6]
    packed_ref, count_ref, member_ref = refs[6:]
    total = sum(r[...].astype(F32) for r in note_refs)
    members = total[:16]
    member_ref[...] = members.astype(BF16)
    count_ref[...] = jnp.concatenate([total[16:, :64], total[16:, 128:192]], axis=1).astype(I32)
    ranks = matmul(members.astype(BF16), earlier_mask(plan.rows))
    slot = iota((plan.held, 1), 0).astype(F32)
    offset = jnp.zeros((1, 1), F32)
    out = jnp.zeros((plan.held, plan.width), F32)
    for j in range(plan.lines):
        row = members[j : j + 1]
        where = jnp.where(row > 0.5, ranks[j : j + 1] + offset, -1.0)
        out = out + matmul(ones_where(slot == where), row_refs[j][...])
        offset = offset + jnp.sum(row, axis=1, keepdims=True)
    packed_ref[...] = out.astype(BF16)


def far_first(pieces):
    return list(pieces[:1]) + list(pieces[:0:-1])


def lay_body(plan, *refs):
    piece_refs, laid_ref = far_first(refs[:-1]), refs[-1]
    for j in range(plan.lines):
        laid_ref[j * plan.cap : (j + 1) * plan.cap] = piece_refs[j][...]


def pack_rows(plan, packed, offset, counts, piece_ref, room):
    if packed:
        room[pl.ds(pl.multiple_of(offset, 16), plan.held), :] = piece_ref[...]
    for j in range(plan.lines):
        if not packed:
            piece = piece_ref[j * plan.cap : (j + 1) * plan.cap, :]
            room[pl.ds(pl.multiple_of(offset, 16), plan.cap), :] = piece
        offset = offset + counts[j]
    return offset


def project_pair(plan, b, rows, weight_ref, at, keys, values):
    width = plan.width
    half = width // 2
    keys[:, at] = matmul(
        weight_ref[b, :, width : 2 * width], rows, (((0,), (1,)), ((), ()))
    ).astype(BF16)
    projected = matmul(rows, weight_ref[b, :, 2 * width :]).astype(BF16)
    ones = jnp.ones((rows.shape[0], half), BF16)
    for g in range(2):
        values[g, at] = jnp.concatenate([projected[:, g * half : (g + 1) * half], ones], axis=1)


def attention(plan, own, query_ref, keys, values, at, scores, finish):
    width = plan.width
    half = width // 2
    half_heads = HEADS // 2
    shape = (half_heads, 1, half)
    head_mask = iota(shape, 0) == iota(shape, 2) // (width // HEADS)
    count = at.stop - at.start

    def own_head(table):
        kept = jnp.where(head_mask, table.reshape(half_heads, TALL, half), 0.0)
        return jnp.sum(kept, axis=0)

    def scored(slot, start, g):
        block = query_ref[pl.ds(start, TALL), g * half : (g + 1) * half]
        spread = jnp.where(head_mask, block[None], jnp.zeros((), BF16))
        scores[slot, :, 0:count] = matmul(
            spread.reshape(half_heads * TALL, half), keys[g * half : (g + 1) * half, at]
        )

    def averaged(slot, start, g):
        table = scores[slot, :, 0:count]
        peak = jnp.max(table, axis=1, keepdims=True)
        weights = jnp.exp(table - peak).astype(BF16)
        summed = matmul(weights, values[g, at])
        finish(pl.ds(start, TALL), slice(g * half, (g + 1) * half), summed, peak, own_head)

    scored(0, 0, 0)
    scored(1, 0, 1)

    def step(i, carry):
        first = pl.multiple_of(i * 2 * TALL, 2 * TALL)
        second = pl.multiple_of(first + TALL, TALL)
        third = pl.multiple_of(second + TALL, TALL)
        scored(2, second, 0)
        averaged(0, first, 0)
        scored(3, second, 1)
        averaged(1, first, 1)
        scored(0, third, 0)
        averaged(2, second, 0)
        scored(1, third, 1)
        averaged(3, second, 1)
        return carry

    full = own // (2 * TALL)
    lax.fori_loop(0, full, step, 0)
    rest = own - full * 2 * TALL
    first = pl.multiple_of(full * 2 * TALL, 2 * TALL)
    second = pl.multiple_of(first + TALL, TALL)

    @pl.when((rest > 0) & (rest <= TALL))
    def _():
        averaged(0, first, 0)
        averaged(1, first, 1)

    @pl.when(rest > TALL)
    def _():
        scored(2, second, 0)
        averaged(0, first, 0)
        scored(3, second, 1)
        averaged(1, first, 1)
        averaged(2, second, 0)
        averaged(3, second, 1)


def early_body(plan, b, count_ref, row_ref, weight_ref, *refs):
    query_ref, sum_ref, total_ref, peak_ref, room, keys, values, scores = refs
    rows, half = plan.rows, plan.width // 2
    counts = [count_ref[j, 64 * b] for j in range(plan.lines)]
    room[...] = jnp.zeros(room.shape, room.dtype)
    own = pack_rows(plan, b == 0, 0, counts, row_ref, room)
    projected = matmul(room[0 : plan.held], weight_ref[b, :, : plan.width]).astype(BF16)
    query_ref[0 : plan.held] = (projected * ((plan.width // HEADS) ** -0.5)).astype(BF16)
    query_ref[plan.held :] = jnp.zeros((2 * TALL, plan.width), BF16)

    def finish(at, lanes, summed, peak, own_head):
        sum_ref[at, lanes] = own_head(summed[:, :half])
        total_ref[at, lanes] = own_head(summed[:, half:])
        peak_ref[at, lanes] = own_head(jnp.broadcast_to(peak, (peak.shape[0], half)))

    @pl.when(own >= rows)
    def _():
        some = slice(0, rows)
        project_pair(plan, b, room[some], weight_ref, some, keys, values)
        attention(plan, own, query_ref, keys, values, some, scores, finish)


def attend_body(plan, b, with_notes, count_ref, *refs):
    group, lines, held, cap, width = plan.group, plan.lines, plan.held, plan.cap, plan.width
    rows, half = plan.rows, width // 2
    part_refs, weight_ref, query_ref = refs[:group], refs[group], refs[group + 1]
    sum_ref, total_ref, peak_ref = refs[group + 2 : group + 5]
    refs = refs[group + 5 :]
    if with_notes:
        member_ref, refs = refs[0], refs[1:]
    out_refs, (all_rows, keys, values, mixed, scores) = refs[:lines], refs[lines:]
    offset = 0
    for k in range(group):
        counts = [count_ref[k * lines + j, 64 * b] for j in range(lines)]
        offset = pack_rows(plan, b == 0, offset, counts, part_refs[k], all_rows)
    mixed[...] = jnp.zeros(mixed.shape, mixed.dtype)
    own = 0
    offsets = []
    for j in range(lines):
        offsets.append(own)
        own = own + count_ref[j, 64 * b]
    first, others = slice(0, rows), slice(rows, PATCH)
    project_pair(plan, b, all_rows[others], weight_ref, others, keys, values)

    def joined(at, lanes, summed, peak, own_head):
        peak = own_head(jnp.broadcast_to(peak, (peak.shape[0], half)))
        most = jnp.maximum(peak, peak_ref[at, lanes])
        here, early = jnp.exp(peak - most), jnp.exp(peak_ref[at, lanes] - most)
        over = own_head(summed[:, :half]) * here + sum_ref[at, lanes] * early
        under = own_head(summed[:, half:]) * here + total_ref[at, lanes] * early
        mixed[at, lanes] = (over / under).astype(BF16)

    def alone(at, lanes, summed, peak, own_head):
        mixed[at, lanes] = own_head(summed[:, :half] / summed[:, half:]).astype(BF16)

    @pl.when(own >= rows)
    def _():
        attention(plan, own, query_ref, keys, values, others, scores, joined)

    @pl.when(own < rows)
    def _():
        project_pair(plan, b, all_rows[first], weight_ref, first, keys, values)
        attention(plan, own, query_ref, keys, values, slice(0, PATCH), scores, alone)

    if with_notes:
        members = member_ref[...].astype(F32)
    for j in range(lines):
        out_refs[j][0:cap, :] = mixed[pl.ds(pl.multiple_of(offsets[j], 16), cap), :]
        if with_notes:
            entry = iota((16, 1), 0)
            now, later = members[j : j + 1], members[8 + j : 9 + j]
            note = jnp.where(entry == 0, now, jnp.where(entry == 1, later, 0.0))
            out_refs[j][cap : cap + 16, :] = note.astype(BF16)


def slots_of(plan, note_refs):
    cap = plan.cap
    notes = [r[cap : cap + 16, :].astype(F32) for r in note_refs]
    members = jnp.concatenate(notes, axis=0)
    ranks = matmul(members.astype(BF16), earlier_mask(plan.rows))
    slot = iota((cap, 1), 0).astype(F32)

    def places(j, block):
        at = 16 * j + block
        where = jnp.where(members[at : at + 1] > 0.5, ranks[at : at + 1], -1.0)
        return ones_where(slot == where)

    return places


def place_body(plan, b, *refs):
    note_refs, where_ref = refs[:-1], refs[-1]
    places = slots_of(plan, note_refs)
    found = jnp.concatenate([places(j, b) for j in range(plan.lines)], axis=0)
    same = ones_where(iota((plan.rows, plan.rows), 0) == iota((plan.rows, plan.rows), 1))
    where_ref[...] = matmul(same, found, NT).astype(BF16)


def store_body(plan, b, last, *refs):
    lines, cap, rows = plan.lines, plan.cap, plan.rows
    piece_refs, refs = far_first(refs[:lines]), refs[lines:]
    note_refs = piece_refs
    if b:
        where_ref, refs = refs[0], refs[1:]
        if not last:
            note_refs, refs = refs[:lines], refs[lines:]
    state_ref, gain_ref, proj_ref, fc1_ref, fc2_ref = refs[:5]
    refs = refs[5:]
    state_out, send_refs = refs[0], refs[1:]
    if not b or not last:
        places = slots_of(plan, note_refs)
    pieces = jnp.concatenate([r[0:cap, :] for r in piece_refs], axis=0)
    if b:
        mixed = matmul(where_ref[...], pieces).astype(BF16)
    else:
        where_from = jnp.concatenate([places(j, b) for j in range(lines)], axis=0)
        mixed = matmul(where_from, pieces, TN).astype(BF16)
    attended = state_ref[...] + matmul(mixed, proj_ref[b])
    normed_two = layer_norm(attended, gain_ref[b, 1:2, :]).astype(BF16)
    state = attended
    units = fc1_ref.shape[2]
    for start in range(0, units, units // 4):
        at = slice(start, start + units // 4)
        hidden = matmul(normed_two, fc1_ref[b, :, at])
        expanded = (0.5 * hidden * (1.0 + lax.erf(hidden * (0.5**0.5)))).astype(BF16)
        state = state + matmul(expanded, fc2_ref[b, at, :])
    state_out[...] = state
    if not last:
        normed = layer_norm(state, gain_ref[b + 1, 0:1, :]).astype(BF16)
        for j in range(lines):
            send_refs[j][...] = matmul(places(j, b + 1), normed).astype(BF16)


def move(block, peers, route):
    slabs = len(route)
    pairs = [
        (slabs * i + s, slabs * route[s](i) + s)
        for s in range(slabs)
        if route[s]
        for i in range(peers)
    ]
    return lax.ppermute(block, ("pts", "slab"), pairs)


def struct(shape, dtype):
    return jax.ShapeDtypeStruct(shape, dtype)


def by_lines(plan, features, orders, norm_gains, qkv_weight, proj_weight, fc1_weight, fc2_weight):
    rows, width, peers = plan.rows, plan.width, plan.peers
    group, lines, held, cap = plan.group, plan.lines, plan.held, plan.cap
    blocks = orders.shape[0]
    me = lax.axis_index("pts").astype(I32)
    slab = lax.axis_index("slab").astype(I32)
    shift = group.bit_length() - 1
    high, low = me >> shift, me & (group - 1)
    by_slab = lambda first, second: jnp.where(slab == 0, first, second)
    place = jnp.stack(
        [by_slab(high, low), by_slab(low, high), by_slab(group, 1), by_slab(1, group), slab]
    ).astype(I32)[None]

    def along_line(pieces):
        def far(j):
            return move(pieces[j], peers, [lambda i: i ^ (group * j), lambda i: i ^ j])

        return [pieces[0]] + [far(j) for j in range(1, lines)]

    def from_group(piece, k):
        return move(piece, peers, [lambda i: i ^ k, lambda i: i ^ (group * k)])

    turned = move(
        orders, peers, [lambda i: i, lambda i: (i & (group - 1)) * group + (i >> shift)]
    )
    (normed,) = kernel_call(norm_body, [struct((rows, width), BF16)], [whole()] * 2)(
        features, norm_gains
    )
    normed, kept, sent = kernel_call(
        functools.partial(note_body, plan),
        [struct((rows, width), BF16)] + [struct((64, width), BF16)] * 2,
        [whole()] * 3,
    )(place, normed, turned)
    mine, sent, near = kernel_call(
        join_body, [struct((32, width), BF16)] * 2 + [struct((rows, width), BF16)], [whole()] * 3
    )(kept, from_group(sent, 1), normed)
    line_rows = along_line([normed, near] + [normed] * (lines - 2))
    notes = [mine, from_group(sent, 2)]
    packed, counts, members = kernel_call(
        functools.partial(first_pack_body, plan),
        [struct((held, width), BF16), struct((16, 128), I32), struct((16, width), BF16)],
        [whole()] * (lines + 2),
    )(*line_rows, *notes)
    state = features
    for b in range(blocks):
        last = b == blocks - 1
        tall = cap if b else cap + 16
        parts = [packed] + [from_group(packed, k) for k in range(1, group)]
        table = HEADS // 2 * TALL
        early = kernel_call(
            functools.partial(early_body, plan, b),
            [struct((held + 2 * TALL, width), BF16)] + [struct((held, width), F32)] * 3,
            [whole()] * 3,
            [
                pltpu.VMEM((held + cap, width), BF16),
                pltpu.VMEM((width, rows), BF16),
                pltpu.VMEM((2, rows, width), BF16),
                pltpu.VMEM((4, table, rows), F32),
            ],
        )(counts, packed, qkv_weight)
        extra = [] if b else [members]
        mixed = kernel_call(
            functools.partial(attend_body, plan, b, b == 0),
            [struct((tall, width), BF16)] * lines,
            [whole()] * (group + 6 + len(extra)),
            [
                pltpu.VMEM((PATCH + held, width), BF16),
                pltpu.VMEM((width, PATCH), BF16),
                pltpu.VMEM((2, PATCH, width), BF16),
                pltpu.VMEM((held + cap, width), BF16),
                pltpu.VMEM((4, table, PATCH), F32),
            ],
        )(counts, *parts, qkv_weight, *early, *extra)
        pieces = along_line(mixed)
        if b == 0:
            kept_notes, told = pieces, []
        else:
            told = kernel_call(
                functools.partial(place_body, plan, b),
                [struct((rows, held), BF16)],
                [whole()] * lines,
            )(*kept_notes)
            told = list(told) + ([] if last else kept_notes)
        outs = [struct((rows, width), F32)]
        if not last:
            outs += [struct((cap, width), BF16)] * lines
        stored = kernel_call(
            functools.partial(store_body, plan, b, last), outs, [whole()] * (lines + len(told) + 5)
        )(*far_first(pieces), *told, state, norm_gains, proj_weight, fc1_weight, fc2_weight)
        state = stored[0]
        if not last:
            arrived = along_line(stored[1:])
            (packed,) = kernel_call(
                functools.partial(lay_body, plan), [struct((held, width), BF16)], [whole()] * lines
            )(*far_first(arrived))
    return state


def from_partner(block, axis, bit):
    count = lax.axis_size(axis)
    route = []
    for low in range(count):
        high = low | 1 << bit
        if high != low and high < count:
            route += [(low, high), (high, low)]
    return lax.ppermute(block, axis, route)


def routing(order_row, row_count, peers, capacity):
    owner_dev = order_row // row_count
    within = order_row % row_count
    onehot = (owner_dev[:, None] == jnp.arange(peers, dtype=jnp.int32)[None, :]).astype(jnp.int32)
    earlier = jnp.cumsum(onehot, axis=0) - onehot
    rank_pos = jnp.sum(onehot * earlier, axis=1)
    slot_pos = owner_dev * capacity + rank_pos
    request = jnp.full((peers * capacity,), row_count, jnp.int32).at[slot_pos].set(within)
    received = lax.all_to_all(request, "pts", split_axis=0, concat_axis=0, tiled=True)
    return (slot_pos, received)


def feed_forward(attended, gain_row, first_weight, second_weight):
    normed_two = layer_norm(attended, gain_row).astype(jnp.bfloat16)
    expanded = jax.nn.gelu(
        jnp.dot(normed_two, first_weight, preferred_element_type=jnp.float32), approximate=False
    ).astype(jnp.bfloat16)
    return jnp.dot(expanded, second_weight, preferred_element_type=jnp.float32)


def mix_heads(normed, in_weight):
    row_count, model_width = normed.shape
    projected_all = jnp.dot(normed, in_weight, preferred_element_type=jnp.float32).astype(
        jnp.bfloat16
    )
    queries = projected_all[:, :model_width]
    paired = projected_all[:, model_width:]
    doublings = (PATCH // row_count).bit_length() - 1
    gathered = paired
    for bit_index in range(doublings):
        gathered = jnp.concatenate((gathered, from_partner(gathered, "pts", bit_index)), axis=0)
    keys_all = gathered[:, :model_width]
    values_all = gathered[:, model_width:]
    head_size = model_width // HEADS
    per_group = min(4, HEADS)
    groups = HEADS // per_group
    score_scale = head_size ** (-0.5)

    def split_heads(matrix):
        return matrix.reshape(matrix.shape[0], groups, per_group, head_size).transpose(1, 0, 2, 3)

    def one_group(operands):
        query_part, key_part, value_part = operands
        scores = (
            jnp.einsum("qhd,khd->hqk", query_part, key_part, preferred_element_type=jnp.float32)
            * score_scale
        )
        row_peak = jnp.max(scores, axis=2, keepdims=True)
        weights = jnp.exp(scores - row_peak)
        probabilities = (weights / jnp.sum(weights, axis=2, keepdims=True)).astype(jnp.bfloat16)
        return jnp.einsum(
            "hqk,khd->qhd", probabilities, value_part, preferred_element_type=jnp.float32
        )

    mixed_heads = lax.map(
        one_group, (split_heads(queries), split_heads(keys_all), split_heads(values_all))
    )
    return mixed_heads.transpose(1, 0, 2, 3).reshape(row_count, model_width).astype(jnp.bfloat16)


def by_request(features, orders, norm_gains, qkv_weight, proj_weight, fc1_weight, fc2_weight):
    row_count, model_width = features.shape
    peers = lax.axis_size("pts")
    capacity = 3 * row_count // (2 * peers)
    state_rows = features
    for block_index in range(orders.shape[0]):
        slot_pos, received = routing(orders[block_index], row_count, peers, capacity)
        source_rows = jnp.minimum(received, row_count - 1)
        normed_local = layer_norm(state_rows, norm_gains[block_index, 0]).astype(jnp.bfloat16)
        arrived = lax.all_to_all(
            normed_local[source_rows], "pts", split_axis=0, concat_axis=0, tiled=True
        )
        mixed_heads = mix_heads(arrived[slot_pos], qkv_weight[block_index])
        returning = (
            jnp.zeros((peers * capacity, model_width), jnp.bfloat16).at[slot_pos].set(mixed_heads)
        )
        landed = lax.all_to_all(returning, "pts", split_axis=0, concat_axis=0, tiled=True)
        stored_mixed = (
            jnp.zeros((row_count, model_width), jnp.bfloat16).at[received].set(landed, mode="drop")
        )
        attended = state_rows + jnp.dot(
            stored_mixed, proj_weight[block_index], preferred_element_type=jnp.float32
        )
        state_rows = attended + feed_forward(
            attended, norm_gains[block_index, 1], fc1_weight[block_index], fc2_weight[block_index]
        )
    return state_rows


def local(*arrays):
    row_count, model_width = arrays[0].shape
    peers = lax.axis_size("pts")
    plan = Plan(row_count, peers, model_width)
    return by_lines(plan, *arrays) if plan.fits() else by_request(*arrays)


def solution(mesh):
    placed = (P(("slab", "pts"), None), P(None, ("slab", "pts")), P(), P(), P(), P(), P())
    return jax.shard_map(
        local, mesh=mesh, in_specs=placed, out_specs=P(("slab", "pts"), None), check_vma=False
    )
```
